32 devices in a mesh: sub: 8 (over z, y), grp: 4 (over x, core).
Axes of the slice: x: 2, y: 2, z: 4, core: 2. Of those that a mesh axis runs over, the one named last changes fastest.
Arguments:
- rhs: float32 [8, 4, 64, 128], P('sub', 'grp')
- guess: float32 [8, 4, 64, 128], P('sub', 'grp'), may hold values from -6 to 6
- blocks: bfloat16 [8, 4, 64, 64, 128], P('sub', 'grp')
- valve: int32 [8, 4, 128], P('sub', 'grp'), may hold values 0 or 1
- jscale: float32 [8, 4, 64, 128], P('sub', 'grp'), may hold values from 0.1 to 0.4
- prolong: float32 [8, 4, 64, 128], P('sub', 'grp'), may hold values from -0.75 to 0.75
- agg_map: int32 [8, 4, 128], P('sub', 'grp'), may hold values from 0 to 47
- cdiag: float32 [1536], P(('sub', 'grp')), may hold values from 0.5 to 2
- coff: bfloat16 [1536, 1536], P(('sub', 'grp')), may hold values from -0.3125 to 0.3125
- send_rows: int32 [8, 4, 2, 128], P('sub', 'grp'), may hold values from 0 to 127
- recv_rows: int32 [8, 4, 2, 128], P('sub', 'grp'), may hold values from 0 to 127
- live_counts: int32 [8, 4, 2], P('sub', 'grp'), may hold values from 32 to 128, as said below
Outputs:
- solution: float32 [8, 4, 64, 128], P('sub', 'grp')
- next_basis: float32 [8, 4, 64, 128], P('sub', 'grp')
The draws below stay inside these ranges and needn't reach their ends.
Inputs may be any that keep to these rules, and one draw needn't show every extreme that they name: `send_rows`: block numbers of the sending subdomain. `recv_rows`: block numbers of the receiving subdomain; several slots may name one block. `live_counts`: some subdomain has every slot live in both lists. `agg_map`: aggregates may be empty.
All inputs are finite; a program needn't handle non-finite values. No bound on the sum of `valve` on one device may be relied on, other than what follows from the above.
Results may differ from the reference program's by a relative error of at most 0.003.
Values may be sent and summed in bfloat16 or wider, within the bound.
No kernel may reach another device: no remote copies, remote signals or barrier semaphores. Data moves between devices by JAX's collectives and lax.ppermute only.
A program may use at most 64 MiB of HBM per device.

```python
import math
import jax
import jax.numpy as jnp
from jax import lax

BS = 64
NB = 128
SLOTS = 128
CPD = 48
NC = 1536
ITERS = 2
N_SUB = 8
N_GRP = 4


def draw_rhs(key, part):
    shape = (N_SUB, N_GRP, BS, NB)
    rise = 1.0 + 2.0 * jnp.arange(N_SUB, dtype=jnp.float32) / max(N_SUB - 1, 1)
    base = jax.random.normal(key, shape, jnp.float32)
    return base * rise[:, None, None, None]


def draw_blocks(key, part):
    shape = (N_SUB, N_GRP, BS, BS, NB)
    places = jnp.arange(BS, dtype=jnp.int32)
    unit = (places[:, None] == places[None, :]).astype(jnp.float32)[None, None, :, :, None]
    noise = jax.random.normal(key, shape, jnp.float32)
    noise = noise * (2.0 / BS ** 0.5)
    return (4.0 * unit + noise * (1.0 - unit)).astype(jnp.bfloat16)


def draw_live_counts(key, part):
    counts = jax.random.randint(key, (N_SUB, N_GRP, 2), NB // 4, NB + 1, dtype=jnp.int32)
    return counts.at[1, 0, :].set(NB)


def place_ends(drawn, stream_key, low, high):
    extent = drawn.shape
    place = [jax.random.randint(jax.random.fold_in(stream_key, axis), (), 0, extent[axis]) for axis in range(len(extent))]
    drawn = drawn.at[tuple(place)].set(low)
    longest = extent.index(max(extent))
    place[longest] = (place[longest] + 1) % extent[longest]
    return drawn.at[tuple(place)].set(high)


def with_spikes(drawn, key, source, target, blocks, factor):
    def block_of(dim):
        return (jnp.arange(drawn.shape[dim]) // (drawn.shape[dim] // blocks)).reshape((-1,) + (1,) * (drawn.ndim - 1 - dim))

    one_side = jax.random.permutation(key, blocks)[block_of(target)]
    other_side = (block_of(target) + blocks // 2) % blocks
    return jnp.where((block_of(source) == one_side) | (block_of(source) == other_side), factor * drawn, drawn)


def steps_of(rng, shape, split, low, top_value):
    loudness = 1.0
    for axis_at, parts in split:
        draws = jax.random.uniform(jax.random.fold_in(jax.random.fold_in(rng, 6), axis_at), (parts,), jnp.float32, low / len(split), top_value / len(split))
        loudness = loudness * jnp.repeat(jnp.exp(draws), shape[axis_at] // parts).reshape((-1,) + (1,) * (len(shape) - 1 - axis_at))
    return loudness


def gaussian(rng, shape, deviation, most, split=(), kind=jnp.bfloat16):
    factor_of = steps_of(rng, shape, split, -0.22, 0.18) if split else 1.0
    drawn = jax.random.normal(rng, shape, jnp.float32) * deviation * factor_of
    return jnp.minimum(jnp.maximum(drawn, -most), most).astype(kind)


def heavy_noise(key, shape, width, most, cuts, heavy, kind=jnp.bfloat16):
    values = width * jax.random.normal(key, shape, jnp.float32)
    if cuts:
        values = values * steps_of(key, shape, cuts, -0.22, 0.18)
    return jnp.clip(with_spikes(values, jax.random.fold_in(key, 3), *heavy), -most, most).astype(kind)


def setup_inputs(seed: int = 0) -> dict:
    keys = jax.random.split(jax.random.key(seed), 13)
    return {
        "rhs": draw_rhs(jax.random.fold_in(keys[12], 71), 0),
        "guess": gaussian(keys[1], (N_SUB, N_GRP, BS, NB), 1.0, 6.0, ((0, 8), (1, 4)), jnp.float32),
        "blocks": draw_blocks(jax.random.fold_in(keys[12], 71), 0),
        "valve": place_ends((jax.random.randint(keys[3], (N_SUB, N_GRP, NB), 0, 3) < 1).astype(jnp.int32), jax.random.fold_in(keys[3], 1), 0, 1),
        "jscale": jnp.clip(jnp.exp(math.log(0.4) - 1.3862944 * jax.random.uniform(keys[4], (N_SUB, N_GRP, BS, NB), jnp.float32) ** steps_of(keys[4], (N_SUB, N_GRP, BS, NB), ((0, 8), (1, 4)), -0.2, 0.2)), 0.1, 0.4),
        "prolong": gaussian(keys[5], (N_SUB, N_GRP, BS, NB), BS ** -0.5, 0.75, ((0, 8), (1, 4)), jnp.float32),
        "agg_map": place_ends(jax.random.randint(keys[6], (N_SUB, N_GRP, NB), 0, CPD), jax.random.fold_in(keys[6], 1), 0, CPD - 1).astype(jnp.int32),
        "cdiag": jnp.clip(jnp.exp(math.log(2.0) - 1.3862944 * jax.random.uniform(keys[7], (NC,), jnp.float32) ** steps_of(keys[7], (NC,), ((0, 32),), -0.2, 0.2)), 0.5, 2.0),
        "coff": heavy_noise(keys[8], (NC, NC), NC ** -0.5, 0.3125, ((0, 32),), (1, 0, 32, 2.75)),
        "send_rows": place_ends(jax.random.randint(keys[9], (N_SUB, N_GRP, 2, SLOTS), 0, NB), jax.random.fold_in(keys[9], 1), 0, NB - 1).astype(jnp.int32),
        "recv_rows": place_ends(jax.random.randint(keys[10], (N_SUB, N_GRP, 2, SLOTS), 0, NB), jax.random.fold_in(keys[10], 1), 0, NB - 1).astype(jnp.int32),
        "live_counts": draw_live_counts(jax.random.fold_in(keys[12], 71), 0),
    }


penalty_gain = 3.0
coupling = 0.5

def received(packed, recv_rows, live_counts, side):
    slots = jnp.arange(recv_rows.shape[3], dtype=jnp.int32)
    places = jnp.arange(NB, dtype=jnp.int32)
    live = slots[None, None, :] < live_counts[:, :, side][:, :, None]
    onehot = ((recv_rows[:, :, side, :, None] == places[None, None, None, :]) & live[:, :, :, None]).astype(jnp.float32)
    return jnp.einsum('sgik,sgkb->sgib', packed, onehot, precision=lax.Precision.HIGHEST)

def operate(field, blocks, valve, send_rows, recv_rows, live_counts):
    out = jnp.einsum('sgijb,sgjb->sgib', blocks.astype(jnp.float32), field, precision=lax.Precision.HIGHEST)
    out = out + penalty_gain * valve.astype(jnp.float32)[:, :, None, :] * field
    shape = (field.shape[0], field.shape[1], field.shape[2], send_rows.shape[3])
    upward = jnp.take_along_axis(field, jnp.broadcast_to(send_rows[:, :, 0][:, :, None, :], shape), axis=3)
    downward = jnp.take_along_axis(field, jnp.broadcast_to(send_rows[:, :, 1][:, :, None, :], shape), axis=3)
    below = jnp.concatenate([jnp.zeros_like(upward[:1]), upward[:-1]], axis=0)
    above = jnp.concatenate([downward[1:], jnp.zeros_like(downward[:1])], axis=0)
    return out - coupling * (received(below, recv_rows, live_counts, 0) + received(above, recv_rows, live_counts, 1))

def precondition(field, jscale, prolong, agg_map, cdiag, coff):
    weighted = lax.optimization_barrier(jnp.sum(prolong * field, axis=2))
    agg_sel = (agg_map[:, :, :, None] == jnp.arange(CPD, dtype=jnp.int32)[None, None, None, :]).astype(jnp.float32)
    coarse = jnp.einsum('sgb,sgbc->sgc', weighted, agg_sel, precision=lax.Precision.HIGHEST)
    flat = coarse.reshape(NC)
    coarse_half = flat.astype(jnp.bfloat16)
    coarse_sol = cdiag * flat + jnp.dot(coff, coarse_half, preferred_element_type=jnp.float32)
    coarse_sol = coarse_sol.reshape(coarse.shape)
    spread = jnp.einsum('sgbc,sgc->sgb', agg_sel, coarse_sol, precision=lax.Precision.HIGHEST)
    return jscale * field + prolong * spread[:, :, None, :]

def solve_small(gram, target):
    count = target.shape[0]
    matrix = [[gram[row, col] for col in range(count)] for row in range(count)]
    vector = [target[row] for row in range(count)]
    for pivot in range(count):
        for row in range(pivot + 1, count):
            factor = matrix[row][pivot] / matrix[pivot][pivot]
            for col in range(pivot, count):
                matrix[row][col] = matrix[row][col] - factor * matrix[pivot][col]
            vector[row] = vector[row] - factor * vector[pivot]
    result = [None] * count
    for row in range(count - 1, -1, -1):
        total = vector[row]
        for col in range(row + 1, count):
            total = total - matrix[row][col] * result[col]
        result[row] = total / matrix[row][row]
    return result

def reference(rhs, guess, blocks, valve, jscale, prolong, agg_map, cdiag, coff, send_rows, recv_rows, live_counts):

    def apply_a(field):
        return operate(field, blocks, valve, send_rows, recv_rows, live_counts)
    first = rhs - apply_a(guess)
    beta = jnp.sqrt(jnp.sum(first * first))
    basis = [first / beta]
    directions = []
    hess = jnp.zeros((ITERS + 1, ITERS), jnp.float32)
    for column in range(ITERS):
        direction = precondition(basis[column], jscale, prolong, agg_map, cdiag, coff)
        image = apply_a(direction)
        heights = jnp.stack([jnp.sum(vector * image) for vector in basis])
        energy = jnp.sum(image * image)
        for row in range(column + 1):
            image = image - heights[row] * basis[row]
        remainder = energy - jnp.sum(heights * heights)
        height = jnp.sqrt(jnp.maximum(remainder, 0.01 * energy))
        hess = hess.at[:column + 1, column].set(heights).at[column + 1, column].set(height)
        basis.append(image / height)
        directions.append(direction)
    gram = jnp.dot(hess.T, hess, precision=lax.Precision.HIGHEST)
    coeffs = solve_small(gram, beta * hess[0])
    solution = guess
    for column in range(ITERS):
        solution = solution + coeffs[column] * directions[column]
    return (solution, basis[ITERS])
```

```python
import functools
import math

import jax
import jax.numpy as jnp
from jax import lax
from jax.experimental import pallas as pl
from jax.experimental.pallas import tpu as pltpu
from jax.sharding import PartitionSpec as P

penalty_gain = 3.0
coupling = 0.5

LANES = 128
SLOT = 64
AXES = ("sub", "grp")
f32 = jnp.float32
bf16 = jnp.bfloat16


def call(body, outs, *args, smem=()):
    vmem = pl.BlockSpec(memory_space=pltpu.VMEM)
    scalars = pl.BlockSpec(memory_space=pltpu.SMEM)
    return pl.pallas_call(
        body,
        out_shape=[jax.ShapeDtypeStruct(shape, kind) for shape, kind in outs],
        in_specs=[scalars if at in smem else vmem for at in range(len(args))],
        out_specs=[vmem] * len(outs),
        compiler_params=pltpu.CompilerParams(vmem_limit_bytes=32 * 1024 * 1024),
    )(*args)


def pick(field, places):
    return jnp.take_along_axis(field, jnp.broadcast_to(places, field.shape), axis=1)


def pieces(field):
    high = field.astype(bf16)
    return high, (field - high.astype(f32)).astype(bf16)


def block_product(blocks_ref, field):
    rows = []
    for at in range(0, blocks_ref.shape[0], 8):
        part = blocks_ref[at : at + 8].astype(f32) * field[None]
        rows.append(jnp.sum(part, axis=1))
    return jnp.concatenate(rows, axis=0)


def received(below, above, arrive_ref):
    high, low = pieces(jnp.concatenate([below, above], axis=1))
    both = jnp.dot(
        jnp.concatenate([high, low], axis=0), arrive_ref[...], preferred_element_type=f32
    )
    count = below.shape[0]
    return both[:count] + both[count:]


def restricted(weighted, gather_ref):
    high = weighted.astype(bf16).astype(f32)
    rest = weighted - high
    middle = rest.astype(bf16).astype(f32)
    last = rest - middle
    row = lax.broadcasted_iota(jnp.int32, (8, weighted.shape[1]), 0)
    stack = jnp.where(row == 0, high, jnp.where(row == 1, middle, jnp.where(row == 2, last, 0.0)))
    sums = jnp.dot(stack.astype(bf16), gather_ref[...], preferred_element_type=f32)
    return jnp.sum(sums, axis=0, keepdims=True)


def total(field):
    value = jnp.sum(jnp.sum(field, axis=0, keepdims=True), axis=1, keepdims=True)
    return jnp.broadcast_to(value, (1, LANES))


def to_all(ref, parts):
    row = jnp.concatenate(parts, axis=1)
    ref[...] = jnp.broadcast_to(row, ref.shape)


def first_send(guess_ref, send_ref, up_ref, down_ref):
    guess = guess_ref[...]
    up_ref[...] = pick(guess, send_ref[0:1, :])
    down_ref[...] = pick(guess, send_ref[1:2, :])


def prepare(live_ref, guess_ref, rhs_ref, blocks_ref, valve_ref, agg_ref, recv_ref, cpd,
            local_ref, arrive_ref, gather_ref):
    guess = guess_ref[...]
    penalty = penalty_gain * valve_ref[...].astype(f32)
    local_ref[...] = rhs_ref[...] - (block_product(blocks_ref, guess) + penalty * guess)
    place = lax.axis_index("sub")
    ends = (place > 0, place < lax.axis_size("sub") - 1)
    count = arrive_ref.shape[1]
    slots = recv_ref.shape[1]
    row = lax.broadcasted_iota(jnp.int32, (count, slots), 0)
    slot = lax.broadcasted_iota(jnp.int32, (count, slots), 1)
    for side in (0, 1):
        live = jnp.where(ends[side], live_ref[0, side], 0)
        hit = (recv_ref[side : side + 1, :] == row) & (slot < live)
        arrive_ref[side * slots : (side + 1) * slots, :] = jnp.where(hit, 1.0, 0.0).T.astype(bf16)
    period = gather_ref.shape[1]
    coarse = lax.rem(lax.broadcasted_iota(jnp.int32, (period, count), 0), cpd)
    gather_ref[...] = jnp.where(agg_ref[...] == coarse, 1.0, 0.0).T.astype(bf16)


def residual(local_ref, below_ref, above_ref, arrive_ref, gather_ref, prolong_ref, jscale_ref,
             send_ref, agg_ref, cdiag_ref, first_ref, out_ref, up_ref, down_ref):
    first = local_ref[...] + coupling * received(below_ref[...], above_ref[...], arrive_ref)
    first_ref[...] = first
    prolong = prolong_ref[...]
    weighted = jnp.sum(prolong * first, axis=0, keepdims=True)
    to_all(out_ref, [restricted(weighted, gather_ref), total(first * first)])
    scaled = jscale_ref[...] * first
    size = first.shape[0]
    agg = jnp.broadcast_to(agg_ref[...].astype(f32), (8, LANES))
    cdiag = jnp.broadcast_to(cdiag_ref[...], (8, LANES))
    for side, ref in ((0, up_ref), (1, down_ref)):
        places = send_ref[side : side + 1, :]
        ref[0:size, :] = pick(scaled, places)
        ref[size : 2 * size, :] = pick(prolong, places)
        ref[2 * size : 2 * size + 8, :] = pick(agg, places)
        ref[2 * size + 8 : 2 * size + 16, :] = cdiag


def own_rows(ref_value, grp_size):
    count = ref_value.shape[0]
    me = lax.axis_index("sub") * grp_size + lax.axis_index("grp")
    return [lax.rem(me + shift + count, count) for shift in (0, -grp_size, grp_size)]


def coarse_solve(coarse_ref, cpd, grp_size, coff_refs, cdiags):
    count, period = coarse_ref.shape
    group = period // cpd
    owner = lax.broadcasted_iota(jnp.int32, (group, period), 1) // cpd
    mask = owner == lax.broadcasted_iota(jnp.int32, (group, period), 0)
    value = jnp.concatenate(
        [
            jnp.where(mask, coarse_ref[at : at + group, :], 0.0)
            for at in range(0, count, group)
        ],
        axis=1,
    ).astype(bf16)
    filler = jnp.zeros((SLOT - cpd, coff_refs[0].shape[1]), bf16)
    matrix = jnp.concatenate([part for ref in coff_refs for part in (ref[...], filler)], axis=0)
    product = lax.dot_general(
        value, matrix, (((1,), (1,)), ((), ())), preferred_element_type=f32
    )
    product = jnp.sum(product, axis=0, keepdims=True)
    product = jnp.concatenate([product, jnp.zeros((1, SLOT), f32)], axis=1)
    low, top = product[:, :LANES], product[:, LANES:]
    shares = [low, pltpu.roll(jnp.broadcast_to(low, (8, LANES)), SLOT, 1)[0:1], top]
    result = []
    head = coarse_ref[:, 0:LANES]
    place = lax.broadcasted_iota(jnp.int32, head.shape, 0)
    for row, cdiag, share in zip(own_rows(coarse_ref, grp_size), cdiags, shares):
        coarse = jnp.sum(jnp.where(place == row, head, 0.0), axis=0, keepdims=True)
        result.append(cdiag * coarse + share)
    return result


def spread_of(solution, agg):
    wide = jnp.broadcast_to(solution, (8, LANES))
    return jnp.take_along_axis(wide, jnp.broadcast_to(agg, (8, LANES)), axis=1)[0:1]


def step_tail(direction, near, blocks_ref, valve_ref, arrive_ref):
    penalty = penalty_gain * valve_ref[...].astype(f32)
    image = block_product(blocks_ref, direction) + penalty * direction
    return image - coupling * received(near[0], near[1], arrive_ref)


def near_constants(ref, size):
    return (
        ref[size : 2 * size, :],
        ref[2 * size : 2 * size + 1, :].astype(jnp.int32),
        ref[2 * size + 8 : 2 * size + 9, :],
    )


def first_step(got_ref, below_ref, above_ref, coff_ref, coff_b_ref, coff_a_ref, cdiag_ref,
               first_ref, jscale_ref, prolong_ref, agg_ref, blocks_ref, valve_ref, arrive_ref,
               gather_ref, send_ref, cpd, grp_size,
               basis_ref, direction_ref, image_ref, coarse_ref, out_ref, up_ref, down_ref):
    size = first_ref.shape[0]
    period = coarse_ref.shape[1]
    sums = jnp.sum(got_ref[:, period : period + LANES], axis=0, keepdims=True)
    beta = jnp.sqrt(sums)
    for at in range(0, period, LANES):
        coarse_ref[:, at : at + LANES] = got_ref[:, at : at + LANES] / beta
    basis = first_ref[...] / beta
    basis_ref[...] = basis
    near = [near_constants(ref, size) for ref in (below_ref, above_ref)]
    solved = coarse_solve(coarse_ref, cpd, grp_size, (coff_ref, coff_b_ref, coff_a_ref),
                          [cdiag_ref[...]] + [item[2] for item in near])
    jscale, prolong = jscale_ref[...], prolong_ref[...]
    direction = jscale * basis + prolong * spread_of(solved[0], agg_ref[...])
    direction_ref[...] = direction
    fields = []
    for ref, (weights, agg, _), part in zip((below_ref, above_ref), near, solved[1:]):
        fields.append(ref[0:size, :] / beta + weights * spread_of(part, agg))
    image = step_tail(direction, fields, blocks_ref, valve_ref, arrive_ref)
    image_ref[...] = image
    weighted = jnp.sum(prolong * image, axis=0, keepdims=True)
    to_all(out_ref, [restricted(weighted, gather_ref), total(basis * image), total(image * image)])
    scaled = jscale * image
    up_ref[...] = pick(scaled, send_ref[0:1, :])
    down_ref[...] = pick(scaled, send_ref[1:2, :])


def second_step(got_ref, first_got_ref, below_ref, above_ref, below_first_ref, above_first_ref,
                coff_ref, coff_b_ref, coff_a_ref, cdiag_ref, basis_ref, image_ref, coarse_ref,
                jscale_ref, prolong_ref, agg_ref, blocks_ref, valve_ref, arrive_ref,
                cpd, grp_size,
                basis_two_ref, direction_ref, image_two_ref, scalars_ref, out_ref, work_ref):
    size = basis_ref.shape[0]
    period = coarse_ref.shape[1]
    beta = jnp.sqrt(jnp.sum(first_got_ref[:, period : period + LANES], axis=0, keepdims=True))
    totals = jnp.sum(got_ref[:, period : period + 2 * LANES], axis=0, keepdims=True)
    along, energy = totals[:, :LANES], totals[:, LANES:]
    height = jnp.sqrt(jnp.maximum(energy - along * along, 0.01 * energy))
    for at in range(0, period, LANES):
        work_ref[:, at : at + LANES] = (
            got_ref[:, at : at + LANES] - along * coarse_ref[:, at : at + LANES]
        ) / height
    basis = (image_ref[...] - along * basis_ref[...]) / height
    basis_two_ref[...] = basis
    near = [near_constants(ref, size) for ref in (below_first_ref, above_first_ref)]
    solved = coarse_solve(work_ref, cpd, grp_size, (coff_ref, coff_b_ref, coff_a_ref),
                          [cdiag_ref[...]] + [item[2] for item in near])
    direction = jscale_ref[...] * basis + prolong_ref[...] * spread_of(solved[0], agg_ref[...])
    direction_ref[...] = direction
    fields = []
    for ref, first_near, (weights, agg, _), part in zip(
        (below_ref, above_ref), (below_first_ref, above_first_ref), near, solved[1:]
    ):
        scaled = (ref[...] - along * (first_near[0:size, :] / beta)) / height
        fields.append(scaled + weights * spread_of(part, agg))
    image = step_tail(direction, fields, blocks_ref, valve_ref, arrive_ref)
    image_two_ref[...] = image
    scalars_ref[0:1, :] = beta
    scalars_ref[1:2, :] = along
    scalars_ref[2:3, :] = height
    scalars_ref[3:8, :] = jnp.zeros((5, LANES), f32)
    to_all(out_ref, [total(basis_ref[...] * image), total(basis * image), total(image * image)])


def finish(got_ref, scalars_ref, guess_ref, basis_ref, basis_two_ref, direction_ref,
           direction_two_ref, image_ref, solution_ref, next_ref):
    beta, h11, h21 = scalars_ref[0:1, :], scalars_ref[1:2, :], scalars_ref[2:3, :]
    totals = jnp.sum(got_ref[...], axis=0, keepdims=True)
    h12, h22, energy = totals[:, :LANES], totals[:, LANES : 2 * LANES], totals[:, 2 * LANES :]
    h32 = jnp.sqrt(jnp.maximum(energy - (h12 * h12 + h22 * h22), 0.01 * energy))
    g00 = h11 * h11 + h21 * h21
    g01 = h11 * h12 + h21 * h22
    g11 = h12 * h12 + h22 * h22 + h32 * h32
    t0, t1 = beta * h11, beta * h12
    factor = g01 / g00
    c1 = (t1 - factor * t0) / (g11 - factor * g01)
    c0 = (t0 - g01 * c1) / g00
    solution_ref[...] = guess_ref[...] + c0 * direction_ref[...] + c1 * direction_two_ref[...]
    next_ref[...] = (image_ref[...] - h12 * basis_ref[...] - h22 * basis_two_ref[...]) / h32


def on_device(rhs, guess, blocks, valve, jscale, prolong, agg_map, cdiag, coff, send_rows,
              recv_rows, live_counts):
    rhs, guess, blocks, jscale, prolong = rhs[0, 0], guess[0, 0], blocks[0, 0], jscale[0, 0], prolong[0, 0]
    valve, agg, live = valve[0], agg_map[0], live_counts[0]
    send, recv = send_rows[0, 0], recv_rows[0, 0]
    size, count = guess.shape
    slots = send.shape[1]
    cpd = cdiag.shape[0]
    subs, grps = lax.axis_size("sub"), lax.axis_size("grp")
    devices = subs * grps
    period = math.lcm(cpd, LANES)
    cdiag_row = jnp.pad(cdiag[None, :], ((0, 0), (0, LANES - cpd)))
    upward = [(at, (at + 1) % subs) for at in range(subs)]
    downward = [((at + 1) % subs, at) for at in range(subs)]

    def exchange(up, down):
        return lax.ppermute(up, "sub", upward), lax.ppermute(down, "sub", downward)

    def everyone(rows):
        return lax.all_to_all(rows, AXES, 0, 0, tiled=True)

    field = ((size, count), f32)
    near = ((size, slots), f32)
    up, down = call(first_send, [near, near], guess, send)
    below, above = exchange(up, down)
    coff_below, coff_above = exchange(coff, coff)
    local, arrive, gather = call(
        lambda *refs: prepare(*refs[:7], cpd, *refs[7:]),
        [field, ((2 * slots, count), bf16), ((count, period), bf16)],
        live, guess, rhs, blocks, valve, agg, recv, smem=(0,),
    )
    packed = ((2 * size + 16, slots), f32)
    first, rows, up, down = call(
        residual,
        [field, ((devices, period + LANES), f32), packed, packed],
        local, below, above, arrive, gather, prolong, jscale, send, agg, cdiag_row,
    )
    below_first, above_first = exchange(up, down)
    first_got = everyone(rows)
    basis, direction, image, coarse, rows, up, down = call(
        lambda *refs: first_step(*refs[:16], cpd, grps, *refs[16:]),
        [field, field, field, ((devices, period), f32), ((devices, period + 2 * LANES), f32), near, near],
        first_got, below_first, above_first, coff, coff_below, coff_above, cdiag_row, first, jscale,
        prolong, agg, blocks, valve, arrive, gather, send,
    )
    below, above = exchange(up, down)
    got = everyone(rows)
    basis_two, direction_two, image_two, scalars, rows, _ = call(
        lambda *refs: second_step(*refs[:19], cpd, grps, *refs[19:]),
        [field, field, field, ((8, LANES), f32), ((devices, 3 * LANES), f32), ((devices, period), f32)],
        got, first_got, below, above, below_first, above_first, coff, coff_below, coff_above,
        cdiag_row, basis, image, coarse, jscale, prolong, agg, blocks, valve, arrive,
    )
    got = everyone(rows)
    solution, next_basis = call(
        finish, [field, field],
        got, scalars, guess, basis, basis_two, direction, direction_two, image_two,
    )
    return solution[None, None], next_basis[None, None]


def solution(mesh):
    return jax.shard_map(
        on_device,
        mesh=mesh,
        in_specs=(
            P("sub", "grp", None, None),
            P("sub", "grp", None, None),
            P("sub", "grp", None, None, None),
            P("sub", "grp", None),
            P("sub", "grp", None, None),
            P("sub", "grp", None, None),
            P("sub", "grp", None),
            P(("sub", "grp")),
            P(("sub", "grp"), None),
            P("sub", "grp", None, None),
            P("sub", "grp", None, None),
            P("sub", "grp", None),
        ),
        out_specs=(P("sub", "grp", None, None), P("sub", "grp", None, None)),
        check_vma=False,
    )
```

```python
import math

import jax
import jax.numpy as jnp
from jax import lax
from jax.experimental import pallas as pl
from jax.experimental.pallas import tpu as pltpu
from jax.sharding import PartitionSpec as P

penalty_gain = 3.0
coupling = 0.5

LANES = 128
SLOT = 64
AXES = ("sub", "grp")
f32 = jnp.float32
bf16 = jnp.bfloat16


def call(body, outs, *args, smem=(), hbm=(), scratch=(), limit=32):
    def spec(at):
        if at in hbm:
            return pl.BlockSpec(memory_space=pl.ANY)
        return pl.BlockSpec(memory_space=pltpu.SMEM if at in smem else pltpu.VMEM)

    return pl.pallas_call(
        body,
        out_shape=[jax.ShapeDtypeStruct(shape, kind) for shape, kind in outs],
        in_specs=[spec(at) for at in range(len(args))],
        out_specs=[pl.BlockSpec(memory_space=pltpu.VMEM)] * len(outs),
        scratch_shapes=list(scratch),
        compiler_params=pltpu.CompilerParams(vmem_limit_bytes=limit * 1024 * 1024),
    )(*args)


def partner(place, side):
    return place + 1 - 2 * ((place + side) % 2)


def pairing(subs, grps, side):
    moves = []
    for place in range(subs):
        other = partner(place, side)
        for group in range(grps):
            if 0 <= other < subs:
                target = other * grps + group
            else:
                target = place * grps + (group ^ 1 if group ^ 1 < grps else group)
            moves.append((place * grps + group, target))
    return moves


def row_of(ref, flipped):
    return jnp.where(flipped == 0, ref[0:1, :], ref[1:2, :])


def parity(side):
    return (lax.axis_index("sub") + side) % 2


def pick(field, places):
    return jnp.take_along_axis(field, jnp.broadcast_to(places, field.shape), axis=1)


def pieces(field):
    high = field.astype(bf16)
    return high, (field - high.astype(f32)).astype(bf16)


def local_product(blocks_ref, valve_ref, field):
    rows = []
    for at in range(0, blocks_ref.shape[0], 8):
        part = blocks_ref[at : at + 8].astype(f32) * field[None]
        rows.append(jnp.sum(part, axis=1))
    return jnp.concatenate(rows, axis=0) + penalty_gain * valve_ref[...].astype(f32) * field


def received(near, arrive_ref):
    high, low = pieces(jnp.concatenate(near, axis=1))
    both = jnp.dot(
        jnp.concatenate([high, low], axis=0), arrive_ref[...], preferred_element_type=f32
    )
    count = near[0].shape[0]
    return both[:count] + both[count:]


def restricted(weighted, gather_ref):
    high = weighted.astype(bf16).astype(f32)
    rest = weighted - high
    middle = rest.astype(bf16).astype(f32)
    last = rest - middle
    row = lax.broadcasted_iota(jnp.int32, (8, weighted.shape[1]), 0)
    stack = jnp.where(row == 0, high, jnp.where(row == 1, middle, jnp.where(row == 2, last, 0.0)))
    sums = jnp.dot(stack.astype(bf16), gather_ref[...], preferred_element_type=f32)
    sums = jnp.sum(sums, axis=0, keepdims=True)
    return [sums[:, at : at + LANES] for at in range(0, sums.shape[1], LANES)]


def total(field):
    value = jnp.sum(jnp.sum(field, axis=0, keepdims=True), axis=1, keepdims=True)
    return jnp.broadcast_to(value, (1, LANES))


def halves(first, second):
    return jnp.where(lax.broadcasted_iota(jnp.int32, (1, LANES), 1) < LANES // 2, first, second)


def turned(row):
    return pltpu.roll(jnp.broadcast_to(row, (8, LANES)), LANES // 2, 1)[0:1]


def to_all(ref, rows):
    ref[...] = jnp.broadcast_to(jnp.concatenate(rows, axis=0)[None], ref.shape)


def first_send(guess_hbm, prolong_hbm, agg_hbm, send_hbm, even_ref, odd_ref,
               guess_ref, prolong_ref, agg_ref, send_ref, sems):
    pairs = ((guess_hbm, guess_ref), (prolong_hbm, prolong_ref), (agg_hbm, agg_ref), (send_hbm, send_ref))
    copies = [pltpu.make_async_copy(*pair, sems.at[at]) for at, pair in enumerate(pairs)]
    for copy in copies:
        copy.start()
    for copy in copies:
        copy.wait()
    size = guess_ref.shape[0]
    agg = jnp.broadcast_to(agg_ref[...].astype(f32), (8, LANES))
    for side, ref in enumerate((even_ref, odd_ref)):
        places = row_of(send_ref, parity(side))
        ref[0:size, :] = pick(guess_ref[...], places)
        ref[size : 2 * size, :] = pick(prolong_ref[...], places)
        ref[2 * size : 2 * size + 8, :] = pick(agg, places)


def prepare(live_ref, guess_ref, rhs_ref, blocks_ref, valve_ref, agg_ref, recv_ref, cpd,
            local_ref, arrive_ref, gather_ref):
    local_ref[...] = rhs_ref[...] - local_product(blocks_ref, valve_ref, guess_ref[...])
    place = lax.axis_index("sub")
    count = arrive_ref.shape[1]
    slots = recv_ref.shape[1]
    row = lax.broadcasted_iota(jnp.int32, (count, slots), 0)
    slot = lax.broadcasted_iota(jnp.int32, (count, slots), 1)
    for side in (0, 1):
        other = place + 1 - 2 * parity(side)
        there = (other >= 0) & (other < lax.axis_size("sub"))
        which = 1 - parity(side)
        live = jnp.where(there, live_ref[0, which], 0)
        hit = (row_of(recv_ref, which) == row) & (slot < live)
        arrive_ref[side * slots : (side + 1) * slots, :] = jnp.where(hit, 1.0, 0.0).T.astype(bf16)
    period = gather_ref.shape[1]
    coarse = lax.rem(lax.broadcasted_iota(jnp.int32, (period, count), 0), cpd)
    gather_ref[...] = jnp.where(agg_ref[...] == coarse, 1.0, 0.0).T.astype(bf16)


def residual(local_ref, even_near_ref, odd_near_ref, arrive_ref, gather_ref, prolong_ref,
             jscale_ref, send_ref, cdiag_ref, first_ref, out_ref, even_ref, odd_ref):
    size = local_ref.shape[0]
    near = [even_near_ref[0:size, :], odd_near_ref[0:size, :]]
    first = local_ref[...] + coupling * received(near, arrive_ref)
    first_ref[...] = first
    weighted = jnp.sum(prolong_ref[...] * first, axis=0, keepdims=True)
    to_all(out_ref, restricted(weighted, gather_ref) + [total(first * first)])
    scaled = jscale_ref[...] * first
    cpd = cdiag_ref.shape[1]
    cdiag = jnp.concatenate([cdiag_ref[...], jnp.zeros((1, LANES - cpd), f32)], axis=1)
    for side, ref in enumerate((even_ref, odd_ref)):
        ref[0:size, :] = pick(scaled, row_of(send_ref, parity(side)))
        ref[size : size + 8, :] = jnp.broadcast_to(cdiag, (8, LANES))


def look_ahead(first_ref, jscale_ref, prolong_ref, blocks_ref, valve_ref, coff_ref, coff_even_ref,
               coff_odd_ref, lead_ref, pull_ref, matrix_ref):
    lead_ref[...] = local_product(blocks_ref, valve_ref, jscale_ref[...] * first_ref[...])
    pull_ref[...] = local_product(blocks_ref, valve_ref, prolong_ref[...])
    cpd = coff_ref.shape[0]
    for at, ref in enumerate((coff_ref, coff_even_ref, coff_odd_ref)):
        matrix_ref[at * SLOT : at * SLOT + cpd, :] = ref[...]
        matrix_ref[at * SLOT + cpd : (at + 1) * SLOT, :] = jnp.zeros((SLOT - cpd, ref.shape[1]), bf16)


def look_further(image_ref, jscale_ref, blocks_ref, valve_ref, lead_ref):
    lead_ref[...] = local_product(blocks_ref, valve_ref, jscale_ref[...] * image_ref[...])


def compact(got_ref, cpd):
    count, rows, _ = got_ref.shape
    shape = (rows, LANES)
    place = lax.broadcasted_iota(jnp.int32, shape, 0) * LANES + lax.broadcasted_iota(jnp.int32, shape, 1)
    owner = place // cpd
    group = (rows - 1) * LANES // cpd
    parts, sums = [], jnp.zeros(shape, f32)
    for at in range(0, count, group):
        part = jnp.zeros(shape, f32)
        for step in range(group):
            tile = got_ref[at + step]
            part = jnp.where(owner == step, tile, part)
            sums = sums + tile
        parts.append(part)
    return parts, sums


def solve_coarse(parts, matrix_ref, near_rows, cdiags):
    rows = parts[0].shape[0] - 1
    vector = jnp.concatenate([part[at : at + 1] for part in parts for at in range(rows)], axis=1)
    product = lax.dot_general(
        jnp.broadcast_to(vector, (8, vector.shape[1])).astype(bf16), matrix_ref[...],
        (((1,), (1,)), ((), ())), preferred_element_type=f32,
    )[0:1]
    low = product[:, :LANES]
    high = jnp.concatenate([product[:, LANES:], jnp.zeros((1, LANES - SLOT), f32)], axis=1)
    return [
        cdiag * row + share for cdiag, row, share in zip(cdiags, near_rows, (low, turned(low), high))
    ]


def rows_near(got_ref, grp_size):
    count = got_ref.shape[0]
    me = lax.axis_index("sub") * grp_size + lax.axis_index("grp")
    shifts = [0] + [grp_size * (1 - 2 * parity(side)) for side in (0, 1)]
    return [got_ref[lax.rem(me + shift + count, count)][0:1] for shift in shifts]


def spread_of(solution, agg):
    wide = jnp.broadcast_to(solution, (8, LANES))
    return jnp.take_along_axis(wide, jnp.broadcast_to(agg, (8, LANES)), axis=1)[0:1]


def cdiags_of(cdiag_ref, near_refs, size):
    cpd = cdiag_ref.shape[1]
    own = jnp.concatenate([cdiag_ref[...], jnp.zeros((1, LANES - cpd), f32)], axis=1)
    return [own] + [ref[size : size + 1, :] for ref in near_refs]


def near_spread(constants_ref, solution, size):
    agg = constants_ref[2 * size : 2 * size + 1, :].astype(jnp.int32)
    return constants_ref[size : 2 * size, :] * spread_of(solution, agg)


def first_step(got_ref, even_near_ref, odd_near_ref, even_const_ref, odd_const_ref, matrix_ref,
               cdiag_ref, first_ref, lead_ref, pull_ref, jscale_ref, prolong_ref, agg_ref,
               arrive_ref, gather_ref, send_ref, grp_size,
               basis_ref, direction_ref, image_ref, out_ref, even_ref, odd_ref):
    size = first_ref.shape[0]
    cpd = cdiag_ref.shape[1]
    parts, sums = compact(got_ref, cpd)
    rows = sums.shape[0]
    inverse = 1.0 / jnp.sqrt(sums[rows - 1 : rows])
    own_rows = [row * inverse for row in rows_near(got_ref, grp_size)]
    near_refs = (even_near_ref, odd_near_ref)
    solved = solve_coarse([part * inverse for part in parts], matrix_ref, own_rows,
                          cdiags_of(cdiag_ref, near_refs, size))
    basis = first_ref[...] * inverse
    basis_ref[...] = basis
    spread = spread_of(solved[0], agg_ref[...])
    jscale, prolong = jscale_ref[...], prolong_ref[...]
    direction_ref[...] = jscale * basis + prolong * spread
    near = [
        ref[0:size, :] * inverse + near_spread(const, part, size)
        for ref, const, part in zip(near_refs, (even_const_ref, odd_const_ref), solved[1:])
    ]
    image = lead_ref[...] * inverse + pull_ref[...] * spread - coupling * received(near, arrive_ref)
    image_ref[...] = image
    weighted = jnp.sum(prolong * image, axis=0, keepdims=True)
    dots = halves(total(basis * image), total(image * image))
    to_all(out_ref, restricted(weighted, gather_ref) + [dots])
    scaled = jscale * image
    for side, ref in enumerate((even_ref, odd_ref)):
        ref[...] = pick(scaled, row_of(send_ref, parity(side)))


def second_step(got_ref, first_got_ref, even_near_ref, odd_near_ref, even_first_ref, odd_first_ref,
                even_const_ref, odd_const_ref, matrix_ref, cdiag_ref, basis_ref, image_ref,
                lead_ref, lead_two_ref, pull_ref, jscale_ref, prolong_ref, agg_ref, arrive_ref,
                grp_size, basis_two_ref, direction_ref, image_two_ref, scalars_ref, out_ref):
    size = basis_ref.shape[0]
    cpd = cdiag_ref.shape[1]
    first_parts, first_sums = compact(first_got_ref, cpd)
    parts, sums = compact(got_ref, cpd)
    rows = sums.shape[0]
    beta = jnp.sqrt(first_sums[rows - 1 : rows])
    totals = sums[rows - 1 : rows]
    swapped = turned(totals)
    along, energy = halves(totals, swapped), halves(swapped, totals)
    height = jnp.sqrt(jnp.maximum(energy - along * along, 0.01 * energy))
    inverse = 1.0 / height
    slope = along / beta

    def mixed(new, old):
        return (new - slope * old) * inverse

    own_rows = [
        mixed(new, old)
        for new, old in zip(rows_near(got_ref, grp_size), rows_near(first_got_ref, grp_size))
    ]
    near_first = (even_first_ref, odd_first_ref)
    solved = solve_coarse([mixed(new, old) for new, old in zip(parts, first_parts)], matrix_ref,
                          own_rows, cdiags_of(cdiag_ref, near_first, size))
    basis = (image_ref[...] - along * basis_ref[...]) * inverse
    basis_two_ref[...] = basis
    spread = spread_of(solved[0], agg_ref[...])
    direction_ref[...] = jscale_ref[...] * basis + prolong_ref[...] * spread
    near = [
        mixed(ref[...], first[0:size, :]) + near_spread(const, part, size)
        for ref, first, const, part in zip(
            (even_near_ref, odd_near_ref), near_first, (even_const_ref, odd_const_ref), solved[1:]
        )
    ]
    image = mixed(lead_two_ref[...], lead_ref[...]) + pull_ref[...] * spread
    image = image - coupling * received(near, arrive_ref)
    image_two_ref[...] = image
    scalars_ref[...] = jnp.concatenate([beta, along, height, jnp.zeros((5, LANES), f32)], axis=0)
    to_all(out_ref, [total(basis_ref[...] * image), total(basis * image), total(image * image),
                     jnp.zeros((1, LANES), f32)])


def finish(got_ref, scalars_ref, guess_ref, basis_ref, basis_two_ref, direction_ref,
           direction_two_ref, image_ref, solution_ref, next_ref):
    beta, h11, h21 = scalars_ref[0:1, :], scalars_ref[1:2, :], scalars_ref[2:3, :]
    totals = jnp.sum(got_ref[...], axis=0)
    h12, h22, energy = totals[0:1], totals[1:2], totals[2:3]
    h32 = jnp.sqrt(jnp.maximum(energy - (h12 * h12 + h22 * h22), 0.01 * energy))
    g00 = h11 * h11 + h21 * h21
    g01 = h11 * h12 + h21 * h22
    g11 = h12 * h12 + h22 * h22 + h32 * h32
    t0, t1 = beta * h11, beta * h12
    factor = g01 / g00
    c1 = (t1 - factor * t0) / (g11 - factor * g01)
    c0 = (t0 - g01 * c1) / g00
    solution_ref[...] = guess_ref[...] + c0 * direction_ref[...] + c1 * direction_two_ref[...]
    next_ref[...] = (image_ref[...] - h12 * basis_ref[...] - h22 * basis_two_ref[...]) * (1.0 / h32)


def on_device(rhs, guess, blocks, valve, jscale, prolong, agg_map, cdiag, coff, send_rows,
              recv_rows, live_counts):
    rhs, guess, blocks, jscale, prolong = rhs[0, 0], guess[0, 0], blocks[0, 0], jscale[0, 0], prolong[0, 0]
    valve, agg, live = valve[0], agg_map[0], live_counts[0]
    send, recv = send_rows[0, 0], recv_rows[0, 0]
    size, count = guess.shape
    slots = send.shape[1]
    cpd = cdiag.shape[0]
    subs, grps = lax.axis_size("sub"), lax.axis_size("grp")
    devices = subs * grps
    period = math.lcm(cpd, LANES)
    cdiag = cdiag[None, :]
    moves = [pairing(subs, grps, side) for side in (0, 1)]

    def exchange(even, odd):
        odd = lax.ppermute(odd, AXES, moves[1])
        return lax.ppermute(even, AXES, moves[0]), odd

    def everyone(rows):
        return lax.all_to_all(rows, AXES, 0, 0, tiled=True)

    field = ((size, count), f32)
    near = ((size, slots), f32)
    rows_out = ((devices, period // LANES + 1, LANES), f32)
    packed = ((2 * size + 8, slots), f32)
    even, odd = call(
        first_send, [packed, packed], guess, prolong, agg, send, hbm=(0, 1, 2, 3), limit=56,
        scratch=[
            pltpu.VMEM(guess.shape, f32), pltpu.VMEM(prolong.shape, f32),
            pltpu.VMEM(agg.shape, jnp.int32), pltpu.VMEM(send.shape, jnp.int32),
            pltpu.SemaphoreType.DMA((4,)),
        ],
    )
    even_const, odd_const = exchange(even, odd)
    coff_even, coff_odd = exchange(coff, coff)
    local, arrive, gather = call(
        lambda *refs: prepare(*refs[:7], cpd, *refs[7:]),
        [field, ((2 * slots, count), bf16), ((count, period), bf16)],
        live, guess, rhs, blocks, valve, agg, recv, smem=(0,),
    )
    packed = ((size + 8, slots), f32)
    first, rows, even, odd = call(
        residual, [field, rows_out, packed, packed],
        local, even_const, odd_const, arrive, gather, prolong, jscale, send, cdiag,
    )
    even_first, odd_first = exchange(even, odd)
    first_got = everyone(rows)
    lead, pull, matrix = call(
        look_ahead, [field, field, ((3 * SLOT, coff.shape[1]), bf16)],
        first, jscale, prolong, blocks, valve, coff, coff_even, coff_odd,
    )
    basis, direction, image, rows, even, odd = call(
        lambda *refs: first_step(*refs[:16], grps, *refs[16:]),
        [field, field, field, rows_out, near, near],
        first_got, even_first, odd_first, even_const, odd_const, matrix, cdiag, first, lead, pull,
        jscale, prolong, agg, arrive, gather, send,
    )
    even_near, odd_near = exchange(even, odd)
    got = everyone(rows)
    (lead_two,) = call(look_further, [field], image, jscale, blocks, valve)
    basis_two, direction_two, image_two, scalars, rows = call(
        lambda *refs: second_step(*refs[:19], grps, *refs[19:]),
        [field, field, field, ((8, LANES), f32), ((devices, 4, LANES), f32)],
        got, first_got, even_near, odd_near, even_first, odd_first, even_const, odd_const, matrix,
        cdiag, basis, image, lead, lead_two, pull, jscale, prolong, agg, arrive,
    )
    got = everyone(rows)
    solution, next_basis = call(
        finish, [field, field],
        got, scalars, guess, basis, basis_two, direction, direction_two, image_two,
    )
    return solution[None, None], next_basis[None, None]


def solution(mesh):
    return jax.shard_map(
        on_device,
        mesh=mesh,
        in_specs=(
            P("sub", "grp", None, None),
            P("sub", "grp", None, None),
            P("sub", "grp", None, None, None),
            P("sub", "grp", None),
            P("sub", "grp", None, None),
            P("sub", "grp", None, None),
            P("sub", "grp", None),
            P(("sub", "grp")),
            P(("sub", "grp"), None),
            P("sub", "grp", None, None),
            P("sub", "grp", None, None),
            P("sub", "grp", None),
        ),
        out_specs=(P("sub", "grp", None, None), P("sub", "grp", None, None)),
        check_vma=False,
    )
```

```python
import math

import jax
import jax.numpy as jnp
from jax import lax
from jax.experimental import pallas as pl
from jax.experimental.pallas import tpu as pltpu
from jax.sharding import PartitionSpec as P

penalty_gain = 3.0
coupling = 0.5

LANES = 128
SLOT = 64
AXES = ("sub", "grp")
f32 = jnp.float32
bf16 = jnp.bfloat16

SEND, RECV, AGG, VALVE = slice(0, 2), slice(2, 4), slice(4, 5), slice(5, 6)


def call(body, outs, *args, smem=(), hbm=(), scratch=(), limit=32, final=False, aliases=None):
    def spec(at):
        if at in hbm:
            return pl.BlockSpec(memory_space=pltpu.HBM)
        return pl.BlockSpec(memory_space=pltpu.SMEM if at in smem else pltpu.VMEM)

    args = [
        pltpu.with_memory_space_constraint(arg, pltpu.HBM) if at in hbm else arg
        for at, arg in enumerate(args)
    ]
    return pl.pallas_call(
        body,
        out_shape=[
            jax.ShapeDtypeStruct(shape, kind) if final else pltpu.VMEM(shape, kind)
            for shape, kind in outs
        ],
        in_specs=[spec(at) for at in range(len(args))],
        out_specs=[pl.BlockSpec(memory_space=pltpu.VMEM)] * len(outs),
        scratch_shapes=list(scratch),
        input_output_aliases=aliases or {},
        compiler_params=pltpu.CompilerParams(vmem_limit_bytes=limit * 1024 * 1024),
    )(*args)


def partner(place, side):
    return place - 1 + 2 * ((place + side) % 2)


def pairing(subs, grps, side):
    moves = []
    for place in range(subs):
        other = partner(place, side)
        for group in range(grps):
            if 0 <= other < subs:
                target = other * grps + group
            else:
                target = place * grps + (group ^ 1 if group ^ 1 < grps else group)
            moves.append((place * grps + group, target))
    return moves


def row_of(ref, flipped):
    return jnp.where(flipped == 0, ref[0:1, :], ref[1:2, :])


def parity(side):
    return (lax.axis_index("sub") + side + 1) % 2


def pick(field, places):
    return jnp.take_along_axis(field, jnp.broadcast_to(places, field.shape), axis=1)


def pieces(field):
    high = field.astype(bf16)
    return high, (field - high.astype(f32)).astype(bf16)


def block_rows(blocks, field):
    return jnp.sum(blocks.astype(f32) * field[None], axis=1)


def local_product(blocks_ref, valve, field):
    rows = [block_rows(blocks_ref[at : at + 8], field) for at in range(0, blocks_ref.shape[0], 8)]
    return jnp.concatenate(rows, axis=0) + penalty_gain * valve.astype(f32) * field


def received(near, arrive_ref):
    high, low = pieces(jnp.concatenate(near, axis=1))
    both = jnp.dot(
        jnp.concatenate([high, low], axis=0), arrive_ref[...], preferred_element_type=f32
    )
    count = near[0].shape[0]
    return both[:count] + both[count:]


def restricted(weighted, gather_ref):
    high = weighted.astype(bf16).astype(f32)
    rest = weighted - high
    middle = rest.astype(bf16).astype(f32)
    last = rest - middle
    row = lax.broadcasted_iota(jnp.int32, (8, weighted.shape[1]), 0)
    stack = jnp.where(row == 0, high, jnp.where(row == 1, middle, jnp.where(row == 2, last, 0.0)))
    sums = jnp.dot(stack.astype(bf16), gather_ref[...], preferred_element_type=f32)
    sums = jnp.sum(sums, axis=0, keepdims=True)
    return [sums[:, at : at + LANES] for at in range(0, sums.shape[1], LANES)]


def total(field):
    value = jnp.sum(jnp.sum(field, axis=0, keepdims=True), axis=1, keepdims=True)
    return jnp.broadcast_to(value, (1, LANES))


def halves(first, second):
    return jnp.where(lax.broadcasted_iota(jnp.int32, (1, LANES), 1) < LANES // 2, first, second)


def turned(row):
    return pltpu.roll(jnp.broadcast_to(row, (8, LANES)), LANES // 2, 1)[0:1]


def to_all(ref, rows):
    ref[...] = jnp.broadcast_to(jnp.concatenate(rows, axis=0)[None], ref.shape)


def copy_all(pairs, sems):
    copies = [pltpu.make_async_copy(*pair, sems.at[at]) for at, pair in enumerate(pairs)]
    for copy in copies:
        copy.start()
    return copies


def first_send(guess_hbm, agg_hbm, send_hbm, recv_hbm, valve_hbm, odd_ref, even_ref, notes_ref,
               guess_ref, agg_ref, send_ref, recv_ref, valve_ref, sems):
    pairs = (
        (send_hbm, send_ref), (guess_hbm, guess_ref), (agg_hbm, agg_ref), (recv_hbm, recv_ref),
        (valve_hbm, valve_ref),
    )
    for copy in copy_all(pairs, sems):
        copy.wait()
    for side, ref in enumerate((odd_ref, even_ref)):
        ref[...] = pick(guess_ref[...], row_of(send_ref, parity(side)))
    notes_ref[...] = jnp.concatenate(
        [send_ref[...], recv_ref[...], agg_ref[...], valve_ref[...], jnp.zeros((2, LANES), jnp.int32)],
        axis=0,
    )


def wide(row):
    return jnp.concatenate([row, jnp.zeros((1, LANES - row.shape[1]), row.dtype)], axis=1)


def pack_constants(ref, coff_ref, prolong, agg, cdiag, places):
    cpd, width = coff_ref.shape
    for at in range(0, width, LANES):
        start = at // LANES * cpd
        ref[start : start + cpd, :] = coff_ref[:, at : at + LANES]
    base = cpd * (width // LANES)
    high, low = pieces(pick(prolong, places))
    size = high.shape[0]
    ref[base : base + size, :] = high
    ref[base + size : base + 2 * size, :] = low
    listed = pick(jnp.broadcast_to(agg.astype(f32), (8, LANES)), places)[0:1]
    one = cdiag.astype(bf16).astype(f32)
    two = (cdiag - one).astype(bf16).astype(f32)
    rows = [listed, one, two, cdiag - one - two, jnp.zeros((12, LANES), f32)]
    ref[base + 2 * size : base + 2 * size + 16, :] = jnp.concatenate(rows, axis=0).astype(bf16)


def prepare(live_hbm, guess_hbm, rhs_hbm, blocks_hbm, coff_hbm, prolong_hbm, cdiag_hbm, notes_ref,
            cpd, local_ref, arrive_ref, gather_ref, odd_ref, even_ref,
            live_ref, guess_ref, rhs_ref, blocks_ref, coff_ref, prolong_ref, cdiag_ref, sems):
    size = guess_ref.shape[0]
    chunk = size // 4
    pairs = [(coff_hbm, coff_ref), (prolong_hbm, prolong_ref), (cdiag_hbm, cdiag_ref),
             (live_hbm, live_ref), (guess_hbm, guess_ref)]
    for at in range(0, size, chunk):
        pairs.append((blocks_hbm.at[at : at + chunk], blocks_ref.at[at : at + chunk]))
    copies = copy_all(pairs + [(rhs_hbm, rhs_ref)], sems)
    for copy in copies[:4]:
        copy.wait()
    cdiag = wide(cdiag_ref[...])
    for side, ref in enumerate((odd_ref, even_ref)):
        places = row_of(notes_ref.at[SEND], parity(side))
        pack_constants(ref, coff_ref, prolong_ref[...], notes_ref[AGG], cdiag, places)
    count = arrive_ref.shape[1]
    slots = notes_ref.shape[1]
    period = gather_ref.shape[1]
    coarse = lax.rem(lax.broadcasted_iota(jnp.int32, (period, count), 0), cpd)
    gather_ref[...] = jnp.where(notes_ref[AGG] == coarse, 1.0, 0.0).T.astype(bf16)
    place = lax.axis_index("sub")
    row = lax.broadcasted_iota(jnp.int32, (count, slots), 0)
    slot = lax.broadcasted_iota(jnp.int32, (count, slots), 1)
    for side in (0, 1):
        other = place + 1 - 2 * parity(side)
        there = (other >= 0) & (other < lax.axis_size("sub"))
        which = 1 - parity(side)
        live = jnp.where(there, live_ref[0, which], 0)
        hit = (row_of(notes_ref.at[RECV], which) == row) & (slot < live)
        arrive_ref[side * slots : (side + 1) * slots, :] = jnp.where(hit, 1.0, 0.0).T.astype(bf16)
    copies[4].wait()
    guess = guess_ref[...]
    penalty = penalty_gain * notes_ref[VALVE].astype(f32)
    for at in range(0, size, 8):
        if at % chunk == 0:
            copies[5 + at // chunk].wait()
        part = slice(at, at + 8)
        local_ref[part, :] = block_rows(blocks_ref[part], guess) + penalty * guess[part]
    copies[-1].wait()
    local_ref[...] = rhs_ref[...] - local_ref[...]


def hand_on(odd_ref, even_ref, odd_after_ref, even_after_ref, odd_out_ref, even_out_ref):
    pass


def residual(local_ref, odd_near_ref, even_near_ref, arrive_ref, gather_ref, prolong_ref,
             jscale_ref, notes_ref, first_ref, out_ref, odd_ref, even_ref):
    near = [odd_near_ref[...], even_near_ref[...]]
    first = local_ref[...] + coupling * received(near, arrive_ref)
    first_ref[...] = first
    weighted = jnp.sum(prolong_ref[...] * first, axis=0, keepdims=True)
    to_all(out_ref, restricted(weighted, gather_ref) + [total(first * first)])
    scaled = jscale_ref[...] * first
    for side, ref in enumerate((odd_ref, even_ref)):
        ref[...] = pick(scaled, row_of(notes_ref.at[SEND], parity(side)))


def look_ahead(first_ref, jscale_ref, prolong_ref, blocks_ref, notes_ref, own_ref, odd_ref,
               even_ref, cpd, lead_ref, pull_ref, matrix_ref, odd_weights_ref, even_weights_ref,
               info_ref):
    lead_ref[...] = local_product(blocks_ref, notes_ref[VALVE], jscale_ref[...] * first_ref[...])
    pull_ref[...] = local_product(blocks_ref, notes_ref[VALVE], prolong_ref[...])
    width = matrix_ref.shape[1]
    size = first_ref.shape[0]
    base = cpd * (width // LANES)
    rows = []
    for slot, ref in enumerate((own_ref, odd_ref, even_ref)):
        for at in range(0, width, LANES):
            start = at // LANES * cpd
            matrix_ref[slot * SLOT : slot * SLOT + cpd, at : at + LANES] = ref[start : start + cpd, :]
        matrix_ref[slot * SLOT + cpd : (slot + 1) * SLOT, :] = jnp.zeros((SLOT - cpd, width), bf16)
        rows.append(ref[base + 2 * size : base + 2 * size + 16, :].astype(f32))
    for ref, weights_ref in ((odd_ref, odd_weights_ref), (even_ref, even_weights_ref)):
        weights_ref[...] = ref[base : base + size, :].astype(f32) + ref[
            base + size : base + 2 * size, :
        ].astype(f32)
    infos = [row[1:2] + row[2:3] + row[3:4] for row in rows] + [row[0:1] for row in rows[1:]]
    info_ref[...] = jnp.concatenate(infos + [jnp.zeros((3, LANES), f32)], axis=0)


def look_further(image_ref, jscale_ref, blocks_ref, notes_ref, lead_ref):
    lead_ref[...] = local_product(blocks_ref, notes_ref[VALVE], jscale_ref[...] * image_ref[...])


def compact(got_ref, cpd):
    count, rows, _ = got_ref.shape
    shape = (rows, LANES)
    place = lax.broadcasted_iota(jnp.int32, shape, 0) * LANES + lax.broadcasted_iota(jnp.int32, shape, 1)
    owner = place // cpd
    group = (rows - 1) * LANES // cpd
    parts, sums = [], jnp.zeros(shape, f32)
    for at in range(0, count, group):
        part = jnp.zeros(shape, f32)
        for step in range(group):
            tile = got_ref[at + step]
            part = jnp.where(owner == step, tile, part)
            sums = sums + tile
        parts.append(part)
    return parts, sums


def solve_coarse(parts, matrix_ref, near_rows, info_ref):
    rows = parts[0].shape[0] - 1
    vector = jnp.concatenate([part[at : at + 1] for part in parts for at in range(rows)], axis=1)
    product = lax.dot_general(
        jnp.broadcast_to(vector, (8, vector.shape[1])).astype(bf16), matrix_ref[...],
        (((1,), (1,)), ((), ())), preferred_element_type=f32,
    )[0:1]
    low = product[:, :LANES]
    high = jnp.concatenate([product[:, LANES:], jnp.zeros((1, LANES - SLOT), f32)], axis=1)
    shares = (low, turned(low), high)
    return [
        info_ref[at : at + 1, :] * row + share
        for at, (row, share) in enumerate(zip(near_rows, shares))
    ]


def rows_near(got_ref, grp_size):
    count = got_ref.shape[0]
    me = lax.axis_index("sub") * grp_size + lax.axis_index("grp")
    shifts = [0] + [grp_size * (1 - 2 * parity(side)) for side in (0, 1)]
    return [got_ref[lax.rem(me + shift + count, count)][0:1] for shift in shifts]


def spread_of(solution, agg):
    wide = jnp.broadcast_to(solution, (8, LANES))
    return jnp.take_along_axis(wide, jnp.broadcast_to(agg, (8, LANES)), axis=1)[0:1]


def near_spread(weights_ref, info_ref, side, solution):
    agg = info_ref[3 + side : 4 + side, :].astype(jnp.int32)
    return weights_ref[...] * spread_of(solution, agg)


def first_step(got_ref, odd_near_ref, even_near_ref, odd_weights_ref, even_weights_ref, matrix_ref,
               info_ref, first_ref, lead_ref, pull_ref, jscale_ref, prolong_ref, notes_ref,
               arrive_ref, gather_ref, grp_size, cpd,
               basis_ref, direction_ref, image_ref, out_ref, odd_ref, even_ref):
    parts, sums = compact(got_ref, cpd)
    rows = sums.shape[0]
    inverse = 1.0 / jnp.sqrt(sums[rows - 1 : rows])
    own_rows = [row * inverse for row in rows_near(got_ref, grp_size)]
    solved = solve_coarse([part * inverse for part in parts], matrix_ref, own_rows, info_ref)
    basis = first_ref[...] * inverse
    basis_ref[...] = basis
    spread = spread_of(solved[0], notes_ref[AGG])
    jscale, prolong = jscale_ref[...], prolong_ref[...]
    direction_ref[...] = jscale * basis + prolong * spread
    near = [
        odd_near_ref[...] * inverse + near_spread(odd_weights_ref, info_ref, 0, solved[1]),
        even_near_ref[...] * inverse + near_spread(even_weights_ref, info_ref, 1, solved[2]),
    ]
    image = lead_ref[...] * inverse + pull_ref[...] * spread - coupling * received(near, arrive_ref)
    image_ref[...] = image
    weighted = jnp.sum(prolong * image, axis=0, keepdims=True)
    dots = halves(total(basis * image), total(image * image))
    to_all(out_ref, restricted(weighted, gather_ref) + [dots])
    scaled = jscale * image
    for side, ref in enumerate((odd_ref, even_ref)):
        ref[...] = pick(scaled, row_of(notes_ref.at[SEND], parity(side)))


def second_step(got_ref, first_got_ref, odd_near_ref, even_near_ref, odd_first_ref, even_first_ref,
                odd_weights_ref, even_weights_ref, matrix_ref, info_ref, basis_ref, image_ref,
                lead_ref, lead_two_ref, pull_ref, jscale_ref, prolong_ref, notes_ref, arrive_ref,
                grp_size, cpd, basis_two_ref, direction_ref, image_two_ref, scalars_ref, out_ref):
    first_parts, first_sums = compact(first_got_ref, cpd)
    parts, sums = compact(got_ref, cpd)
    rows = sums.shape[0]
    beta = jnp.sqrt(first_sums[rows - 1 : rows])
    totals = sums[rows - 1 : rows]
    swapped = turned(totals)
    along, energy = halves(totals, swapped), halves(swapped, totals)
    height = jnp.sqrt(jnp.maximum(energy - along * along, 0.01 * energy))
    inverse = 1.0 / height
    slope = along / beta

    def mixed(new, old):
        return (new - slope * old) * inverse

    own_rows = [
        mixed(new, old)
        for new, old in zip(rows_near(got_ref, grp_size), rows_near(first_got_ref, grp_size))
    ]
    solved = solve_coarse(
        [mixed(new, old) for new, old in zip(parts, first_parts)], matrix_ref, own_rows, info_ref
    )
    basis = (image_ref[...] - along * basis_ref[...]) * inverse
    basis_two_ref[...] = basis
    spread = spread_of(solved[0], notes_ref[AGG])
    direction_ref[...] = jscale_ref[...] * basis + prolong_ref[...] * spread
    near = [
        mixed(odd_near_ref[...], odd_first_ref[...])
        + near_spread(odd_weights_ref, info_ref, 0, solved[1]),
        mixed(even_near_ref[...], even_first_ref[...])
        + near_spread(even_weights_ref, info_ref, 1, solved[2]),
    ]
    image = mixed(lead_two_ref[...], lead_ref[...]) + pull_ref[...] * spread
    image = image - coupling * received(near, arrive_ref)
    image_two_ref[...] = image
    scalars_ref[...] = jnp.concatenate([beta, along, height, jnp.zeros((5, LANES), f32)], axis=0)
    to_all(out_ref, [total(basis_ref[...] * image), total(basis * image), total(image * image),
                     jnp.zeros((1, LANES), f32)])


def finish(got_ref, scalars_ref, guess_ref, basis_ref, basis_two_ref, direction_ref,
           direction_two_ref, image_ref, solution_ref, next_ref):
    beta, h11, h21 = scalars_ref[0:1, :], scalars_ref[1:2, :], scalars_ref[2:3, :]
    totals = jnp.sum(got_ref[...], axis=0)
    h12, h22, energy = totals[0:1], totals[1:2], totals[2:3]
    h32 = jnp.sqrt(jnp.maximum(energy - (h12 * h12 + h22 * h22), 0.01 * energy))
    g00 = h11 * h11 + h21 * h21
    g01 = h11 * h12 + h21 * h22
    g11 = h12 * h12 + h22 * h22 + h32 * h32
    t0, t1 = beta * h11, beta * h12
    factor = g01 / g00
    c1 = (t1 - factor * t0) / (g11 - factor * g01)
    c0 = (t0 - g01 * c1) / g00
    solution_ref[...] = guess_ref[...] + c0 * direction_ref[...] + c1 * direction_two_ref[...]
    next_ref[...] = (image_ref[...] - h12 * basis_ref[...] - h22 * basis_two_ref[...]) * (1.0 / h32)


def on_device(rhs, guess, blocks, valve, jscale, prolong, agg_map, cdiag, coff, send_rows,
              recv_rows, live_counts):
    rhs, guess, blocks, jscale, prolong = rhs[0, 0], guess[0, 0], blocks[0, 0], jscale[0, 0], prolong[0, 0]
    valve, agg, live = valve[0], agg_map[0], live_counts[0]
    send, recv = send_rows[0, 0], recv_rows[0, 0]
    size, count = guess.shape
    slots = send.shape[1]
    cpd = cdiag.shape[0]
    subs, grps = lax.axis_size("sub"), lax.axis_size("grp")
    devices = subs * grps
    period = math.lcm(cpd, LANES)
    cdiag = cdiag[None, :]
    moves = [pairing(subs, grps, side) for side in (0, 1)]

    def exchange(odd, even):
        return lax.ppermute(odd, AXES, moves[0]), lax.ppermute(even, AXES, moves[1])

    def everyone(rows):
        return lax.all_to_all(rows, AXES, 0, 0, tiled=True)

    field = ((size, count), f32)
    near = ((size, slots), f32)
    rows_out = ((devices, period // LANES + 1, LANES), f32)
    small = ((8, LANES), f32)
    items = (guess, agg, send, recv, valve)
    odd, even, notes = call(
        first_send, [near, near, ((8, LANES), jnp.int32)], *items, hbm=range(5), limit=16,
        scratch=[pltpu.VMEM(item.shape, item.dtype) for item in items]
        + [pltpu.SemaphoreType.DMA((5,))],
    )
    odd_guess, even_guess = exchange(odd, even)
    packed = ((cpd * (coff.shape[1] // LANES) + 2 * size + 16, LANES), bf16)
    items = (guess, rhs, blocks, coff, prolong, cdiag)
    local, arrive, gather, odd, even = call(
        lambda *refs: prepare(*refs[:8], cpd, *refs[8:]),
        [field, ((2 * slots, count), bf16), ((count, period), bf16), packed, packed],
        live, *items, notes, hbm=range(7),
        scratch=[pltpu.SMEM(live.shape, live.dtype)]
        + [pltpu.VMEM(item.shape, item.dtype) for item in items]
        + [pltpu.SemaphoreType.DMA((10,))],
    )
    odd, even = call(
        hand_on, [packed, packed], odd, even, odd_guess, even_guess, aliases={0: 0, 1: 1}
    )
    odd_pack, even_pack = exchange(odd, even)
    own_pack = odd
    first, rows, odd, even = call(
        residual, [field, rows_out, near, near],
        local, odd_guess, even_guess, arrive, gather, prolong, jscale, notes,
    )
    odd_first, even_first = exchange(odd, even)
    first_got = everyone(rows)
    lead, pull, matrix, odd_weights, even_weights, info = call(
        lambda *refs: look_ahead(*refs[:8], cpd, *refs[8:]), [field, field, ((3 * SLOT, coff.shape[1]), bf16), near, near, small],
        first, jscale, prolong, blocks, notes, own_pack, odd_pack, even_pack,
    )
    basis, direction, image, rows, odd, even = call(
        lambda *refs: first_step(*refs[:15], grps, cpd, *refs[15:]),
        [field, field, field, rows_out, near, near],
        first_got, odd_first, even_first, odd_weights, even_weights, matrix, info, first, lead, pull,
        jscale, prolong, notes, arrive, gather,
    )
    odd_near, even_near = exchange(odd, even)
    got = everyone(rows)
    (lead_two,) = call(look_further, [field], image, jscale, blocks, notes)
    basis_two, direction_two, image_two, scalars, rows = call(
        lambda *refs: second_step(*refs[:19], grps, cpd, *refs[19:]),
        [field, field, field, ((8, LANES), f32), ((devices, 4, LANES), f32)],
        got, first_got, odd_near, even_near, odd_first, even_first, odd_weights, even_weights, matrix,
        info, basis, image, lead, lead_two, pull, jscale, prolong, notes, arrive,
    )
    got = everyone(rows)
    solution, next_basis = call(
        finish, [field, field],
        got, scalars, guess, basis, basis_two, direction, direction_two, image_two, final=True,
    )
    return solution[None, None], next_basis[None, None]


def solution(mesh):
    return jax.shard_map(
        on_device,
        mesh=mesh,
        in_specs=(
            P("sub", "grp", None, None),
            P("sub", "grp", None, None),
            P("sub", "grp", None, None, None),
            P("sub", "grp", None),
            P("sub", "grp", None, None),
            P("sub", "grp", None, None),
            P("sub", "grp", None),
            P(("sub", "grp")),
            P(("sub", "grp"), None),
            P("sub", "grp", None, None),
            P("sub", "grp", None, None),
            P("sub", "grp", None),
        ),
        out_specs=(P("sub", "grp", None, None), P("sub", "grp", None, None)),
        check_vma=False,
    )
```

```python
import math

import jax
import jax.numpy as jnp
from jax import lax
from jax.experimental import pallas as pl
from jax.experimental.pallas import tpu as pltpu
from jax.sharding import PartitionSpec as P

penalty_gain = 3.0
coupling = 0.5

LANES = 128
SLOT = 64
AXES = ("sub", "grp")
f32 = jnp.float32
bf16 = jnp.bfloat16

SEND, RECV, AGG, VALVE = slice(0, 2), slice(2, 4), slice(4, 5), slice(5, 6)


def call(body, outs, *args, smem=(), hbm=(), scratch=(), limit=32, final=False, aliases=None):
    def spec(at):
        if at in hbm:
            return pl.BlockSpec(memory_space=pltpu.HBM)
        return pl.BlockSpec(memory_space=pltpu.SMEM if at in smem else pltpu.VMEM)

    args = [
        pltpu.with_memory_space_constraint(arg, pltpu.HBM) if at in hbm else arg
        for at, arg in enumerate(args)
    ]
    return pl.pallas_call(
        body,
        out_shape=[
            jax.ShapeDtypeStruct(shape, kind) if final else pltpu.VMEM(shape, kind)
            for shape, kind in outs
        ],
        in_specs=[spec(at) for at in range(len(args))],
        out_specs=[pl.BlockSpec(memory_space=pltpu.VMEM)] * len(outs),
        scratch_shapes=list(scratch),
        input_output_aliases=aliases or {},
        compiler_params=pltpu.CompilerParams(vmem_limit_bytes=limit * 1024 * 1024),
    )(*args)


def partner(place, side):
    return place - 1 + 2 * ((place + side) % 2)


def pairing(subs, grps, side):
    moves = []
    for place in range(subs):
        other = partner(place, side)
        for group in range(grps):
            if 0 <= other < subs:
                target = other * grps + group
            else:
                target = place * grps + (group ^ 1 if group ^ 1 < grps else group)
            moves.append((place * grps + group, target))
    return moves


def row_of(ref, flipped):
    return jnp.where(flipped == 0, ref[0:1, :], ref[1:2, :])


def parity(side):
    return (lax.axis_index("sub") + side + 1) % 2


def pick(field, places):
    return jnp.take_along_axis(field, jnp.broadcast_to(places, field.shape), axis=1)


def pieces(field):
    high = field.astype(bf16)
    return high, (field - high.astype(f32)).astype(bf16)


def block_rows(blocks, field):
    return jnp.sum(blocks.astype(f32) * field[None], axis=1)


def local_product(blocks_ref, valve, field):
    rows = [block_rows(blocks_ref[at : at + 8], field) for at in range(0, blocks_ref.shape[0], 8)]
    return jnp.concatenate(rows, axis=0) + penalty_gain * valve.astype(f32) * field


def received(near, arrive_ref):
    high, low = pieces(jnp.concatenate(near, axis=1))
    both = jnp.dot(
        jnp.concatenate([high, low], axis=0), arrive_ref[...], preferred_element_type=f32
    )
    count = near[0].shape[0]
    return both[:count] + both[count:]


def restricted(weighted, gather_ref):
    high = weighted.astype(bf16).astype(f32)
    rest = weighted - high
    middle = rest.astype(bf16).astype(f32)
    last = rest - middle
    row = lax.broadcasted_iota(jnp.int32, (8, weighted.shape[1]), 0)
    stack = jnp.where(row == 0, high, jnp.where(row == 1, middle, jnp.where(row == 2, last, 0.0)))
    sums = jnp.dot(stack.astype(bf16), gather_ref[...], preferred_element_type=f32)
    return jnp.sum(sums, axis=0, keepdims=True)


def total(field):
    return jnp.sum(jnp.sum(field, axis=0, keepdims=True), axis=1, keepdims=True)


def to_all(ref, row, first_lane, totals):
    lane = lax.broadcasted_iota(jnp.int32, (1, LANES), 1)
    for at, value in enumerate(totals):
        row = jnp.where(lane == first_lane + at, value, row)
    ref[...] = jnp.broadcast_to(row, ref.shape)


def flat(ref):
    return ref[...] if len(ref.shape) == 2 else ref[:, 0, :]


def summed(ref, first_lane, count):
    rows = jnp.broadcast_to(jnp.sum(flat(ref), axis=0, keepdims=True), (8, LANES))
    return [
        jnp.take_along_axis(rows, jnp.full((8, LANES), first_lane + at, jnp.int32), axis=1)[0:1]
        for at in range(count)
    ]


def copy_all(pairs, sems):
    copies = [pltpu.make_async_copy(*pair, sems.at[at]) for at, pair in enumerate(pairs)]
    for copy in copies:
        copy.start()
    return copies


def first_send(guess_hbm, agg_hbm, send_hbm, recv_hbm, valve_hbm, odd_ref, even_ref, notes_ref,
               guess_ref, agg_ref, send_ref, recv_ref, valve_ref, sems):
    pairs = (
        (send_hbm, send_ref), (guess_hbm, guess_ref), (agg_hbm, agg_ref), (recv_hbm, recv_ref),
        (valve_hbm, valve_ref),
    )
    for copy in copy_all(pairs, sems):
        copy.wait()
    for side, ref in enumerate((odd_ref, even_ref)):
        ref[...] = pick(guess_ref[...], row_of(send_ref, parity(side)))
    notes_ref[...] = jnp.concatenate(
        [send_ref[...], recv_ref[...], agg_ref[...], valve_ref[...], jnp.zeros((2, LANES), jnp.int32)],
        axis=0,
    )


def wide(row):
    return jnp.concatenate([row, jnp.zeros((1, LANES - row.shape[1]), row.dtype)], axis=1)


def pack_constants(ref, coff_ref, prolong, agg, cdiag, places):
    cpd, width = coff_ref.shape
    for at in range(0, width, LANES):
        start = at // LANES * cpd
        ref[start : start + cpd, :] = coff_ref[:, at : at + LANES]
    base = cpd * (width // LANES)
    high, low = pieces(pick(prolong, places))
    size = high.shape[0]
    ref[base : base + size, :] = high
    ref[base + size : base + 2 * size, :] = low
    listed = pick(jnp.broadcast_to(agg.astype(f32), (8, LANES)), places)[0:1]
    one = cdiag.astype(bf16).astype(f32)
    two = (cdiag - one).astype(bf16).astype(f32)
    rows = [listed, one, two, cdiag - one - two, jnp.zeros((12, LANES), f32)]
    ref[base + 2 * size : base + 2 * size + 16, :] = jnp.concatenate(rows, axis=0).astype(bf16)


def prepare(live_hbm, guess_hbm, rhs_hbm, blocks_hbm, coff_hbm, prolong_hbm, cdiag_hbm, notes_ref,
            local_ref, arrive_ref, gather_ref, odd_ref, even_ref,
            live_ref, guess_ref, rhs_ref, blocks_ref, coff_ref, prolong_ref, cdiag_ref, sems):
    size = guess_ref.shape[0]
    chunk = size // 4
    pairs = [(coff_hbm, coff_ref), (prolong_hbm, prolong_ref), (cdiag_hbm, cdiag_ref),
             (live_hbm, live_ref), (guess_hbm, guess_ref)]
    for at in range(0, size, chunk):
        pairs.append((blocks_hbm.at[at : at + chunk], blocks_ref.at[at : at + chunk]))
    copies = copy_all(pairs + [(rhs_hbm, rhs_ref)], sems)
    for copy in copies[:4]:
        copy.wait()
    cdiag = wide(cdiag_ref[...])
    for side, ref in enumerate((odd_ref, even_ref)):
        places = row_of(notes_ref.at[SEND], parity(side))
        pack_constants(ref, coff_ref, prolong_ref[...], notes_ref[AGG], cdiag, places)
    count = arrive_ref.shape[1]
    slots = notes_ref.shape[1]
    coarse = lax.broadcasted_iota(jnp.int32, (LANES, count), 0)
    gather_ref[...] = jnp.where(notes_ref[AGG] == coarse, 1.0, 0.0).T.astype(bf16)
    place = lax.axis_index("sub")
    row = lax.broadcasted_iota(jnp.int32, (count, slots), 0)
    slot = lax.broadcasted_iota(jnp.int32, (count, slots), 1)
    for side in (0, 1):
        other = place + 1 - 2 * parity(side)
        there = (other >= 0) & (other < lax.axis_size("sub"))
        which = 1 - parity(side)
        live = jnp.where(there, live_ref[0, which], 0)
        hit = (row_of(notes_ref.at[RECV], which) == row) & (slot < live)
        arrive_ref[side * slots : (side + 1) * slots, :] = jnp.where(hit, 1.0, 0.0).T.astype(bf16)
    copies[4].wait()
    guess = guess_ref[...]
    penalty = penalty_gain * notes_ref[VALVE].astype(f32)
    for at in range(0, size, 8):
        if at % chunk == 0:
            copies[5 + at // chunk].wait()
        part = slice(at, at + 8)
        local_ref[part, :] = block_rows(blocks_ref[part], guess) + penalty * guess[part]
    copies[-1].wait()
    local_ref[...] = rhs_ref[...] - local_ref[...]


def residual(local_ref, odd_near_ref, even_near_ref, arrive_ref, gather_ref, prolong_ref,
             jscale_ref, notes_ref, odd_pack_ref, even_pack_ref, cpd, first_ref, out_ref, odd_ref,
             even_ref):
    near = [odd_near_ref[...], even_near_ref[...]]
    first = local_ref[...] + coupling * received(near, arrive_ref)
    first_ref[...] = first
    weighted = jnp.sum(prolong_ref[...] * first, axis=0, keepdims=True)
    to_all(out_ref, restricted(weighted, gather_ref), cpd, [total(first * first)])
    scaled = jscale_ref[...] * first
    size = first.shape[0]
    tail = odd_ref.shape[0] - 2 * size
    for side, ref in enumerate((odd_ref, even_ref)):
        high, low = pieces(pick(scaled, row_of(notes_ref.at[SEND], parity(side))))
        ref[tail : tail + size, :] = high
        ref[tail + size :, :] = low


def unpack(own_ref, even_ref, odd_ref, cpd, matrix_ref, odd_weights_ref, even_weights_ref,
           odd_first_ref, even_first_ref, info_ref):
    width = matrix_ref.shape[1]
    size = odd_first_ref.shape[0]
    base = cpd * (width // LANES)
    rows = []
    for slot, ref in enumerate((own_ref, odd_ref, even_ref)):
        for at in range(0, width, LANES):
            start = at // LANES * cpd
            matrix_ref[slot * SLOT : slot * SLOT + cpd, at : at + LANES] = ref[start : start + cpd, :]
        matrix_ref[slot * SLOT + cpd : (slot + 1) * SLOT, :] = jnp.zeros((SLOT - cpd, width), bf16)
        rows.append(ref[base + 2 * size : base + 2 * size + 16, :].astype(f32))
    for ref, weights_ref, near_ref in (
        (odd_ref, odd_weights_ref, odd_first_ref), (even_ref, even_weights_ref, even_first_ref)
    ):
        for start, to_ref in ((base, weights_ref), (base + 2 * size + 16, near_ref)):
            high, low = ref[start : start + size, :], ref[start + size : start + 2 * size, :]
            to_ref[...] = high.astype(f32) + low.astype(f32)
    infos = [row[1:2] + row[2:3] + row[3:4] for row in rows] + [row[0:1] for row in rows[1:]]
    info_ref[...] = jnp.concatenate(infos + [jnp.zeros((3, LANES), f32)], axis=0)


def look_ahead(image_ref, first_ref, jscale_ref, prolong_ref, blocks_ref, notes_ref,
               lead_two_ref, lead_ref, pull_ref):
    valve, jscale = notes_ref[VALVE], jscale_ref[...]
    lead_two_ref[...] = local_product(blocks_ref, valve, jscale * image_ref[...])
    lead_ref[...] = local_product(blocks_ref, valve, jscale * first_ref[...])
    pull_ref[...] = local_product(blocks_ref, valve, prolong_ref[...])


def solve_coarse(parts, matrix_ref, near_rows, cdiags, cpd):
    group = parts[0].shape[0]
    shape = (group, LANES)
    row = lax.broadcasted_iota(jnp.int32, shape, 0)
    lane = lax.broadcasted_iota(jnp.int32, shape, 1)
    masks = [(at + lane) // cpd == row for at in range(0, group * cpd, LANES)]
    source = lax.rem(lane - cpd * row + cpd * group, LANES)
    tiles = []
    for part in parts:
        shifted = jnp.take_along_axis(part, source, axis=1)
        tiles.extend(jnp.where(mask, shifted, 0.0) for mask in masks)
    product = lax.dot_general(
        jnp.concatenate(tiles, axis=1).astype(bf16), matrix_ref[...], (((1,), (1,)), ((), ())),
        preferred_element_type=f32,
    )
    product = jnp.sum(product, axis=0, keepdims=True)
    low = product[:, :LANES]
    high = jnp.concatenate([product[:, LANES:], jnp.zeros((1, LANES - SLOT), f32)], axis=1)
    turned = pltpu.roll(jnp.broadcast_to(low, (8, LANES)), LANES - SLOT, 1)[0:1]
    shares = (low, turned, high)
    return [cdiag * row + share for cdiag, row, share in zip(cdiags, near_rows, shares)]


def parts_of(ref, cpd):
    group = math.lcm(cpd, LANES) // cpd
    rows = flat(ref)
    return [rows[at : at + group, :] for at in range(0, rows.shape[0], group)]


def rows_near(parts, grp_size):
    group = parts[0].shape[0]
    count = group * len(parts)
    me = lax.axis_index("sub") * grp_size + lax.axis_index("grp")
    place = lax.broadcasted_iota(jnp.int32, parts[0].shape, 0)
    rows = []
    for shift in [0] + [grp_size * (1 - 2 * parity(side)) for side in (0, 1)]:
        wanted = lax.rem(me + shift + count, count)
        found = jnp.where(place == wanted, parts[0], 0.0)
        for at, part in enumerate(parts[1:], 1):
            found = jnp.where(place + at * group == wanted, part, found)
        rows.append(jnp.sum(found, axis=0, keepdims=True))
    return rows


def spread_of(solution, agg):
    wide = jnp.broadcast_to(solution, (8, LANES))
    return jnp.take_along_axis(wide, jnp.broadcast_to(agg, (8, LANES)), axis=1)[0:1]


def near_spread(weights_ref, info_ref, side, solution):
    agg = info_ref[3 + side : 4 + side, :].astype(jnp.int32)
    return weights_ref[...] * spread_of(solution, agg)


def first_step(got_ref, own_pack_ref, even_pack_ref, odd_pack_ref, first_ref, jscale_ref,
               prolong_ref, blocks_ref, notes_ref, arrive_ref, gather_ref, grp_size, cpd,
               basis_ref, direction_ref, image_ref, out_ref, odd_ref, even_ref, matrix_ref,
               odd_weights_ref, even_weights_ref, odd_near_ref, even_near_ref, info_ref):
    unpack(own_pack_ref, even_pack_ref, odd_pack_ref, cpd, matrix_ref, odd_weights_ref,
           even_weights_ref, odd_near_ref, even_near_ref, info_ref)
    inverse = 1.0 / jnp.sqrt(summed(got_ref, cpd, 1)[0])
    parts = [part * inverse for part in parts_of(got_ref, cpd)]
    cdiags = [info_ref[at : at + 1, :] for at in range(3)]
    solved = solve_coarse(parts, matrix_ref, rows_near(parts, grp_size), cdiags, cpd)
    basis = first_ref[...] * inverse
    basis_ref[...] = basis
    spread = spread_of(solved[0], notes_ref[AGG])
    jscale, prolong = jscale_ref[...], prolong_ref[...]
    direction = jscale * basis + prolong * spread
    direction_ref[...] = direction
    near = [
        odd_near_ref[...] * inverse + near_spread(odd_weights_ref, info_ref, 0, solved[1]),
        even_near_ref[...] * inverse + near_spread(even_weights_ref, info_ref, 1, solved[2]),
    ]
    image = local_product(blocks_ref, notes_ref[VALVE], direction)
    image = image - coupling * received(near, arrive_ref)
    image_ref[...] = image
    weighted = jnp.sum(prolong * image, axis=0, keepdims=True)
    dots = [total(basis * image), total(image * image)]
    to_all(out_ref, restricted(weighted, gather_ref), cpd, dots)
    scaled = jscale * image
    for side, ref in enumerate((odd_ref, even_ref)):
        ref[...] = pick(scaled, row_of(notes_ref.at[SEND], parity(side)))


def second_step(got_ref, first_got_ref, odd_near_ref, even_near_ref, odd_first_ref, even_first_ref,
                odd_weights_ref, even_weights_ref, matrix_ref, info_ref, basis_ref, image_ref,
                lead_ref, lead_two_ref, pull_ref, jscale_ref, prolong_ref, notes_ref, arrive_ref,
                grp_size, cpd, basis_two_ref, direction_ref, image_two_ref, scalars_ref, out_ref):
    beta = jnp.sqrt(summed(first_got_ref, cpd, 1)[0])
    along, energy = summed(got_ref, cpd, 2)
    height = jnp.sqrt(jnp.maximum(energy - along * along, 0.01 * energy))
    inverse = 1.0 / height
    slope = along / beta

    def mixed(new, old):
        return (new - slope * old) * inverse

    parts = [
        mixed(new, old) for new, old in zip(parts_of(got_ref, cpd), parts_of(first_got_ref, cpd))
    ]
    cdiags = [info_ref[at : at + 1, :] for at in range(3)]
    solved = solve_coarse(parts, matrix_ref, rows_near(parts, grp_size), cdiags, cpd)
    basis = (image_ref[...] - along * basis_ref[...]) * inverse
    basis_two_ref[...] = basis
    spread = spread_of(solved[0], notes_ref[AGG])
    direction_ref[...] = jscale_ref[...] * basis + prolong_ref[...] * spread
    near = [
        mixed(odd_near_ref[...], odd_first_ref[...])
        + near_spread(odd_weights_ref, info_ref, 0, solved[1]),
        mixed(even_near_ref[...], even_first_ref[...])
        + near_spread(even_weights_ref, info_ref, 1, solved[2]),
    ]
    image = mixed(lead_two_ref[...], lead_ref[...]) + pull_ref[...] * spread
    image = image - coupling * received(near, arrive_ref)
    image_two_ref[...] = image
    scalars_ref[...] = jnp.concatenate([beta, along, height, jnp.zeros((5, LANES), f32)], axis=0)
    dots = [total(basis_ref[...] * image), total(basis * image), total(image * image)]
    to_all(out_ref, jnp.zeros((1, LANES), f32), 0, dots)


def finish(got_ref, scalars_ref, guess_ref, basis_ref, basis_two_ref, direction_ref,
           direction_two_ref, image_ref, solution_ref, next_ref):
    beta, h11, h21 = scalars_ref[0:1, :], scalars_ref[1:2, :], scalars_ref[2:3, :]
    h12, h22, energy = summed(got_ref, 0, 3)
    h32 = jnp.sqrt(jnp.maximum(energy - (h12 * h12 + h22 * h22), 0.01 * energy))
    g00 = h11 * h11 + h21 * h21
    g01 = h11 * h12 + h21 * h22
    g11 = h12 * h12 + h22 * h22 + h32 * h32
    t0, t1 = beta * h11, beta * h12
    factor = g01 / g00
    c1 = (t1 - factor * t0) / (g11 - factor * g01)
    c0 = (t0 - g01 * c1) / g00
    solution_ref[...] = guess_ref[...] + c0 * direction_ref[...] + c1 * direction_two_ref[...]
    next_ref[...] = (image_ref[...] - h12 * basis_ref[...] - h22 * basis_two_ref[...]) * (1.0 / h32)


def on_device(rhs, guess, blocks, valve, jscale, prolong, agg_map, cdiag, coff, send_rows,
              recv_rows, live_counts):
    rhs, guess, blocks, jscale, prolong = rhs[0, 0], guess[0, 0], blocks[0, 0], jscale[0, 0], prolong[0, 0]
    valve, agg, live = valve[0], agg_map[0], live_counts[0]
    send, recv = send_rows[0, 0], recv_rows[0, 0]
    size, count = guess.shape
    slots = send.shape[1]
    cpd = cdiag.shape[0]
    subs, grps = lax.axis_size("sub"), lax.axis_size("grp")
    devices = subs * grps
    cdiag = cdiag[None, :]
    moves = [pairing(subs, grps, side) for side in (0, 1)]

    def exchange(odd, even):
        return lax.ppermute(odd, AXES, moves[0]), lax.ppermute(even, AXES, moves[1])

    def everyone(rows):
        return lax.all_to_all(rows, AXES, 0, 0, tiled=True)

    field = ((size, count), f32)
    near = ((size, slots), f32)
    rows_out = ((devices, LANES), f32)
    small = ((8, LANES), f32)
    items = (guess, agg, send, recv, valve)
    odd, even, notes = call(
        first_send, [near, near, ((8, LANES), jnp.int32)], *items, hbm=range(5), limit=16,
        scratch=[pltpu.VMEM(item.shape, item.dtype) for item in items]
        + [pltpu.SemaphoreType.DMA((5,))],
    )
    odd_guess, even_guess = exchange(odd, even)
    packed = ((cpd * (coff.shape[1] // LANES) + 4 * size + 16, LANES), bf16)
    items = (guess, rhs, blocks, coff, prolong, cdiag)
    local, arrive, gather, odd, even = call(
        prepare,
        [field, ((2 * slots, count), bf16), ((count, LANES), bf16), packed, packed],
        live, *items, notes, hbm=range(7),
        scratch=[pltpu.SMEM(live.shape, live.dtype)]
        + [pltpu.VMEM(item.shape, item.dtype) for item in items]
        + [pltpu.SemaphoreType.DMA((10,))],
    )
    first, rows, odd, even = call(
        lambda *refs: residual(*refs[:10], cpd, *refs[10:]), [field, rows_out, packed, packed],
        local, odd_guess, even_guess, arrive, gather, prolong, jscale, notes, odd, even,
        aliases={8: 2, 9: 3},
    )
    even_pack = lax.ppermute(even, AXES, moves[1])
    odd_pack = lax.ppermute(odd, AXES, moves[0])
    own_pack = odd
    first_got = everyone(rows)
    (basis, direction, image, rows, odd, even, matrix, odd_weights, even_weights, odd_first,
     even_first, info) = call(
        lambda *refs: first_step(*refs[:11], grps, cpd, *refs[11:]),
        [field, field, field, ((devices, 2, LANES), f32), near, near,
         ((3 * SLOT, coff.shape[1]), bf16)] + [near] * 4 + [small],
        first_got, own_pack, even_pack, odd_pack, first, jscale, prolong, blocks, notes, arrive,
        gather,
    )
    odd_near, even_near = exchange(odd, even)
    got = everyone(rows)
    lead_two, lead, pull = call(
        look_ahead, [field, field, field], image, first, jscale, prolong, blocks, notes
    )
    basis_two, direction_two, image_two, scalars, rows = call(
        lambda *refs: second_step(*refs[:19], grps, cpd, *refs[19:]),
        [field, field, field, ((8, LANES), f32), rows_out],
        got, first_got, odd_near, even_near, odd_first, even_first, odd_weights, even_weights, matrix,
        info, basis, image, lead, lead_two, pull, jscale, prolong, notes, arrive,
    )
    got = everyone(rows)
    solution, next_basis = call(
        finish, [field, field],
        got, scalars, guess, basis, basis_two, direction, direction_two, image_two, final=True,
    )
    return solution[None, None], next_basis[None, None]


def solution(mesh):
    return jax.shard_map(
        on_device,
        mesh=mesh,
        in_specs=(
            P("sub", "grp", None, None),
            P("sub", "grp", None, None),
            P("sub", "grp", None, None, None),
            P("sub", "grp", None),
            P("sub", "grp", None, None),
            P("sub", "grp", None, None),
            P("sub", "grp", None),
            P(("sub", "grp")),
            P(("sub", "grp"), None),
            P("sub", "grp", None, None),
            P("sub", "grp", None, None),
            P("sub", "grp", None),
        ),
        out_specs=(P("sub", "grp", None, None), P("sub", "grp", None, None)),
        check_vma=False,
    )
```

```python
import math

import jax
import jax.numpy as jnp
from jax import lax
from jax.experimental import pallas as pl
from jax.experimental.pallas import tpu as pltpu
from jax.sharding import PartitionSpec as P

penalty_gain = 3.0
coupling = 0.5

LANES = 128
SLOT = 64
AXES = ("sub", "grp")
f32 = jnp.float32
bf16 = jnp.bfloat16

SEND, RECV, AGG, VALVE = slice(0, 2), slice(2, 4), slice(4, 5), slice(5, 6)


def call(body, outs, *args, smem=(), hbm=(), scratch=(), limit=32, final=False, aliases=None):
    def spec(at):
        if at in hbm:
            return pl.BlockSpec(memory_space=pltpu.HBM)
        return pl.BlockSpec(memory_space=pltpu.SMEM if at in smem else pltpu.VMEM)

    args = [
        pltpu.with_memory_space_constraint(arg, pltpu.HBM) if at in hbm else arg
        for at, arg in enumerate(args)
    ]
    return pl.pallas_call(
        body,
        out_shape=[
            jax.ShapeDtypeStruct(shape, kind) if final else pltpu.VMEM(shape, kind)
            for shape, kind in outs
        ],
        in_specs=[spec(at) for at in range(len(args))],
        out_specs=[pl.BlockSpec(memory_space=pltpu.VMEM)] * len(outs),
        scratch_shapes=list(scratch),
        input_output_aliases=aliases or {},
        compiler_params=pltpu.CompilerParams(vmem_limit_bytes=limit * 1024 * 1024),
    )(*args)


def partner(place, side):
    return place - 1 + 2 * ((place + side) % 2)


def pairing(subs, grps, side):
    moves = []
    for place in range(subs):
        other = partner(place, side)
        for group in range(grps):
            if 0 <= other < subs:
                target = other * grps + group
            else:
                target = place * grps + (group ^ 1 if group ^ 1 < grps else group)
            moves.append((place * grps + group, target))
    return moves


def row_of(ref, flipped):
    return jnp.where(flipped == 0, ref[0:1, :], ref[1:2, :])


def parity(side):
    return (lax.axis_index("sub") + side + 1) % 2


def pick(field, places):
    return jnp.take_along_axis(field, jnp.broadcast_to(places, field.shape), axis=1)


def pieces(field):
    high = field.astype(bf16)
    return high, (field - high.astype(f32)).astype(bf16)


def block_rows(blocks, field):
    return jnp.sum(blocks.astype(f32) * field[None], axis=1)


def local_product(blocks_ref, valve, field):
    rows = [block_rows(blocks_ref[at : at + 8], field) for at in range(0, blocks_ref.shape[0], 8)]
    return jnp.concatenate(rows, axis=0) + penalty_gain * valve.astype(f32) * field


def received(near, arrive_ref):
    high, low = pieces(jnp.concatenate(near, axis=1))
    both = jnp.dot(
        jnp.concatenate([high, low], axis=0), arrive_ref[...], preferred_element_type=f32
    )
    count = near[0].shape[0]
    return both[:count] + both[count:]


def restricted(weighted, gather_ref):
    high = weighted.astype(bf16).astype(f32)
    rest = weighted - high
    middle = rest.astype(bf16).astype(f32)
    last = rest - middle
    row = lax.broadcasted_iota(jnp.int32, (8, weighted.shape[1]), 0)
    stack = jnp.where(row == 0, high, jnp.where(row == 1, middle, jnp.where(row == 2, last, 0.0)))
    sums = jnp.dot(stack.astype(bf16), gather_ref[...], preferred_element_type=f32)
    return jnp.sum(sums, axis=0, keepdims=True)


def total(field):
    return jnp.sum(jnp.sum(field, axis=0, keepdims=True), axis=1, keepdims=True)


def to_all(ref, row, first_lane, totals):
    lane = lax.broadcasted_iota(jnp.int32, (1, LANES), 1)
    for at, value in enumerate(totals):
        row = jnp.where(lane == first_lane + at, value, row)
    ref[...] = jnp.broadcast_to(row, ref.shape)


def flat(ref):
    return ref[...] if len(ref.shape) == 2 else ref[:, 0, :]


def summed(ref, first_lane, count):
    rows = jnp.broadcast_to(jnp.sum(flat(ref), axis=0, keepdims=True), (8, LANES))
    return [
        jnp.take_along_axis(rows, jnp.full((8, LANES), first_lane + at, jnp.int32), axis=1)[0:1]
        for at in range(count)
    ]


def copy_all(pairs, sems):
    copies = [pltpu.make_async_copy(*pair, sems.at[at]) for at, pair in enumerate(pairs)]
    for copy in copies:
        copy.start()
    return copies


def first_send(guess_hbm, agg_hbm, send_hbm, recv_hbm, valve_hbm, odd_ref, even_ref, notes_ref,
               guess_ref, agg_ref, send_ref, recv_ref, valve_ref, sems):
    pairs = (
        (send_hbm, send_ref), (guess_hbm, guess_ref), (agg_hbm, agg_ref), (recv_hbm, recv_ref),
        (valve_hbm, valve_ref),
    )
    for copy in copy_all(pairs, sems):
        copy.wait()
    for side, ref in enumerate((odd_ref, even_ref)):
        ref[...] = pick(guess_ref[...], row_of(send_ref, parity(side)))
    notes_ref[...] = jnp.concatenate(
        [send_ref[...], recv_ref[...], agg_ref[...], valve_ref[...], jnp.zeros((2, LANES), jnp.int32)],
        axis=0,
    )


def wide(row):
    return jnp.concatenate([row, jnp.zeros((1, LANES - row.shape[1]), row.dtype)], axis=1)


def pack_constants(ref, coff_ref, prolong, agg, cdiag, places):
    cpd, width = coff_ref.shape
    for at in range(0, width, LANES):
        start = at // LANES * cpd
        ref[start : start + cpd, :] = coff_ref[:, at : at + LANES]
    base = cpd * (width // LANES)
    high, low = pieces(pick(prolong, places))
    size = high.shape[0]
    ref[base : base + size, :] = high
    ref[base + size : base + 2 * size, :] = low
    listed = pick(jnp.broadcast_to(agg.astype(f32), (8, LANES)), places)[0:1]
    one = cdiag.astype(bf16).astype(f32)
    two = (cdiag - one).astype(bf16).astype(f32)
    rows = [listed, one, two, cdiag - one - two, jnp.zeros((12, LANES), f32)]
    ref[base + 2 * size : base + 2 * size + 16, :] = jnp.concatenate(rows, axis=0).astype(bf16)


def prepare(live_hbm, guess_hbm, rhs_hbm, blocks_hbm, coff_hbm, prolong_hbm, cdiag_hbm, notes_ref,
            local_ref, arrive_ref, gather_ref, odd_ref, even_ref,
            live_ref, guess_ref, rhs_ref, blocks_ref, coff_ref, prolong_ref, cdiag_ref, sems):
    size = guess_ref.shape[0]
    chunk = size // 4
    pairs = [(coff_hbm, coff_ref), (prolong_hbm, prolong_ref), (cdiag_hbm, cdiag_ref),
             (live_hbm, live_ref), (guess_hbm, guess_ref)]
    for at in range(0, size, chunk):
        pairs.append((blocks_hbm.at[at : at + chunk], blocks_ref.at[at : at + chunk]))
    copies = copy_all(pairs + [(rhs_hbm, rhs_ref)], sems)
    for copy in copies[:4]:
        copy.wait()
    cdiag = wide(cdiag_ref[...])
    for side, ref in enumerate((odd_ref, even_ref)):
        places = row_of(notes_ref.at[SEND], parity(side))
        pack_constants(ref, coff_ref, prolong_ref[...], notes_ref[AGG], cdiag, places)
    count = arrive_ref.shape[1]
    slots = notes_ref.shape[1]
    coarse = lax.broadcasted_iota(jnp.int32, (LANES, count), 0)
    gather_ref[...] = jnp.where(notes_ref[AGG] == coarse, 1.0, 0.0).T.astype(bf16)
    place = lax.axis_index("sub")
    row = lax.broadcasted_iota(jnp.int32, (count, slots), 0)
    slot = lax.broadcasted_iota(jnp.int32, (count, slots), 1)
    for side in (0, 1):
        other = place + 1 - 2 * parity(side)
        there = (other >= 0) & (other < lax.axis_size("sub"))
        which = 1 - parity(side)
        live = jnp.where(there, live_ref[0, which], 0)
        hit = (row_of(notes_ref.at[RECV], which) == row) & (slot < live)
        arrive_ref[side * slots : (side + 1) * slots, :] = jnp.where(hit, 1.0, 0.0).T.astype(bf16)
    copies[4].wait()
    guess = guess_ref[...]
    penalty = penalty_gain * notes_ref[VALVE].astype(f32)
    for at in range(0, size, 8):
        if at % chunk == 0:
            copies[5 + at // chunk].wait()
        part = slice(at, at + 8)
        local_ref[part, :] = block_rows(blocks_ref[part], guess) + penalty * guess[part]
    copies[-1].wait()
    local_ref[...] = rhs_ref[...] - local_ref[...]


def residual(local_ref, odd_near_ref, even_near_ref, arrive_ref, gather_ref, prolong_ref,
             jscale_ref, notes_ref, odd_pack_ref, even_pack_ref, cpd, first_ref, out_ref, odd_ref,
             even_ref):
    near = [odd_near_ref[...], even_near_ref[...]]
    first = local_ref[...] + coupling * received(near, arrive_ref)
    first_ref[...] = first
    weighted = jnp.sum(prolong_ref[...] * first, axis=0, keepdims=True)
    to_all(out_ref, restricted(weighted, gather_ref), cpd, [total(first * first)])
    scaled = jscale_ref[...] * first
    size = first.shape[0]
    tail = odd_ref.shape[0] - 2 * size
    for side, ref in enumerate((odd_ref, even_ref)):
        high, low = pieces(pick(scaled, row_of(notes_ref.at[SEND], parity(side))))
        ref[tail : tail + size, :] = high
        ref[tail + size :, :] = low


def unpack(own_ref, even_ref, odd_ref, cpd, matrix_ref, odd_weights_ref, even_weights_ref,
           odd_first_ref, even_first_ref, info_ref):
    width = matrix_ref.shape[1]
    size = odd_first_ref.shape[0]
    base = cpd * (width // LANES)
    rows = []
    for slot, ref in enumerate((own_ref, odd_ref, even_ref)):
        for at in range(0, width, LANES):
            start = at // LANES * cpd
            matrix_ref[slot * SLOT : slot * SLOT + cpd, at : at + LANES] = ref[start : start + cpd, :]
        matrix_ref[slot * SLOT + cpd : (slot + 1) * SLOT, :] = jnp.zeros((SLOT - cpd, width), bf16)
        rows.append(ref[base + 2 * size : base + 2 * size + 16, :].astype(f32))
    for ref, weights_ref, near_ref in (
        (odd_ref, odd_weights_ref, odd_first_ref), (even_ref, even_weights_ref, even_first_ref)
    ):
        for start, to_ref in ((base, weights_ref), (base + 2 * size + 16, near_ref)):
            high, low = ref[start : start + size, :], ref[start + size : start + 2 * size, :]
            to_ref[...] = high.astype(f32) + low.astype(f32)
    infos = [row[1:2] + row[2:3] + row[3:4] for row in rows] + [row[0:1] for row in rows[1:]]
    info_ref[...] = jnp.concatenate(infos + [jnp.zeros((3, LANES), f32)], axis=0)


def unpack(own_ref, even_ref, odd_ref, cpd, matrix_ref, odd_weights_ref, even_weights_ref,
           odd_first_ref, even_first_ref, info_ref):
    width = matrix_ref.shape[1]
    size = odd_first_ref.shape[0]
    base = cpd * (width // LANES)
    rows = []
    for slot, ref in enumerate((own_ref, odd_ref, even_ref)):
        for at in range(0, width, LANES):
            start = at // LANES * cpd
            matrix_ref[slot * SLOT : slot * SLOT + cpd, at : at + LANES] = ref[start : start + cpd, :]
        matrix_ref[slot * SLOT + cpd : (slot + 1) * SLOT, :] = jnp.zeros((SLOT - cpd, width), bf16)
        rows.append(ref[base + 2 * size : base + 2 * size + 16, :].astype(f32))
    for ref, weights_ref, near_ref in (
        (odd_ref, odd_weights_ref, odd_first_ref), (even_ref, even_weights_ref, even_first_ref)
    ):
        for start, to_ref in ((base, weights_ref), (base + 2 * size + 16, near_ref)):
            high, low = ref[start : start + size, :], ref[start + size : start + 2 * size, :]
            to_ref[...] = high.astype(f32) + low.astype(f32)
    infos = [row[1:2] + row[2:3] + row[3:4] for row in rows] + [row[0:1] for row in rows[1:]]
    info_ref[...] = jnp.concatenate(infos + [jnp.zeros((3, LANES), f32)], axis=0)


def look_ahead(image_ref, first_ref, jscale_ref, prolong_ref, blocks_ref, notes_ref,
               lead_two_ref, lead_ref, pull_ref):
    valve, jscale = notes_ref[VALVE], jscale_ref[...]
    lead_two_ref[...] = local_product(blocks_ref, valve, jscale * image_ref[...])
    lead_ref[...] = local_product(blocks_ref, valve, jscale * first_ref[...])
    pull_ref[...] = local_product(blocks_ref, valve, prolong_ref[...])


def solve_coarse(parts, matrix_ref, near_rows, cdiags, cpd):
    group = parts[0].shape[0]
    shape = (group, LANES)
    row = lax.broadcasted_iota(jnp.int32, shape, 0)
    lane = lax.broadcasted_iota(jnp.int32, shape, 1)
    masks = [(at + lane) // cpd == row for at in range(0, group * cpd, LANES)]
    source = lax.rem(lane - cpd * row + cpd * group, LANES)
    tiles = []
    for part in parts:
        shifted = jnp.take_along_axis(part, source, axis=1)
        tiles.extend(jnp.where(mask, shifted, 0.0) for mask in masks)
    product = lax.dot_general(
        jnp.concatenate(tiles, axis=1).astype(bf16), matrix_ref[...], (((1,), (1,)), ((), ())),
        preferred_element_type=f32,
    )
    product = jnp.sum(product, axis=0, keepdims=True)
    low = product[:, :LANES]
    high = jnp.concatenate([product[:, LANES:], jnp.zeros((1, LANES - SLOT), f32)], axis=1)
    turned = pltpu.roll(jnp.broadcast_to(low, (8, LANES)), LANES - SLOT, 1)[0:1]
    shares = (low, turned, high)
    return [cdiag * row + share for cdiag, row, share in zip(cdiags, near_rows, shares)]


def parts_of(ref, cpd):
    group = math.lcm(cpd, LANES) // cpd
    rows = flat(ref)
    return [rows[at : at + group, :] for at in range(0, rows.shape[0], group)]


def rows_near(parts, grp_size):
    group = parts[0].shape[0]
    count = group * len(parts)
    me = lax.axis_index("sub") * grp_size + lax.axis_index("grp")
    place = lax.broadcasted_iota(jnp.int32, parts[0].shape, 0)
    rows = []
    for shift in [0] + [grp_size * (1 - 2 * parity(side)) for side in (0, 1)]:
        wanted = lax.rem(me + shift + count, count)
        found = jnp.where(place == wanted, parts[0], 0.0)
        for at, part in enumerate(parts[1:], 1):
            found = jnp.where(place + at * group == wanted, part, found)
        rows.append(jnp.sum(found, axis=0, keepdims=True))
    return rows


def spread_of(solution, agg):
    wide = jnp.broadcast_to(solution, (8, LANES))
    return jnp.take_along_axis(wide, jnp.broadcast_to(agg, (8, LANES)), axis=1)[0:1]


def near_spread(weights_ref, info_ref, side, solution):
    agg = info_ref[3 + side : 4 + side, :].astype(jnp.int32)
    return weights_ref[...] * spread_of(solution, agg)


def first_step(got_ref, own_pack_ref, even_pack_ref, odd_pack_ref, first_ref, jscale_ref,
               prolong_ref, blocks_ref, notes_ref, arrive_ref, gather_ref, grp_size, cpd,
               basis_ref, direction_ref, image_ref, out_ref, odd_ref, even_ref, matrix_ref,
               odd_weights_ref, even_weights_ref, odd_near_ref, even_near_ref, info_ref):
    unpack(own_pack_ref, even_pack_ref, odd_pack_ref, cpd, matrix_ref, odd_weights_ref,
           even_weights_ref, odd_near_ref, even_near_ref, info_ref)
    inverse = 1.0 / jnp.sqrt(summed(got_ref, cpd, 1)[0])
    parts = [part * inverse for part in parts_of(got_ref, cpd)]
    cdiags = [info_ref[at : at + 1, :] for at in range(3)]
    solved = solve_coarse(parts, matrix_ref, rows_near(parts, grp_size), cdiags, cpd)
    basis = first_ref[...] * inverse
    basis_ref[...] = basis
    spread = spread_of(solved[0], notes_ref[AGG])
    jscale, prolong = jscale_ref[...], prolong_ref[...]
    direction = jscale * basis + prolong * spread
    direction_ref[...] = direction
    near = [
        odd_near_ref[...] * inverse + near_spread(odd_weights_ref, info_ref, 0, solved[1]),
        even_near_ref[...] * inverse + near_spread(even_weights_ref, info_ref, 1, solved[2]),
    ]
    image = local_product(blocks_ref, notes_ref[VALVE], direction)
    image = image - coupling * received(near, arrive_ref)
    image_ref[...] = image
    weighted = jnp.sum(prolong * image, axis=0, keepdims=True)
    dots = [total(basis * image), total(image * image)]
    to_all(out_ref, restricted(weighted, gather_ref), cpd, dots)
    scaled = jscale * image
    for side, ref in enumerate((odd_ref, even_ref)):
        ref[...] = pick(scaled, row_of(notes_ref.at[SEND], parity(side)))


def second_step(got_ref, first_got_ref, even_near_ref, odd_near_ref, odd_first_ref, even_first_ref,
                odd_weights_ref, even_weights_ref, matrix_ref, info_ref, basis_ref, image_ref,
                jscale_ref, prolong_ref, blocks_ref, notes_ref, arrive_ref,
                grp_size, cpd, basis_two_ref, direction_ref, image_two_ref, scalars_ref, out_ref):
    beta = jnp.sqrt(summed(first_got_ref, cpd, 1)[0])
    along, energy = summed(got_ref, cpd, 2)
    height = jnp.sqrt(jnp.maximum(energy - along * along, 0.01 * energy))
    inverse = 1.0 / height
    slope = along / beta

    def mixed(new, old):
        return (new - slope * old) * inverse

    parts = [
        mixed(new, old) for new, old in zip(parts_of(got_ref, cpd), parts_of(first_got_ref, cpd))
    ]
    cdiags = [info_ref[at : at + 1, :] for at in range(3)]
    solved = solve_coarse(parts, matrix_ref, rows_near(parts, grp_size), cdiags, cpd)
    basis = (image_ref[...] - along * basis_ref[...]) * inverse
    basis_two_ref[...] = basis
    spread = spread_of(solved[0], notes_ref[AGG])
    direction = jscale_ref[...] * basis + prolong_ref[...] * spread
    direction_ref[...] = direction
    near = [
        mixed(odd_near_ref[...], odd_first_ref[...])
        + near_spread(odd_weights_ref, info_ref, 0, solved[1]),
        mixed(even_near_ref[...], even_first_ref[...])
        + near_spread(even_weights_ref, info_ref, 1, solved[2]),
    ]
    image = local_product(blocks_ref, notes_ref[VALVE], direction)
    image = image - coupling * received(near, arrive_ref)
    image_two_ref[...] = image
    scalars_ref[...] = jnp.concatenate([beta, along, height, jnp.zeros((5, LANES), f32)], axis=0)
    dots = [total(basis_ref[...] * image), total(basis * image), total(image * image)]
    to_all(out_ref, jnp.zeros((1, LANES), f32), 0, dots)


def finish(got_ref, scalars_ref, guess_ref, basis_ref, basis_two_ref, direction_ref,
           direction_two_ref, image_ref, solution_ref, next_ref):
    beta, h11, h21 = scalars_ref[0:1, :], scalars_ref[1:2, :], scalars_ref[2:3, :]
    h12, h22, energy = summed(got_ref, 0, 3)
    h32 = jnp.sqrt(jnp.maximum(energy - (h12 * h12 + h22 * h22), 0.01 * energy))
    g00 = h11 * h11 + h21 * h21
    g01 = h11 * h12 + h21 * h22
    g11 = h12 * h12 + h22 * h22 + h32 * h32
    t0, t1 = beta * h11, beta * h12
    factor = g01 / g00
    c1 = (t1 - factor * t0) / (g11 - factor * g01)
    c0 = (t0 - g01 * c1) / g00
    solution_ref[...] = guess_ref[...] + c0 * direction_ref[...] + c1 * direction_two_ref[...]
    next_ref[...] = (image_ref[...] - h12 * basis_ref[...] - h22 * basis_two_ref[...]) * (1.0 / h32)


def on_device(rhs, guess, blocks, valve, jscale, prolong, agg_map, cdiag, coff, send_rows,
              recv_rows, live_counts):
    rhs, guess, blocks, jscale, prolong = rhs[0, 0], guess[0, 0], blocks[0, 0], jscale[0, 0], prolong[0, 0]
    valve, agg, live = valve[0], agg_map[0], live_counts[0]
    send, recv = send_rows[0, 0], recv_rows[0, 0]
    size, count = guess.shape
    slots = send.shape[1]
    cpd = cdiag.shape[0]
    subs, grps = lax.axis_size("sub"), lax.axis_size("grp")
    devices = subs * grps
    cdiag = cdiag[None, :]
    moves = [pairing(subs, grps, side) for side in (0, 1)]

    def exchange(odd, even):
        return lax.ppermute(odd, AXES, moves[0]), lax.ppermute(even, AXES, moves[1])

    def everyone(rows):
        return lax.all_to_all(rows, AXES, 0, 0, tiled=True)

    field = ((size, count), f32)
    near = ((size, slots), f32)
    rows_out = ((devices, LANES), f32)
    small = ((8, LANES), f32)
    items = (guess, agg, send, recv, valve)
    odd, even, notes = call(
        first_send, [near, near, ((8, LANES), jnp.int32)], *items, hbm=range(5), limit=16,
        scratch=[pltpu.VMEM(item.shape, item.dtype) for item in items]
        + [pltpu.SemaphoreType.DMA((5,))],
    )
    odd_guess, even_guess = exchange(odd, even)
    packed = ((cpd * (coff.shape[1] // LANES) + 4 * size + 16, LANES), bf16)
    items = (guess, rhs, blocks, coff, prolong, cdiag)
    local, arrive, gather, odd, even = call(
        prepare,
        [field, ((2 * slots, count), bf16), ((count, LANES), bf16), packed, packed],
        live, *items, notes, hbm=range(7),
        scratch=[pltpu.SMEM(live.shape, live.dtype)]
        + [pltpu.VMEM(item.shape, item.dtype) for item in items]
        + [pltpu.SemaphoreType.DMA((10,))],
    )
    first, rows, odd, even = call(
        lambda *refs: residual(*refs[:10], cpd, *refs[10:]), [field, rows_out, packed, packed],
        local, odd_guess, even_guess, arrive, gather, prolong, jscale, notes, odd, even,
        aliases={8: 2, 9: 3},
    )
    even_pack = lax.ppermute(even, AXES, moves[1])
    odd_pack = lax.ppermute(odd, AXES, moves[0])
    own_pack = odd
    first_got = everyone(rows)
    (basis, direction, image, rows, odd, even, matrix, odd_weights, even_weights, odd_first,
     even_first, info) = call(
        lambda *refs: first_step(*refs[:11], grps, cpd, *refs[11:]),
        [field, field, field, rows_out, near, near,
         ((3 * SLOT, coff.shape[1]), bf16)] + [near] * 4 + [small],
        first_got, own_pack, even_pack, odd_pack, first, jscale, prolong, blocks, notes, arrive,
        gather,
    )
    odd_near, even_near = exchange(odd, even)
    got = everyone(rows)
    basis_two, direction_two, image_two, scalars, rows = call(
        lambda *refs: second_step(*refs[:17], grps, cpd, *refs[17:]),
        [field, field, field, ((8, LANES), f32), rows_out],
        got, first_got, even_near, odd_near, odd_first, even_first, odd_weights, even_weights, matrix,
        info, basis, image, jscale, prolong, blocks, notes, arrive,
    )
    got = everyone(rows)
    solution, next_basis = call(
        finish, [field, field],
        got, scalars, guess, basis, basis_two, direction, direction_two, image_two, final=True,
    )
    return solution[None, None], next_basis[None, None]


def solution(mesh):
    return jax.shard_map(
        on_device,
        mesh=mesh,
        in_specs=(
            P("sub", "grp", None, None),
            P("sub", "grp", None, None),
            P("sub", "grp", None, None, None),
            P("sub", "grp", None),
            P("sub", "grp", None, None),
            P("sub", "grp", None, None),
            P("sub", "grp", None),
            P(("sub", "grp")),
            P(("sub", "grp"), None),
            P("sub", "grp", None, None),
            P("sub", "grp", None, None),
            P("sub", "grp", None),
        ),
        out_specs=(P("sub", "grp", None, None), P("sub", "grp", None, None)),
        check_vma=False,
    )
```

```python
import math

import jax
import jax.numpy as jnp
from jax import lax
from jax.experimental import pallas as pl
from jax.experimental.pallas import tpu as pltpu
from jax.sharding import PartitionSpec as P

penalty_gain = 3.0
coupling = 0.5

LANES = 128
SLOT = 64
AXES = ("sub", "grp")
f32 = jnp.float32
bf16 = jnp.bfloat16

SEND, RECV, AGG, VALVE = slice(0, 2), slice(2, 4), slice(4, 5), slice(5, 6)


def call(body, outs, *args, smem=(), hbm=(), scratch=(), limit=32, final=False, aliases=None):
    def spec(at):
        if at in hbm:
            return pl.BlockSpec(memory_space=pltpu.HBM)
        return pl.BlockSpec(memory_space=pltpu.SMEM if at in smem else pltpu.VMEM)

    args = [
        pltpu.with_memory_space_constraint(arg, pltpu.HBM) if at in hbm else arg
        for at, arg in enumerate(args)
    ]
    return pl.pallas_call(
        body,
        out_shape=[
            jax.ShapeDtypeStruct(shape, kind) if final else pltpu.VMEM(shape, kind)
            for shape, kind in outs
        ],
        in_specs=[spec(at) for at in range(len(args))],
        out_specs=[pl.BlockSpec(memory_space=pltpu.VMEM)] * len(outs),
        scratch_shapes=list(scratch),
        input_output_aliases=aliases or {},
        compiler_params=pltpu.CompilerParams(vmem_limit_bytes=limit * 1024 * 1024),
    )(*args)


def partner(place, side):
    return place - 1 + 2 * ((place + side) % 2)


def pairing(subs, grps, side):
    moves = []
    for place in range(subs):
        other = partner(place, side)
        for group in range(grps):
            if 0 <= other < subs:
                target = other * grps + group
            else:
                target = place * grps + (group ^ 1 if group ^ 1 < grps else group)
            moves.append((place * grps + group, target))
    return moves


def row_of(ref, flipped):
    return jnp.where(flipped == 0, ref[0:1, :], ref[1:2, :])


def parity(side):
    return (lax.axis_index("sub") + side + 1) % 2


def along_lanes(field, places, axis):
    return jnp.take_along_axis(field, places, axis=axis, mode="promise_in_bounds")


def pick(field, places):
    return along_lanes(field, jnp.broadcast_to(places, field.shape), axis=1)


def pieces(field, count=2):
    result = []
    for _ in range(count):
        result.append(field.astype(bf16))
        field = field - result[-1].astype(f32)
    return result


def block_rows(blocks, field):
    return jnp.sum(blocks.astype(f32) * field[None], axis=1)


def local_product(blocks_ref, valve, field):
    rows = [block_rows(blocks_ref[at : at + 8], field) for at in range(0, blocks_ref.shape[0], 8)]
    return jnp.concatenate(rows, axis=0) + penalty_gain * valve.astype(f32) * field


def received(near, arrive_ref, count=2):
    parts = pieces(jnp.concatenate(near, axis=1), count)
    sums = jnp.dot(jnp.concatenate(parts, axis=0), arrive_ref[...], preferred_element_type=f32)
    size = near[0].shape[0]
    result = sums[:size]
    for at in range(size, count * size, size):
        result = result + sums[at : at + size]
    return result


def restricted(weighted, gather_ref):
    high = weighted.astype(bf16).astype(f32)
    rest = weighted - high
    middle = rest.astype(bf16).astype(f32)
    last = rest - middle
    row = lax.broadcasted_iota(jnp.int32, (8, weighted.shape[1]), 0)
    stack = jnp.where(row == 0, high, jnp.where(row == 1, middle, jnp.where(row == 2, last, 0.0)))
    sums = jnp.dot(stack.astype(bf16), gather_ref[...], preferred_element_type=f32)
    return jnp.sum(sums, axis=0, keepdims=True)


def total(field):
    return jnp.sum(jnp.sum(field, axis=0, keepdims=True), axis=1, keepdims=True)


def to_all(ref, row, first_lane, totals):
    lane = lax.broadcasted_iota(jnp.int32, (1, LANES), 1)
    for at, value in enumerate(totals):
        row = jnp.where(lane == first_lane + at, value, row)
    ref[...] = jnp.broadcast_to(row, ref.shape)


def flat(ref):
    return ref[...] if len(ref.shape) == 2 else ref[:, 0, :]


def summed(ref, first_lane, count):
    rows = jnp.broadcast_to(jnp.sum(flat(ref), axis=0, keepdims=True), (8, LANES))
    return [
        along_lanes(rows, jnp.full((8, LANES), first_lane + at, jnp.int32), axis=1)[0:1]
        for at in range(count)
    ]


def copy_all(pairs, sems):
    copies = [pltpu.make_async_copy(*pair, sems.at[at]) for at, pair in enumerate(pairs)]
    for copy in copies:
        copy.start()
    return copies


def first_send(guess_hbm, agg_hbm, send_hbm, recv_hbm, valve_hbm, odd_ref, even_ref, notes_ref,
               guess_ref, agg_ref, send_ref, recv_ref, valve_ref, sems):
    pairs = (
        (send_hbm, send_ref), (guess_hbm, guess_ref), (agg_hbm, agg_ref), (recv_hbm, recv_ref),
        (valve_hbm, valve_ref),
    )
    for copy in copy_all(pairs, sems):
        copy.wait()
    for side, ref in enumerate((odd_ref, even_ref)):
        ref[...] = pick(guess_ref[...], row_of(send_ref, parity(side)))
    notes_ref[...] = jnp.concatenate(
        [send_ref[...], recv_ref[...], agg_ref[...], valve_ref[...], jnp.zeros((2, LANES), jnp.int32)],
        axis=0,
    )


def wide(row):
    return jnp.concatenate([row, jnp.zeros((1, LANES - row.shape[1]), row.dtype)], axis=1)


def pack_constants(ref, coff_ref, prolong, agg, cdiag, places):
    cpd, width = coff_ref.shape
    for at in range(0, width, LANES):
        start = at // LANES * cpd
        ref[start : start + cpd, :] = coff_ref[:, at : at + LANES]
    base = cpd * (width // LANES)
    high, low = pieces(pick(prolong, places))
    size = high.shape[0]
    ref[base : base + size, :] = high
    ref[base + size : base + 2 * size, :] = low
    listed = pick(jnp.broadcast_to(agg.astype(f32), (8, LANES)), places)[0:1]
    one = cdiag.astype(bf16).astype(f32)
    two = (cdiag - one).astype(bf16).astype(f32)
    rows = [listed, one, two, cdiag - one - two, jnp.zeros((12, LANES), f32)]
    ref[base + 2 * size : base + 2 * size + 16, :] = jnp.concatenate(rows, axis=0).astype(bf16)


def prepare(live_hbm, guess_hbm, rhs_hbm, blocks_hbm, coff_hbm, prolong_hbm, cdiag_hbm, notes_ref,
            local_ref, arrive_ref, gather_ref, odd_ref, even_ref,
            live_ref, guess_ref, rhs_ref, blocks_ref, coff_ref, prolong_ref, cdiag_ref, sems):
    size = guess_ref.shape[0]
    chunk = size // 4
    pairs = [(coff_hbm, coff_ref), (prolong_hbm, prolong_ref), (cdiag_hbm, cdiag_ref),
             (live_hbm, live_ref), (guess_hbm, guess_ref)]
    for at in range(0, size, chunk):
        pairs.append((blocks_hbm.at[at : at + chunk], blocks_ref.at[at : at + chunk]))
    copies = copy_all(pairs + [(rhs_hbm, rhs_ref)], sems)
    for copy in copies[:4]:
        copy.wait()
    cdiag = wide(cdiag_ref[...])
    for side, ref in enumerate((odd_ref, even_ref)):
        places = row_of(notes_ref.at[SEND], parity(side))
        pack_constants(ref, coff_ref, prolong_ref[...], notes_ref[AGG], cdiag, places)
    count = arrive_ref.shape[1]
    slots = notes_ref.shape[1]
    coarse = lax.broadcasted_iota(jnp.int32, (LANES, count), 0)
    gather_ref[...] = jnp.where(notes_ref[AGG] == coarse, 1.0, 0.0).T.astype(bf16)
    place = lax.axis_index("sub")
    row = lax.broadcasted_iota(jnp.int32, (count, slots), 0)
    slot = lax.broadcasted_iota(jnp.int32, (count, slots), 1)
    for side in (0, 1):
        other = place + 1 - 2 * parity(side)
        there = (other >= 0) & (other < lax.axis_size("sub"))
        which = 1 - parity(side)
        live = jnp.where(there, live_ref[0, which], 0)
        hit = (row_of(notes_ref.at[RECV], which) == row) & (slot < live)
        arrive_ref[side * slots : (side + 1) * slots, :] = jnp.where(hit, 1.0, 0.0).T.astype(bf16)
    copies[4].wait()
    guess = guess_ref[...]
    penalty = penalty_gain * notes_ref[VALVE].astype(f32)
    for at in range(0, size, 8):
        if at % chunk == 0:
            copies[5 + at // chunk].wait()
        part = slice(at, at + 8)
        local_ref[part, :] = block_rows(blocks_ref[part], guess) + penalty * guess[part]
    copies[-1].wait()
    local_ref[...] = rhs_ref[...] - local_ref[...]


def residual(local_ref, odd_near_ref, even_near_ref, arrive_ref, gather_ref, prolong_ref,
             jscale_ref, notes_ref, odd_pack_ref, even_pack_ref, cpd, first_ref, out_ref, odd_ref,
             even_ref):
    near = [odd_near_ref[...], even_near_ref[...]]
    first = local_ref[...] + coupling * received(near, arrive_ref, 3)
    first_ref[...] = first
    weighted = jnp.sum(prolong_ref[...] * first, axis=0, keepdims=True)
    to_all(out_ref, restricted(weighted, gather_ref), cpd, [total(first * first)])
    scaled = jscale_ref[...] * first
    size = first.shape[0]
    tail = odd_ref.shape[0] - 2 * size
    for side, ref in enumerate((odd_ref, even_ref)):
        high, low = pieces(pick(scaled, row_of(notes_ref.at[SEND], parity(side))))
        ref[tail : tail + size, :] = high
        ref[tail + size :, :] = low


def unpack(own_ref, even_ref, odd_ref, cpd, matrix_ref, odd_weights_ref, even_weights_ref,
           odd_first_ref, even_first_ref, info_ref):
    width = matrix_ref.shape[1]
    size = odd_first_ref.shape[0]
    base = cpd * (width // LANES)
    rows = []
    for slot, ref in enumerate((own_ref, odd_ref, even_ref)):
        for at in range(0, width, LANES):
            start = at // LANES * cpd
            matrix_ref[slot * SLOT : slot * SLOT + cpd, at : at + LANES] = ref[start : start + cpd, :]
        matrix_ref[slot * SLOT + cpd : (slot + 1) * SLOT, :] = jnp.zeros((SLOT - cpd, width), bf16)
        rows.append(ref[base + 2 * size : base + 2 * size + 16, :].astype(f32))
    for ref, weights_ref, near_ref in (
        (odd_ref, odd_weights_ref, odd_first_ref), (even_ref, even_weights_ref, even_first_ref)
    ):
        for start, to_ref in ((base, weights_ref), (base + 2 * size + 16, near_ref)):
            high, low = ref[start : start + size, :], ref[start + size : start + 2 * size, :]
            to_ref[...] = high.astype(f32) + low.astype(f32)
    infos = [row[1:2] + row[2:3] + row[3:4] for row in rows] + [row[0:1] for row in rows[1:]]
    info_ref[...] = jnp.concatenate(infos + [jnp.zeros((3, LANES), f32)], axis=0)


def unpack(own_ref, even_ref, odd_ref, cpd, matrix_ref, odd_weights_ref, even_weights_ref,
           odd_first_ref, even_first_ref, info_ref):
    width = matrix_ref.shape[1]
    size = odd_first_ref.shape[0]
    base = cpd * (width // LANES)
    rows = []
    for slot, ref in enumerate((own_ref, odd_ref, even_ref)):
        for at in range(0, width, LANES):
            start = at // LANES * cpd
            matrix_ref[slot * SLOT : slot * SLOT + cpd, at : at + LANES] = ref[start : start + cpd, :]
        matrix_ref[slot * SLOT + cpd : (slot + 1) * SLOT, :] = jnp.zeros((SLOT - cpd, width), bf16)
        rows.append(ref[base + 2 * size : base + 2 * size + 16, :].astype(f32))
    for ref, weights_ref, near_ref in (
        (odd_ref, odd_weights_ref, odd_first_ref), (even_ref, even_weights_ref, even_first_ref)
    ):
        for start, to_ref in ((base, weights_ref), (base + 2 * size + 16, near_ref)):
            high, low = ref[start : start + size, :], ref[start + size : start + 2 * size, :]
            to_ref[...] = high.astype(f32) + low.astype(f32)
    infos = [row[1:2] + row[2:3] + row[3:4] for row in rows] + [row[0:1] for row in rows[1:]]
    info_ref[...] = jnp.concatenate(infos + [jnp.zeros((3, LANES), f32)], axis=0)


def look_ahead(image_ref, first_ref, jscale_ref, prolong_ref, blocks_ref, notes_ref,
               lead_two_ref, lead_ref, pull_ref):
    valve, jscale = notes_ref[VALVE], jscale_ref[...]
    lead_two_ref[...] = local_product(blocks_ref, valve, jscale * image_ref[...])
    lead_ref[...] = local_product(blocks_ref, valve, jscale * first_ref[...])
    pull_ref[...] = local_product(blocks_ref, valve, prolong_ref[...])


def solve_coarse(parts, matrix_ref, near_rows, cdiags, cpd):
    group = parts[0].shape[0]
    shape = (group, LANES)
    row = lax.broadcasted_iota(jnp.int32, shape, 0)
    lane = lax.broadcasted_iota(jnp.int32, shape, 1)
    masks = [(at + lane) // cpd == row for at in range(0, group * cpd, LANES)]
    source = lax.rem(lane - cpd * row + cpd * group, LANES)
    tiles = []
    for part in parts:
        shifted = along_lanes(part, source, axis=1)
        tiles.extend(jnp.where(mask, shifted, 0.0) for mask in masks)
    product = lax.dot_general(
        jnp.concatenate(tiles, axis=1).astype(bf16), matrix_ref[...], (((1,), (1,)), ((), ())),
        preferred_element_type=f32,
    )
    product = jnp.sum(product, axis=0, keepdims=True)
    low = product[:, :LANES]
    high = jnp.concatenate([product[:, LANES:], jnp.zeros((1, LANES - SLOT), f32)], axis=1)
    turned = pltpu.roll(jnp.broadcast_to(low, (8, LANES)), LANES - SLOT, 1)[0:1]
    shares = (low, turned, high)
    return [cdiag * row + share for cdiag, row, share in zip(cdiags, near_rows, shares)]


def parts_of(ref, cpd):
    group = math.lcm(cpd, LANES) // cpd
    rows = flat(ref)
    return [rows[at : at + group, :] for at in range(0, rows.shape[0], group)]


def rows_near(parts, grp_size):
    group = parts[0].shape[0]
    count = group * len(parts)
    me = lax.axis_index("sub") * grp_size + lax.axis_index("grp")
    place = lax.broadcasted_iota(jnp.int32, parts[0].shape, 0)
    rows = []
    for shift in [0] + [grp_size * (1 - 2 * parity(side)) for side in (0, 1)]:
        wanted = lax.rem(me + shift + count, count)
        found = jnp.where(place == wanted, parts[0], 0.0)
        for at, part in enumerate(parts[1:], 1):
            found = jnp.where(place + at * group == wanted, part, found)
        rows.append(jnp.sum(found, axis=0, keepdims=True))
    return rows


def spread_of(solution, agg):
    wide = jnp.broadcast_to(solution, (8, LANES))
    return along_lanes(wide, jnp.broadcast_to(agg, (8, LANES)), axis=1)[0:1]


def near_spread(weights_ref, info_ref, side, solution):
    agg = info_ref[3 + side : 4 + side, :].astype(jnp.int32)
    return weights_ref[...] * spread_of(solution, agg)


def first_step(got_ref, own_pack_ref, even_pack_ref, odd_pack_ref, first_ref, jscale_ref,
               prolong_ref, blocks_ref, notes_ref, arrive_ref, gather_ref, grp_size, cpd,
               basis_ref, direction_ref, image_ref, out_ref, odd_ref, even_ref, matrix_ref,
               odd_weights_ref, even_weights_ref, odd_near_ref, even_near_ref, info_ref):
    unpack(own_pack_ref, even_pack_ref, odd_pack_ref, cpd, matrix_ref, odd_weights_ref,
           even_weights_ref, odd_near_ref, even_near_ref, info_ref)
    inverse = 1.0 / jnp.sqrt(summed(got_ref, cpd, 1)[0])
    parts = [part * inverse for part in parts_of(got_ref, cpd)]
    cdiags = [info_ref[at : at + 1, :] for at in range(3)]
    solved = solve_coarse(parts, matrix_ref, rows_near(parts, grp_size), cdiags, cpd)
    basis = first_ref[...] * inverse
    basis_ref[...] = basis
    spread = spread_of(solved[0], notes_ref[AGG])
    jscale, prolong = jscale_ref[...], prolong_ref[...]
    direction = jscale * basis + prolong * spread
    direction_ref[...] = direction
    near = [
        odd_near_ref[...] * inverse + near_spread(odd_weights_ref, info_ref, 0, solved[1]),
        even_near_ref[...] * inverse + near_spread(even_weights_ref, info_ref, 1, solved[2]),
    ]
    image = local_product(blocks_ref, notes_ref[VALVE], direction)
    image = image - coupling * received(near, arrive_ref)
    image_ref[...] = image
    weighted = jnp.sum(prolong * image, axis=0, keepdims=True)
    dots = [total(basis * image), total(image * image)]
    to_all(out_ref, restricted(weighted, gather_ref), cpd, dots)
    scaled = jscale * image
    for side, ref in enumerate((odd_ref, even_ref)):
        ref[...] = pick(scaled, row_of(notes_ref.at[SEND], parity(side)))


def second_step(got_ref, first_got_ref, even_near_ref, odd_near_ref, odd_first_ref, even_first_ref,
                odd_weights_ref, even_weights_ref, matrix_ref, info_ref, basis_ref, image_ref,
                jscale_ref, prolong_ref, blocks_ref, notes_ref, arrive_ref,
                grp_size, cpd, basis_two_ref, direction_ref, image_two_ref, scalars_ref, out_ref):
    beta = jnp.sqrt(summed(first_got_ref, cpd, 1)[0])
    along, energy = summed(got_ref, cpd, 2)
    height = jnp.sqrt(jnp.maximum(energy - along * along, 0.01 * energy))
    inverse = 1.0 / height
    slope = along / beta

    def mixed(new, old):
        return (new - slope * old) * inverse

    parts = [
        mixed(new, old) for new, old in zip(parts_of(got_ref, cpd), parts_of(first_got_ref, cpd))
    ]
    cdiags = [info_ref[at : at + 1, :] for at in range(3)]
    solved = solve_coarse(parts, matrix_ref, rows_near(parts, grp_size), cdiags, cpd)
    basis = (image_ref[...] - along * basis_ref[...]) * inverse
    basis_two_ref[...] = basis
    spread = spread_of(solved[0], notes_ref[AGG])
    direction = jscale_ref[...] * basis + prolong_ref[...] * spread
    direction_ref[...] = direction
    near = [
        mixed(odd_near_ref[...], odd_first_ref[...])
        + near_spread(odd_weights_ref, info_ref, 0, solved[1]),
        mixed(even_near_ref[...], even_first_ref[...])
        + near_spread(even_weights_ref, info_ref, 1, solved[2]),
    ]
    image = local_product(blocks_ref, notes_ref[VALVE], direction)
    image = image - coupling * received(near, arrive_ref)
    image_two_ref[...] = image
    scalars_ref[...] = jnp.concatenate([beta, along, height, jnp.zeros((5, LANES), f32)], axis=0)
    dots = [total(basis_ref[...] * image), total(basis * image), total(image * image)]
    to_all(out_ref, jnp.zeros((1, LANES), f32), 0, dots)


def finish(got_ref, scalars_ref, guess_ref, basis_ref, basis_two_ref, direction_ref,
           direction_two_ref, image_ref, solution_ref, next_ref):
    beta, h11, h21 = scalars_ref[0:1, :], scalars_ref[1:2, :], scalars_ref[2:3, :]
    h12, h22, energy = summed(got_ref, 0, 3)
    h32 = jnp.sqrt(jnp.maximum(energy - (h12 * h12 + h22 * h22), 0.01 * energy))
    g00 = h11 * h11 + h21 * h21
    g01 = h11 * h12 + h21 * h22
    g11 = h12 * h12 + h22 * h22 + h32 * h32
    t0, t1 = beta * h11, beta * h12
    factor = g01 / g00
    c1 = (t1 - factor * t0) / (g11 - factor * g01)
    c0 = (t0 - g01 * c1) / g00
    solution_ref[...] = guess_ref[...] + c0 * direction_ref[...] + c1 * direction_two_ref[...]
    next_ref[...] = (image_ref[...] - h12 * basis_ref[...] - h22 * basis_two_ref[...]) * (1.0 / h32)


def on_device(rhs, guess, blocks, valve, jscale, prolong, agg_map, cdiag, coff, send_rows,
              recv_rows, live_counts):
    rhs, guess, blocks, jscale, prolong = rhs[0, 0], guess[0, 0], blocks[0, 0], jscale[0, 0], prolong[0, 0]
    valve, agg, live = valve[0], agg_map[0], live_counts[0]
    send, recv = send_rows[0, 0], recv_rows[0, 0]
    size, count = guess.shape
    slots = send.shape[1]
    cpd = cdiag.shape[0]
    subs, grps = lax.axis_size("sub"), lax.axis_size("grp")
    devices = subs * grps
    cdiag = cdiag[None, :]
    moves = [pairing(subs, grps, side) for side in (0, 1)]

    def exchange(odd, even):
        return lax.ppermute(odd, AXES, moves[0]), lax.ppermute(even, AXES, moves[1])

    def everyone(rows):
        return lax.all_to_all(rows, AXES, 0, 0, tiled=True)

    field = ((size, count), f32)
    near = ((size, slots), f32)
    rows_out = ((devices, LANES), f32)
    small = ((8, LANES), f32)
    items = (guess, agg, send, recv, valve)
    odd, even, notes = call(
        first_send, [near, near, ((8, LANES), jnp.int32)], *items, hbm=range(5), limit=16,
        scratch=[pltpu.VMEM(item.shape, item.dtype) for item in items]
        + [pltpu.SemaphoreType.DMA((5,))],
    )
    odd_guess, even_guess = exchange(odd, even)
    packed = ((cpd * (coff.shape[1] // LANES) + 4 * size + 16, LANES), bf16)
    items = (guess, rhs, blocks, coff, prolong, cdiag)
    local, arrive, gather, odd, even = call(
        prepare,
        [field, ((2 * slots, count), bf16), ((count, LANES), bf16), packed, packed],
        live, *items, notes, hbm=range(7),
        scratch=[pltpu.SMEM(live.shape, live.dtype)]
        + [pltpu.VMEM(item.shape, item.dtype) for item in items]
        + [pltpu.SemaphoreType.DMA((10,))],
    )
    first, rows, odd, even = call(
        lambda *refs: residual(*refs[:10], cpd, *refs[10:]), [field, rows_out, packed, packed],
        local, odd_guess, even_guess, arrive, gather, prolong, jscale, notes, odd, even,
        aliases={8: 2, 9: 3},
    )
    even_pack = lax.ppermute(even, AXES, moves[1])
    odd_pack = lax.ppermute(odd, AXES, moves[0])
    own_pack = odd
    first_got = everyone(rows)
    (basis, direction, image, rows, odd, even, matrix, odd_weights, even_weights, odd_first,
     even_first, info) = call(
        lambda *refs: first_step(*refs[:11], grps, cpd, *refs[11:]),
        [field, field, field, rows_out, near, near,
         ((3 * SLOT, coff.shape[1]), bf16)] + [near] * 4 + [small],
        first_got, own_pack, even_pack, odd_pack, first, jscale, prolong, blocks, notes, arrive,
        gather,
    )
    odd_near, even_near = exchange(odd, even)
    got = everyone(rows)
    basis_two, direction_two, image_two, scalars, rows = call(
        lambda *refs: second_step(*refs[:17], grps, cpd, *refs[17:]),
        [field, field, field, ((8, LANES), f32), rows_out],
        got, first_got, even_near, odd_near, odd_first, even_first, odd_weights, even_weights, matrix,
        info, basis, image, jscale, prolong, blocks, notes, arrive,
    )
    got = everyone(rows)
    solution, next_basis = call(
        finish, [field, field],
        got, scalars, guess, basis, basis_two, direction, direction_two, image_two, final=True,
    )
    return solution[None, None], next_basis[None, None]


def solution(mesh):
    return jax.shard_map(
        on_device,
        mesh=mesh,
        in_specs=(
            P("sub", "grp", None, None),
            P("sub", "grp", None, None),
            P("sub", "grp", None, None, None),
            P("sub", "grp", None),
            P("sub", "grp", None, None),
            P("sub", "grp", None, None),
            P("sub", "grp", None),
            P(("sub", "grp")),
            P(("sub", "grp"), None),
            P("sub", "grp", None, None),
            P("sub", "grp", None, None),
            P("sub", "grp", None),
        ),
        out_specs=(P("sub", "grp", None, None), P("sub", "grp", None, None)),
        check_vma=False,
    )
```

```python
import math

import jax
import jax.numpy as jnp
from jax import lax
from jax.experimental import pallas as pl
from jax.experimental.pallas import tpu as pltpu
from jax.sharding import PartitionSpec as P

penalty_gain = 3.0
coupling = 0.5

LANES = 128
SLOT = 64
AXES = ("sub", "grp")
f32 = jnp.float32
bf16 = jnp.bfloat16

SEND, RECV, AGG, VALVE = slice(0, 2), slice(2, 4), slice(4, 5), slice(5, 6)


def call(body, outs, *args, smem=(), hbm=(), scratch=(), limit=32, final=False, aliases=None):
    def spec(at):
        if at in hbm:
            return pl.BlockSpec(memory_space=pltpu.HBM)
        return pl.BlockSpec(memory_space=pltpu.SMEM if at in smem else pltpu.VMEM)

    args = [
        pltpu.with_memory_space_constraint(arg, pltpu.HBM) if at in hbm else arg
        for at, arg in enumerate(args)
    ]
    return pl.pallas_call(
        body,
        out_shape=[
            jax.ShapeDtypeStruct(shape, kind) if final else pltpu.VMEM(shape, kind)
            for shape, kind in outs
        ],
        in_specs=[spec(at) for at in range(len(args))],
        out_specs=[pl.BlockSpec(memory_space=pltpu.VMEM)] * len(outs),
        scratch_shapes=list(scratch),
        input_output_aliases=aliases or {},
        compiler_params=pltpu.CompilerParams(vmem_limit_bytes=limit * 1024 * 1024),
    )(*args)


def partner(place, side):
    return place - 1 + 2 * ((place + side) % 2)


def pairing(subs, grps, side):
    moves = []
    for place in range(subs):
        other = partner(place, side)
        for group in range(grps):
            if 0 <= other < subs:
                target = other * grps + group
            else:
                target = place * grps + (group ^ 1 if group ^ 1 < grps else group)
            moves.append((place * grps + group, target))
    return moves


def row_of(ref, flipped):
    return jnp.where(flipped == 0, ref[0:1, :], ref[1:2, :])


def parity(side):
    return (lax.axis_index("sub") + side + 1) % 2


def along_lanes(field, places, axis):
    return jnp.take_along_axis(field, places, axis=axis, mode="promise_in_bounds")


def pick(field, places):
    return along_lanes(field, jnp.broadcast_to(places, field.shape), axis=1)


def pieces(field, count=2):
    result = []
    for _ in range(count):
        result.append(field.astype(bf16))
        field = field - result[-1].astype(f32)
    return result


def block_rows(blocks, field):
    return jnp.sum(blocks.astype(f32) * field[None], axis=1)


def local_product(blocks_ref, valve, field):
    rows = [block_rows(blocks_ref[at : at + 8], field) for at in range(0, blocks_ref.shape[0], 8)]
    return jnp.concatenate(rows, axis=0) + penalty_gain * valve.astype(f32) * field


def received(near, arrive_ref, count=2):
    parts = pieces(jnp.concatenate(near, axis=1), count)
    sums = jnp.dot(jnp.concatenate(parts, axis=0), arrive_ref[...], preferred_element_type=f32)
    size = near[0].shape[0]
    result = sums[:size]
    for at in range(size, count * size, size):
        result = result + sums[at : at + size]
    return result


def restricted(weighted, gather_ref):
    high = weighted.astype(bf16).astype(f32)
    rest = weighted - high
    middle = rest.astype(bf16).astype(f32)
    last = rest - middle
    row = lax.broadcasted_iota(jnp.int32, (8, weighted.shape[1]), 0)
    stack = jnp.where(row == 0, high, jnp.where(row == 1, middle, jnp.where(row == 2, last, 0.0)))
    sums = jnp.dot(stack.astype(bf16), gather_ref[...], preferred_element_type=f32)
    return jnp.sum(sums, axis=0, keepdims=True)


def total(field):
    return jnp.sum(jnp.sum(field, axis=0, keepdims=True), axis=1, keepdims=True)


def to_all(ref, row, first_lane, totals):
    lane = lax.broadcasted_iota(jnp.int32, (1, LANES), 1)
    for at, value in enumerate(totals):
        row = jnp.where(lane == first_lane + at, value, row)
    ref[...] = jnp.broadcast_to(row, ref.shape)


def flat(ref):
    return ref[...] if len(ref.shape) == 2 else ref[:, 0, :]


def summed(ref, first_lane, count):
    rows = jnp.broadcast_to(jnp.sum(flat(ref), axis=0, keepdims=True), (8, LANES))
    return [
        along_lanes(rows, jnp.full((8, LANES), first_lane + at, jnp.int32), axis=1)[0:1]
        for at in range(count)
    ]


def copy_all(pairs, sems):
    copies = [pltpu.make_async_copy(*pair, sems.at[at]) for at, pair in enumerate(pairs)]
    for copy in copies:
        copy.start()
    return copies


def first_send(guess_hbm, agg_hbm, send_hbm, recv_hbm, valve_hbm, odd_ref, even_ref, notes_ref,
               guess_ref, agg_ref, send_ref, recv_ref, valve_ref, sems):
    pairs = (
        (send_hbm, send_ref), (guess_hbm, guess_ref), (agg_hbm, agg_ref), (recv_hbm, recv_ref),
        (valve_hbm, valve_ref),
    )
    for copy in copy_all(pairs, sems):
        copy.wait()
    for side, ref in enumerate((odd_ref, even_ref)):
        ref[...] = pick(guess_ref[...], row_of(send_ref, parity(side)))
    notes_ref[...] = jnp.concatenate(
        [send_ref[...], recv_ref[...], agg_ref[...], valve_ref[...], jnp.zeros((2, LANES), jnp.int32)],
        axis=0,
    )


def wide(row):
    return jnp.concatenate([row, jnp.zeros((1, LANES - row.shape[1]), row.dtype)], axis=1)


def pack_constants(ref, coff_ref, prolong, agg, cdiag, places):
    cpd, width = coff_ref.shape
    for at in range(0, width, LANES):
        start = at // LANES * cpd
        ref[start : start + cpd, :] = coff_ref[:, at : at + LANES]
    base = cpd * (width // LANES)
    high, low = pieces(pick(prolong, places))
    size = high.shape[0]
    ref[base : base + size, :] = high
    ref[base + size : base + 2 * size, :] = low
    listed = pick(jnp.broadcast_to(agg.astype(f32), (8, LANES)), places)[0:1]
    one = cdiag.astype(bf16).astype(f32)
    two = (cdiag - one).astype(bf16).astype(f32)
    rows = [listed, one, two, cdiag - one - two, jnp.zeros((12, LANES), f32)]
    ref[base + 2 * size : base + 2 * size + 16, :] = jnp.concatenate(rows, axis=0).astype(bf16)


def prepare(live_hbm, guess_hbm, rhs_hbm, blocks_hbm, coff_hbm, prolong_hbm, cdiag_hbm, notes_ref,
            local_ref, arrive_ref, gather_ref, odd_ref, even_ref, blocks_ref,
            live_ref, guess_ref, rhs_ref, coff_ref, prolong_ref, cdiag_ref, sems):
    size = guess_ref.shape[0]
    chunk = size // 4
    pairs = [(coff_hbm, coff_ref), (prolong_hbm, prolong_ref), (cdiag_hbm, cdiag_ref),
             (live_hbm, live_ref), (guess_hbm, guess_ref)]
    for at in range(0, size, chunk):
        pairs.append((blocks_hbm.at[at : at + chunk], blocks_ref.at[at : at + chunk]))
    copies = copy_all(pairs + [(rhs_hbm, rhs_ref)], sems)
    for copy in copies[:4]:
        copy.wait()
    cdiag = wide(cdiag_ref[...])
    for side, ref in enumerate((odd_ref, even_ref)):
        places = row_of(notes_ref.at[SEND], parity(side))
        pack_constants(ref, coff_ref, prolong_ref[...], notes_ref[AGG], cdiag, places)
    count = arrive_ref.shape[1]
    slots = notes_ref.shape[1]
    coarse = lax.broadcasted_iota(jnp.int32, (LANES, count), 0)
    gather_ref[...] = jnp.where(notes_ref[AGG] == coarse, 1.0, 0.0).T.astype(bf16)
    place = lax.axis_index("sub")
    row = lax.broadcasted_iota(jnp.int32, (count, slots), 0)
    slot = lax.broadcasted_iota(jnp.int32, (count, slots), 1)
    for side in (0, 1):
        other = place + 1 - 2 * parity(side)
        there = (other >= 0) & (other < lax.axis_size("sub"))
        which = 1 - parity(side)
        live = jnp.where(there, live_ref[0, which], 0)
        hit = (row_of(notes_ref.at[RECV], which) == row) & (slot < live)
        arrive_ref[side * slots : (side + 1) * slots, :] = jnp.where(hit, 1.0, 0.0).T.astype(bf16)
    copies[4].wait()
    guess = guess_ref[...]
    penalty = penalty_gain * notes_ref[VALVE].astype(f32)
    for at in range(0, size, 8):
        if at % chunk == 0:
            copies[5 + at // chunk].wait()
        part = slice(at, at + 8)
        local_ref[part, :] = block_rows(blocks_ref[part], guess) + penalty * guess[part]
    copies[-1].wait()
    local_ref[...] = rhs_ref[...] - local_ref[...]


def residual(local_ref, odd_near_ref, even_near_ref, arrive_ref, gather_ref, prolong_ref,
             jscale_ref, notes_ref, odd_pack_ref, even_pack_ref, cpd, first_ref, out_ref, odd_ref,
             even_ref):
    near = [odd_near_ref[...], even_near_ref[...]]
    first = local_ref[...] + coupling * received(near, arrive_ref, 3)
    first_ref[...] = first
    weighted = jnp.sum(prolong_ref[...] * first, axis=0, keepdims=True)
    to_all(out_ref, restricted(weighted, gather_ref), cpd, [total(first * first)])
    scaled = jscale_ref[...] * first
    size = first.shape[0]
    tail = odd_ref.shape[0] - 2 * size
    for side, ref in enumerate((odd_ref, even_ref)):
        high, low = pieces(pick(scaled, row_of(notes_ref.at[SEND], parity(side))))
        ref[tail : tail + size, :] = high
        ref[tail + size :, :] = low


def unpack(own_ref, even_ref, odd_ref, cpd, matrix_ref, odd_weights_ref, even_weights_ref,
           odd_first_ref, even_first_ref, info_ref):
    width = matrix_ref.shape[1]
    size = odd_first_ref.shape[0]
    base = cpd * (width // LANES)
    rows = []
    for slot, ref in enumerate((own_ref, odd_ref, even_ref)):
        for at in range(0, width, LANES):
            start = at // LANES * cpd
            matrix_ref[slot * SLOT : slot * SLOT + cpd, at : at + LANES] = ref[start : start + cpd, :]
        matrix_ref[slot * SLOT + cpd : (slot + 1) * SLOT, :] = jnp.zeros((SLOT - cpd, width), bf16)
        rows.append(ref[base + 2 * size : base + 2 * size + 16, :].astype(f32))
    for ref, weights_ref, near_ref in (
        (odd_ref, odd_weights_ref, odd_first_ref), (even_ref, even_weights_ref, even_first_ref)
    ):
        for start, to_ref in ((base, weights_ref), (base + 2 * size + 16, near_ref)):
            high, low = ref[start : start + size, :], ref[start + size : start + 2 * size, :]
            to_ref[...] = high.astype(f32) + low.astype(f32)
    infos = [row[1:2] + row[2:3] + row[3:4] for row in rows] + [row[0:1] for row in rows[1:]]
    info_ref[...] = jnp.concatenate(infos + [jnp.zeros((3, LANES), f32)], axis=0)


def unpack(own_ref, even_ref, odd_ref, cpd, matrix_ref, odd_weights_ref, even_weights_ref,
           odd_first_ref, even_first_ref, info_ref):
    width = matrix_ref.shape[1]
    size = odd_first_ref.shape[0]
    base = cpd * (width // LANES)
    rows = []
    for slot, ref in enumerate((own_ref, odd_ref, even_ref)):
        for at in range(0, width, LANES):
            start = at // LANES * cpd
            matrix_ref[slot * SLOT : slot * SLOT + cpd, at : at + LANES] = ref[start : start + cpd, :]
        matrix_ref[slot * SLOT + cpd : (slot + 1) * SLOT, :] = jnp.zeros((SLOT - cpd, width), bf16)
        rows.append(ref[base + 2 * size : base + 2 * size + 16, :].astype(f32))
    for ref, weights_ref, near_ref in (
        (odd_ref, odd_weights_ref, odd_first_ref), (even_ref, even_weights_ref, even_first_ref)
    ):
        for start, to_ref in ((base, weights_ref), (base + 2 * size + 16, near_ref)):
            high, low = ref[start : start + size, :], ref[start + size : start + 2 * size, :]
            to_ref[...] = high.astype(f32) + low.astype(f32)
    infos = [row[1:2] + row[2:3] + row[3:4] for row in rows] + [row[0:1] for row in rows[1:]]
    info_ref[...] = jnp.concatenate(infos + [jnp.zeros((3, LANES), f32)], axis=0)


def look_ahead(image_ref, first_ref, jscale_ref, prolong_ref, blocks_ref, notes_ref,
               lead_two_ref, lead_ref, pull_ref):
    valve, jscale = notes_ref[VALVE], jscale_ref[...]
    lead_two_ref[...] = local_product(blocks_ref, valve, jscale * image_ref[...])
    lead_ref[...] = local_product(blocks_ref, valve, jscale * first_ref[...])
    pull_ref[...] = local_product(blocks_ref, valve, prolong_ref[...])


def solve_coarse(parts, matrix_ref, near_rows, cdiags, cpd):
    group = parts[0].shape[0]
    shape = (group, LANES)
    row = lax.broadcasted_iota(jnp.int32, shape, 0)
    lane = lax.broadcasted_iota(jnp.int32, shape, 1)
    masks = [(at + lane) // cpd == row for at in range(0, group * cpd, LANES)]
    source = lax.rem(lane - cpd * row + cpd * group, LANES)
    tiles = []
    for part in parts:
        shifted = along_lanes(part, source, axis=1)
        tiles.extend(jnp.where(mask, shifted, 0.0) for mask in masks)
    product = lax.dot_general(
        jnp.concatenate(tiles, axis=1).astype(bf16), matrix_ref[...], (((1,), (1,)), ((), ())),
        preferred_element_type=f32,
    )
    product = jnp.sum(product, axis=0, keepdims=True)
    low = product[:, :LANES]
    high = jnp.concatenate([product[:, LANES:], jnp.zeros((1, LANES - SLOT), f32)], axis=1)
    turned = pltpu.roll(jnp.broadcast_to(low, (8, LANES)), LANES - SLOT, 1)[0:1]
    shares = (low, turned, high)
    return [cdiag * row + share for cdiag, row, share in zip(cdiags, near_rows, shares)]


def parts_of(ref, cpd):
    group = math.lcm(cpd, LANES) // cpd
    rows = flat(ref)
    return [rows[at : at + group, :] for at in range(0, rows.shape[0], group)]


def rows_near(parts, grp_size):
    group = parts[0].shape[0]
    count = group * len(parts)
    me = lax.axis_index("sub") * grp_size + lax.axis_index("grp")
    place = lax.broadcasted_iota(jnp.int32, parts[0].shape, 0)
    rows = []
    for shift in [0] + [grp_size * (1 - 2 * parity(side)) for side in (0, 1)]:
        wanted = lax.rem(me + shift + count, count)
        found = jnp.where(place == wanted, parts[0], 0.0)
        for at, part in enumerate(parts[1:], 1):
            found = jnp.where(place + at * group == wanted, part, found)
        rows.append(jnp.sum(found, axis=0, keepdims=True))
    return rows


def spread_of(solution, agg):
    wide = jnp.broadcast_to(solution, (8, LANES))
    return along_lanes(wide, jnp.broadcast_to(agg, (8, LANES)), axis=1)[0:1]


def near_spread(weights_ref, info_ref, side, solution):
    agg = info_ref[3 + side : 4 + side, :].astype(jnp.int32)
    return weights_ref[...] * spread_of(solution, agg)


def first_step(got_ref, own_pack_ref, even_pack_ref, odd_pack_ref, first_ref, jscale_ref,
               prolong_ref, blocks_ref, notes_ref, arrive_ref, gather_ref, grp_size, cpd,
               basis_ref, direction_ref, image_ref, out_ref, odd_ref, even_ref, matrix_ref,
               odd_weights_ref, even_weights_ref, odd_near_ref, even_near_ref, info_ref):
    unpack(own_pack_ref, even_pack_ref, odd_pack_ref, cpd, matrix_ref, odd_weights_ref,
           even_weights_ref, odd_near_ref, even_near_ref, info_ref)
    inverse = 1.0 / jnp.sqrt(summed(got_ref, cpd, 1)[0])
    parts = [part * inverse for part in parts_of(got_ref, cpd)]
    cdiags = [info_ref[at : at + 1, :] for at in range(3)]
    solved = solve_coarse(parts, matrix_ref, rows_near(parts, grp_size), cdiags, cpd)
    basis = first_ref[...] * inverse
    basis_ref[...] = basis
    spread = spread_of(solved[0], notes_ref[AGG])
    jscale, prolong = jscale_ref[...], prolong_ref[...]
    direction = jscale * basis + prolong * spread
    direction_ref[...] = direction
    near = [
        odd_near_ref[...] * inverse + near_spread(odd_weights_ref, info_ref, 0, solved[1]),
        even_near_ref[...] * inverse + near_spread(even_weights_ref, info_ref, 1, solved[2]),
    ]
    image = local_product(blocks_ref, notes_ref[VALVE], direction)
    image = image - coupling * received(near, arrive_ref)
    image_ref[...] = image
    weighted = jnp.sum(prolong * image, axis=0, keepdims=True)
    dots = [total(basis * image), total(image * image)]
    to_all(out_ref, restricted(weighted, gather_ref), cpd, dots)
    scaled = jscale * image
    for side, ref in enumerate((odd_ref, even_ref)):
        ref[...] = pick(scaled, row_of(notes_ref.at[SEND], parity(side)))


def second_step(got_ref, first_got_ref, even_near_ref, odd_near_ref, odd_first_ref, even_first_ref,
                odd_weights_ref, even_weights_ref, matrix_ref, info_ref, basis_ref, image_ref,
                jscale_ref, prolong_ref, blocks_ref, notes_ref, arrive_ref,
                grp_size, cpd, basis_two_ref, direction_ref, image_two_ref, scalars_ref, out_ref):
    beta = jnp.sqrt(summed(first_got_ref, cpd, 1)[0])
    along, energy = summed(got_ref, cpd, 2)
    height = jnp.sqrt(jnp.maximum(energy - along * along, 0.01 * energy))
    inverse = 1.0 / height
    slope = along / beta

    def mixed(new, old):
        return (new - slope * old) * inverse

    parts = [
        mixed(new, old) for new, old in zip(parts_of(got_ref, cpd), parts_of(first_got_ref, cpd))
    ]
    cdiags = [info_ref[at : at + 1, :] for at in range(3)]
    solved = solve_coarse(parts, matrix_ref, rows_near(parts, grp_size), cdiags, cpd)
    basis = (image_ref[...] - along * basis_ref[...]) * inverse
    basis_two_ref[...] = basis
    spread = spread_of(solved[0], notes_ref[AGG])
    direction = jscale_ref[...] * basis + prolong_ref[...] * spread
    direction_ref[...] = direction
    near = [
        mixed(odd_near_ref[...], odd_first_ref[...])
        + near_spread(odd_weights_ref, info_ref, 0, solved[1]),
        mixed(even_near_ref[...], even_first_ref[...])
        + near_spread(even_weights_ref, info_ref, 1, solved[2]),
    ]
    image = local_product(blocks_ref, notes_ref[VALVE], direction)
    image = image - coupling * received(near, arrive_ref)
    image_two_ref[...] = image
    scalars_ref[...] = jnp.concatenate([beta, along, height, jnp.zeros((5, LANES), f32)], axis=0)
    dots = [total(basis_ref[...] * image), total(basis * image), total(image * image)]
    to_all(out_ref, jnp.zeros((1, LANES), f32), 0, dots)


def finish(got_ref, scalars_ref, guess_ref, basis_ref, basis_two_ref, direction_ref,
           direction_two_ref, image_ref, solution_ref, next_ref):
    beta, h11, h21 = scalars_ref[0:1, :], scalars_ref[1:2, :], scalars_ref[2:3, :]
    h12, h22, energy = summed(got_ref, 0, 3)
    h32 = jnp.sqrt(jnp.maximum(energy - (h12 * h12 + h22 * h22), 0.01 * energy))
    g00 = h11 * h11 + h21 * h21
    g01 = h11 * h12 + h21 * h22
    g11 = h12 * h12 + h22 * h22 + h32 * h32
    t0, t1 = beta * h11, beta * h12
    factor = g01 / g00
    c1 = (t1 - factor * t0) / (g11 - factor * g01)
    c0 = (t0 - g01 * c1) / g00
    solution_ref[...] = guess_ref[...] + c0 * direction_ref[...] + c1 * direction_two_ref[...]
    next_ref[...] = (image_ref[...] - h12 * basis_ref[...] - h22 * basis_two_ref[...]) * (1.0 / h32)


def on_device(rhs, guess, blocks, valve, jscale, prolong, agg_map, cdiag, coff, send_rows,
              recv_rows, live_counts):
    rhs, guess, blocks, jscale, prolong = rhs[0, 0], guess[0, 0], blocks[0, 0], jscale[0, 0], prolong[0, 0]
    valve, agg, live = valve[0], agg_map[0], live_counts[0]
    send, recv = send_rows[0, 0], recv_rows[0, 0]
    size, count = guess.shape
    slots = send.shape[1]
    cpd = cdiag.shape[0]
    subs, grps = lax.axis_size("sub"), lax.axis_size("grp")
    devices = subs * grps
    cdiag = cdiag[None, :]
    moves = [pairing(subs, grps, side) for side in (0, 1)]

    def exchange(odd, even):
        return lax.ppermute(odd, AXES, moves[0]), lax.ppermute(even, AXES, moves[1])

    def everyone(rows):
        return lax.all_to_all(rows, AXES, 0, 0, tiled=True)

    field = ((size, count), f32)
    near = ((size, slots), f32)
    rows_out = ((devices, LANES), f32)
    small = ((8, LANES), f32)
    items = (guess, agg, send, recv, valve)
    odd, even, notes = call(
        first_send, [near, near, ((8, LANES), jnp.int32)], *items, hbm=range(5), limit=16,
        scratch=[pltpu.VMEM(item.shape, item.dtype) for item in items]
        + [pltpu.SemaphoreType.DMA((5,))],
    )
    odd_guess, even_guess = exchange(odd, even)
    packed = ((cpd * (coff.shape[1] // LANES) + 4 * size + 16, LANES), bf16)
    items = (guess, rhs, coff, prolong, cdiag)
    local, arrive, gather, odd, even, blocks = call(
        prepare,
        [field, ((2 * slots, count), bf16), ((count, LANES), bf16), packed, packed,
         (blocks.shape, bf16)],
        live, guess, rhs, blocks, coff, prolong, cdiag, notes, hbm=range(7),
        scratch=[pltpu.SMEM(live.shape, live.dtype)]
        + [pltpu.VMEM(item.shape, item.dtype) for item in items]
        + [pltpu.SemaphoreType.DMA((10,))],
    )
    first, rows, odd, even = call(
        lambda *refs: residual(*refs[:10], cpd, *refs[10:]), [field, rows_out, packed, packed],
        local, odd_guess, even_guess, arrive, gather, prolong, jscale, notes, odd, even,
        aliases={8: 2, 9: 3},
    )
    even_pack = lax.ppermute(even, AXES, moves[1])
    odd_pack = lax.ppermute(odd, AXES, moves[0])
    own_pack = odd
    first_got = everyone(rows)
    (basis, direction, image, rows, odd, even, matrix, odd_weights, even_weights, odd_first,
     even_first, info) = call(
        lambda *refs: first_step(*refs[:11], grps, cpd, *refs[11:]),
        [field, field, field, rows_out, near, near,
         ((3 * SLOT, coff.shape[1]), bf16)] + [near] * 4 + [small],
        first_got, own_pack, even_pack, odd_pack, first, jscale, prolong, blocks, notes, arrive,
        gather,
    )
    odd_near, even_near = exchange(odd, even)
    got = everyone(rows)
    basis_two, direction_two, image_two, scalars, rows = call(
        lambda *refs: second_step(*refs[:17], grps, cpd, *refs[17:]),
        [field, field, field, ((8, LANES), f32), rows_out],
        got, first_got, even_near, odd_near, odd_first, even_first, odd_weights, even_weights, matrix,
        info, basis, image, jscale, prolong, blocks, notes, arrive,
    )
    got = everyone(rows)
    solution, next_basis = call(
        finish, [field, field],
        got, scalars, guess, basis, basis_two, direction, direction_two, image_two, final=True,
    )
    return solution[None, None], next_basis[None, None]


def solution(mesh):
    return jax.shard_map(
        on_device,
        mesh=mesh,
        in_specs=(
            P("sub", "grp", None, None),
            P("sub", "grp", None, None),
            P("sub", "grp", None, None, None),
            P("sub", "grp", None),
            P("sub", "grp", None, None),
            P("sub", "grp", None, None),
            P("sub", "grp", None),
            P(("sub", "grp")),
            P(("sub", "grp"), None),
            P("sub", "grp", None, None),
            P("sub", "grp", None, None),
            P("sub", "grp", None),
        ),
        out_specs=(P("sub", "grp", None, None), P("sub", "grp", None, None)),
        check_vma=False,
    )
```

```python
import math

import jax
import jax.numpy as jnp
from jax import lax
from jax.experimental import pallas as pl
from jax.experimental.pallas import tpu as pltpu
from jax.sharding import PartitionSpec as P

penalty_gain = 3.0
coupling = 0.5

LANES = 128
SLOT = 64
AXES = ("sub", "grp")
f32 = jnp.float32
bf16 = jnp.bfloat16

SEND, RECV, AGG, VALVE = slice(0, 2), slice(2, 4), slice(4, 5), slice(5, 6)


def call(body, outs, *args, smem=(), hbm=(), scratch=(), limit=32, final=False, aliases=None):
    def spec(at):
        if at in hbm:
            return pl.BlockSpec(memory_space=pltpu.HBM)
        return pl.BlockSpec(memory_space=pltpu.SMEM if at in smem else pltpu.VMEM)

    args = [
        pltpu.with_memory_space_constraint(arg, pltpu.HBM) if at in hbm else arg
        for at, arg in enumerate(args)
    ]
    return pl.pallas_call(
        body,
        out_shape=[
            jax.ShapeDtypeStruct(shape, kind) if final else pltpu.VMEM(shape, kind)
            for shape, kind in outs
        ],
        in_specs=[spec(at) for at in range(len(args))],
        out_specs=[pl.BlockSpec(memory_space=pltpu.VMEM)] * len(outs),
        scratch_shapes=list(scratch),
        input_output_aliases=aliases or {},
        compiler_params=pltpu.CompilerParams(vmem_limit_bytes=limit * 1024 * 1024),
    )(*args)


def partner(place, side):
    return place - 1 + 2 * ((place + side) % 2)


def pairing(subs, grps, side):
    moves = []
    for place in range(subs):
        other = partner(place, side)
        for group in range(grps):
            if 0 <= other < subs:
                target = other * grps + group
            else:
                target = place * grps + (group ^ 1 if group ^ 1 < grps else group)
            moves.append((place * grps + group, target))
    return moves


def row_of(ref, flipped):
    return jnp.where(flipped == 0, ref[0:1, :], ref[1:2, :])


def parity(side):
    return (lax.axis_index("sub") + side + 1) % 2


def along_lanes(field, places):
    return jnp.take_along_axis(field, places, axis=1, mode="promise_in_bounds")


def pick(field, places):
    return along_lanes(field, jnp.broadcast_to(places, field.shape))


def pieces(field, count=2):
    result = []
    for _ in range(count):
        result.append(field.astype(bf16))
        field = field - result[-1].astype(f32)
    return result


def block_rows(blocks, field):
    return jnp.sum(blocks.astype(f32) * field[None], axis=1)


def local_product(blocks_ref, valve, field):
    rows = [block_rows(blocks_ref[at : at + 8], field) for at in range(0, blocks_ref.shape[0], 8)]
    return jnp.concatenate(rows, axis=0) + penalty_gain * valve.astype(f32) * field


def received(near, arrive_ref, count=2):
    parts = pieces(jnp.concatenate(near, axis=1), count)
    sums = jnp.dot(jnp.concatenate(parts, axis=0), arrive_ref[...], preferred_element_type=f32)
    size = near[0].shape[0]
    result = sums[:size]
    for at in range(size, count * size, size):
        result = result + sums[at : at + size]
    return result


def restricted(weighted, gather_ref):
    high = weighted.astype(bf16).astype(f32)
    rest = weighted - high
    middle = rest.astype(bf16).astype(f32)
    last = rest - middle
    row = lax.broadcasted_iota(jnp.int32, (8, weighted.shape[1]), 0)
    stack = jnp.where(row == 0, high, jnp.where(row == 1, middle, jnp.where(row == 2, last, 0.0)))
    sums = jnp.dot(stack.astype(bf16), gather_ref[...], preferred_element_type=f32)
    return jnp.sum(sums, axis=0, keepdims=True)


def total(field):
    return jnp.sum(jnp.sum(field, axis=0, keepdims=True), axis=1, keepdims=True)


def to_all(ref, row, first_lane, totals):
    lane = lax.broadcasted_iota(jnp.int32, (1, LANES), 1)
    for at, value in enumerate(totals):
        row = jnp.where(lane == first_lane + at, value, row)
    ref[...] = jnp.broadcast_to(row, ref.shape)


def summed(ref, first_lane, count):
    rows = jnp.broadcast_to(jnp.sum(ref[...], axis=0, keepdims=True), (8, LANES))
    return [
        along_lanes(rows, jnp.full((8, LANES), first_lane + at, jnp.int32))[0:1]
        for at in range(count)
    ]


def copy_all(pairs, sems):
    copies = [pltpu.make_async_copy(*pair, sems.at[at]) for at, pair in enumerate(pairs)]
    for copy in copies:
        copy.start()
    return copies


def first_send(guess_hbm, agg_hbm, send_hbm, recv_hbm, valve_hbm, odd_ref, even_ref, notes_ref,
               guess_ref, agg_ref, send_ref, recv_ref, valve_ref, sems):
    pairs = (
        (send_hbm, send_ref), (guess_hbm, guess_ref), (agg_hbm, agg_ref), (recv_hbm, recv_ref),
        (valve_hbm, valve_ref),
    )
    for copy in copy_all(pairs, sems):
        copy.wait()
    for side, ref in enumerate((odd_ref, even_ref)):
        ref[...] = pick(guess_ref[...], row_of(send_ref, parity(side)))
    notes_ref[...] = jnp.concatenate(
        [send_ref[...], recv_ref[...], agg_ref[...], valve_ref[...], jnp.zeros((2, LANES), jnp.int32)],
        axis=0,
    )


def wide(row):
    return jnp.concatenate([row, jnp.zeros((1, LANES - row.shape[1]), row.dtype)], axis=1)


def pack_constants(ref, coff_ref, prolong, agg, cdiag, places):
    cpd, width = coff_ref.shape
    for at in range(0, width, LANES):
        start = at // LANES * cpd
        ref[start : start + cpd, :] = coff_ref[:, at : at + LANES]
    base = cpd * (width // LANES)
    high, low = pieces(pick(prolong, places))
    size = high.shape[0]
    ref[base : base + size, :] = high
    ref[base + size : base + 2 * size, :] = low
    listed = pick(jnp.broadcast_to(agg.astype(f32), (8, LANES)), places)[0:1]
    one = cdiag.astype(bf16).astype(f32)
    two = (cdiag - one).astype(bf16).astype(f32)
    rows = [listed, one, two, cdiag - one - two, jnp.zeros((12, LANES), f32)]
    ref[base + 2 * size : base + 2 * size + 16, :] = jnp.concatenate(rows, axis=0).astype(bf16)


def prepare(live_hbm, guess_hbm, rhs_hbm, blocks_hbm, coff_hbm, prolong_hbm, cdiag_hbm, notes_ref,
            local_ref, arrive_ref, gather_ref, odd_ref, even_ref, blocks_ref,
            live_ref, guess_ref, rhs_ref, coff_ref, prolong_ref, cdiag_ref, sems):
    size = guess_ref.shape[0]
    chunk = size // 4
    pairs = [(coff_hbm, coff_ref), (prolong_hbm, prolong_ref), (cdiag_hbm, cdiag_ref),
             (live_hbm, live_ref), (guess_hbm, guess_ref)]
    for at in range(0, size, chunk):
        pairs.append((blocks_hbm.at[at : at + chunk], blocks_ref.at[at : at + chunk]))
    copies = copy_all(pairs + [(rhs_hbm, rhs_ref)], sems)
    for copy in copies[:4]:
        copy.wait()
    cdiag = wide(cdiag_ref[...])
    for side, ref in enumerate((odd_ref, even_ref)):
        places = row_of(notes_ref.at[SEND], parity(side))
        pack_constants(ref, coff_ref, prolong_ref[...], notes_ref[AGG], cdiag, places)
    count = arrive_ref.shape[1]
    slots = notes_ref.shape[1]
    coarse = lax.broadcasted_iota(jnp.int32, (LANES, count), 0)
    gather_ref[...] = jnp.where(notes_ref[AGG] == coarse, 1.0, 0.0).T.astype(bf16)
    place = lax.axis_index("sub")
    row = lax.broadcasted_iota(jnp.int32, (count, slots), 0)
    slot = lax.broadcasted_iota(jnp.int32, (count, slots), 1)
    for side in (0, 1):
        other = place + 1 - 2 * parity(side)
        there = (other >= 0) & (other < lax.axis_size("sub"))
        which = 1 - parity(side)
        live = jnp.where(there, live_ref[0, which], 0)
        hit = (row_of(notes_ref.at[RECV], which) == row) & (slot < live)
        arrive_ref[side * slots : (side + 1) * slots, :] = jnp.where(hit, 1.0, 0.0).T.astype(bf16)
    copies[4].wait()
    guess = guess_ref[...]
    penalty = penalty_gain * notes_ref[VALVE].astype(f32)
    for at in range(0, size, 8):
        if at % chunk == 0:
            copies[5 + at // chunk].wait()
        part = slice(at, at + 8)
        local_ref[part, :] = block_rows(blocks_ref[part], guess) + penalty * guess[part]
    copies[-1].wait()
    local_ref[...] = rhs_ref[...] - local_ref[...]


def residual(local_ref, odd_near_ref, even_near_ref, arrive_ref, gather_ref, prolong_ref,
             jscale_ref, notes_ref, odd_pack_ref, even_pack_ref, cpd, first_ref, out_ref, odd_ref,
             even_ref):
    near = [odd_near_ref[...], even_near_ref[...]]
    first = local_ref[...] + coupling * received(near, arrive_ref, 3)
    first_ref[...] = first
    weighted = jnp.sum(prolong_ref[...] * first, axis=0, keepdims=True)
    to_all(out_ref, restricted(weighted, gather_ref), cpd, [total(first * first)])
    scaled = jscale_ref[...] * first
    size = first.shape[0]
    tail = odd_ref.shape[0] - 2 * size
    for side, ref in enumerate((odd_ref, even_ref)):
        high, low = pieces(pick(scaled, row_of(notes_ref.at[SEND], parity(side))))
        ref[tail : tail + size, :] = high
        ref[tail + size :, :] = low


def unpack(own_ref, even_ref, odd_ref, cpd, matrix_ref, odd_weights_ref, even_weights_ref,
           odd_first_ref, even_first_ref, info_ref):
    width = matrix_ref.shape[1]
    size = odd_first_ref.shape[0]
    base = cpd * (width // LANES)
    rows = []
    for slot, ref in enumerate((own_ref, odd_ref, even_ref)):
        for at in range(0, width, LANES):
            start = at // LANES * cpd
            matrix_ref[slot * SLOT : slot * SLOT + cpd, at : at + LANES] = ref[start : start + cpd, :]
        matrix_ref[slot * SLOT + cpd : (slot + 1) * SLOT, :] = jnp.zeros((SLOT - cpd, width), bf16)
        rows.append(ref[base + 2 * size : base + 2 * size + 16, :].astype(f32))
    for ref, weights_ref, near_ref in (
        (odd_ref, odd_weights_ref, odd_first_ref), (even_ref, even_weights_ref, even_first_ref)
    ):
        for start, to_ref in ((base, weights_ref), (base + 2 * size + 16, near_ref)):
            high, low = ref[start : start + size, :], ref[start + size : start + 2 * size, :]
            to_ref[...] = high.astype(f32) + low.astype(f32)
    infos = [row[1:2] + row[2:3] + row[3:4] for row in rows] + [row[0:1] for row in rows[1:]]
    info_ref[...] = jnp.concatenate(infos + [jnp.zeros((3, LANES), f32)], axis=0)


def solve_coarse(parts, matrix_ref, near_rows, cdiags, cpd):
    group = parts[0].shape[0]
    shape = (group, LANES)
    row = lax.broadcasted_iota(jnp.int32, shape, 0)
    lane = lax.broadcasted_iota(jnp.int32, shape, 1)
    masks = [(at + lane) // cpd == row for at in range(0, group * cpd, LANES)]
    source = lax.rem(lane - cpd * row + cpd * group, LANES)
    tiles = []
    for part in parts:
        shifted = along_lanes(part, source)
        tiles.extend(jnp.where(mask, shifted, 0.0) for mask in masks)
    product = lax.dot_general(
        jnp.concatenate(tiles, axis=1).astype(bf16), matrix_ref[...], (((1,), (1,)), ((), ())),
        preferred_element_type=f32,
    )
    product = jnp.sum(product, axis=0, keepdims=True)
    low = product[:, :LANES]
    high = jnp.concatenate([product[:, LANES:], jnp.zeros((1, LANES - SLOT), f32)], axis=1)
    turned = pltpu.roll(jnp.broadcast_to(low, (8, LANES)), LANES - SLOT, 1)[0:1]
    shares = (low, turned, high)
    return [cdiag * row + share for cdiag, row, share in zip(cdiags, near_rows, shares)]


def parts_of(ref, cpd):
    group = math.lcm(cpd, LANES) // cpd
    rows = ref[...]
    return [rows[at : at + group, :] for at in range(0, rows.shape[0], group)]


def rows_near(parts, grp_size):
    group = parts[0].shape[0]
    count = group * len(parts)
    me = lax.axis_index("sub") * grp_size + lax.axis_index("grp")
    place = lax.broadcasted_iota(jnp.int32, parts[0].shape, 0)
    rows = []
    for shift in [0] + [grp_size * (1 - 2 * parity(side)) for side in (0, 1)]:
        wanted = lax.rem(me + shift + count, count)
        found = jnp.where(place == wanted, parts[0], 0.0)
        for at, part in enumerate(parts[1:], 1):
            found = jnp.where(place + at * group == wanted, part, found)
        rows.append(jnp.sum(found, axis=0, keepdims=True))
    return rows


def spread_of(solution, agg):
    wide = jnp.broadcast_to(solution, (8, LANES))
    return along_lanes(wide, jnp.broadcast_to(agg, (8, LANES)))[0:1]


def near_spread(weights_ref, info_ref, side, solution):
    agg = info_ref[3 + side : 4 + side, :].astype(jnp.int32)
    return weights_ref[...] * spread_of(solution, agg)


def first_step(got_ref, own_pack_ref, even_pack_ref, odd_pack_ref, first_ref, jscale_ref,
               prolong_ref, blocks_ref, notes_ref, arrive_ref, gather_ref, grp_size, cpd,
               basis_ref, direction_ref, image_ref, out_ref, odd_ref, even_ref, matrix_ref,
               odd_weights_ref, even_weights_ref, odd_near_ref, even_near_ref, info_ref):
    unpack(own_pack_ref, even_pack_ref, odd_pack_ref, cpd, matrix_ref, odd_weights_ref,
           even_weights_ref, odd_near_ref, even_near_ref, info_ref)
    inverse = 1.0 / jnp.sqrt(summed(got_ref, cpd, 1)[0])
    parts = [part * inverse for part in parts_of(got_ref, cpd)]
    cdiags = [info_ref[at : at + 1, :] for at in range(3)]
    solved = solve_coarse(parts, matrix_ref, rows_near(parts, grp_size), cdiags, cpd)
    basis = first_ref[...] * inverse
    basis_ref[...] = basis
    spread = spread_of(solved[0], notes_ref[AGG])
    jscale, prolong = jscale_ref[...], prolong_ref[...]
    direction = jscale * basis + prolong * spread
    direction_ref[...] = direction
    near = [
        odd_near_ref[...] * inverse + near_spread(odd_weights_ref, info_ref, 0, solved[1]),
        even_near_ref[...] * inverse + near_spread(even_weights_ref, info_ref, 1, solved[2]),
    ]
    image = local_product(blocks_ref, notes_ref[VALVE], direction)
    image = image - coupling * received(near, arrive_ref)
    image_ref[...] = image
    weighted = jnp.sum(prolong * image, axis=0, keepdims=True)
    dots = [total(basis * image), total(image * image)]
    to_all(out_ref, restricted(weighted, gather_ref), cpd, dots)
    scaled = jscale * image
    for side, ref in enumerate((odd_ref, even_ref)):
        ref[...] = pick(scaled, row_of(notes_ref.at[SEND], parity(side)))


def second_step(got_ref, first_got_ref, even_near_ref, odd_near_ref, odd_first_ref, even_first_ref,
                odd_weights_ref, even_weights_ref, matrix_ref, info_ref, basis_ref, image_ref,
                jscale_ref, prolong_ref, blocks_ref, notes_ref, arrive_ref,
                grp_size, cpd, basis_two_ref, direction_ref, image_two_ref, scalars_ref, out_ref):
    beta = jnp.sqrt(summed(first_got_ref, cpd, 1)[0])
    along, energy = summed(got_ref, cpd, 2)
    height = jnp.sqrt(jnp.maximum(energy - along * along, 0.01 * energy))
    inverse = 1.0 / height
    slope = along / beta

    def mixed(new, old):
        return (new - slope * old) * inverse

    parts = [
        mixed(new, old) for new, old in zip(parts_of(got_ref, cpd), parts_of(first_got_ref, cpd))
    ]
    cdiags = [info_ref[at : at + 1, :] for at in range(3)]
    solved = solve_coarse(parts, matrix_ref, rows_near(parts, grp_size), cdiags, cpd)
    basis = (image_ref[...] - along * basis_ref[...]) * inverse
    basis_two_ref[...] = basis
    spread = spread_of(solved[0], notes_ref[AGG])
    direction = jscale_ref[...] * basis + prolong_ref[...] * spread
    direction_ref[...] = direction
    near = [
        mixed(odd_near_ref[...], odd_first_ref[...])
        + near_spread(odd_weights_ref, info_ref, 0, solved[1]),
        mixed(even_near_ref[...], even_first_ref[...])
        + near_spread(even_weights_ref, info_ref, 1, solved[2]),
    ]
    image = local_product(blocks_ref, notes_ref[VALVE], direction)
    image = image - coupling * received(near, arrive_ref)
    image_two_ref[...] = image
    scalars_ref[...] = jnp.concatenate([beta, along, height, jnp.zeros((5, LANES), f32)], axis=0)
    dots = [total(basis_ref[...] * image), total(basis * image), total(image * image)]
    to_all(out_ref, jnp.zeros((1, LANES), f32), 0, dots)


def finish(got_ref, scalars_ref, guess_ref, basis_ref, basis_two_ref, direction_ref,
           direction_two_ref, image_ref, solution_ref, next_ref):
    beta, h11, h21 = scalars_ref[0:1, :], scalars_ref[1:2, :], scalars_ref[2:3, :]
    h12, h22, energy = summed(got_ref, 0, 3)
    h32 = jnp.sqrt(jnp.maximum(energy - (h12 * h12 + h22 * h22), 0.01 * energy))
    g00 = h11 * h11 + h21 * h21
    g01 = h11 * h12 + h21 * h22
    g11 = h12 * h12 + h22 * h22 + h32 * h32
    t0, t1 = beta * h11, beta * h12
    factor = g01 / g00
    c1 = (t1 - factor * t0) / (g11 - factor * g01)
    c0 = (t0 - g01 * c1) / g00
    solution_ref[...] = guess_ref[...] + c0 * direction_ref[...] + c1 * direction_two_ref[...]
    next_ref[...] = (image_ref[...] - h12 * basis_ref[...] - h22 * basis_two_ref[...]) * (1.0 / h32)


def on_device(rhs, guess, blocks, valve, jscale, prolong, agg_map, cdiag, coff, send_rows,
              recv_rows, live_counts):
    rhs, guess, blocks, jscale, prolong = rhs[0, 0], guess[0, 0], blocks[0, 0], jscale[0, 0], prolong[0, 0]
    valve, agg, live = valve[0], agg_map[0], live_counts[0]
    send, recv = send_rows[0, 0], recv_rows[0, 0]
    size, count = guess.shape
    slots = send.shape[1]
    cpd = cdiag.shape[0]
    subs, grps = lax.axis_size("sub"), lax.axis_size("grp")
    devices = subs * grps
    cdiag = cdiag[None, :]
    moves = [pairing(subs, grps, side) for side in (0, 1)]

    def exchange(odd, even):
        return lax.ppermute(odd, AXES, moves[0]), lax.ppermute(even, AXES, moves[1])

    def everyone(rows):
        return lax.all_to_all(rows, AXES, 0, 0, tiled=True)

    field = ((size, count), f32)
    near = ((size, slots), f32)
    rows_out = ((devices, LANES), f32)
    small = ((8, LANES), f32)
    items = (guess, agg, send, recv, valve)
    odd, even, notes = call(
        first_send, [near, near, ((8, LANES), jnp.int32)], *items, hbm=range(5), limit=16,
        scratch=[pltpu.VMEM(item.shape, item.dtype) for item in items]
        + [pltpu.SemaphoreType.DMA((5,))],
    )
    odd_guess, even_guess = exchange(odd, even)
    packed = ((cpd * (coff.shape[1] // LANES) + 4 * size + 16, LANES), bf16)
    items = (guess, rhs, coff, prolong, cdiag)
    local, arrive, gather, odd, even, blocks = call(
        prepare,
        [field, ((2 * slots, count), bf16), ((count, LANES), bf16), packed, packed,
         (blocks.shape, bf16)],
        live, guess, rhs, blocks, coff, prolong, cdiag, notes, hbm=range(7),
        scratch=[pltpu.SMEM(live.shape, live.dtype)]
        + [pltpu.VMEM(item.shape, item.dtype) for item in items]
        + [pltpu.SemaphoreType.DMA((10,))],
    )
    first, rows, odd, even = call(
        lambda *refs: residual(*refs[:10], cpd, *refs[10:]), [field, rows_out, packed, packed],
        local, odd_guess, even_guess, arrive, gather, prolong, jscale, notes, odd, even,
        aliases={8: 2, 9: 3},
    )
    even_pack = lax.ppermute(even, AXES, moves[1])
    odd_pack = lax.ppermute(odd, AXES, moves[0])
    own_pack = odd
    first_got = everyone(rows)
    (basis, direction, image, rows, odd, even, matrix, odd_weights, even_weights, odd_first,
     even_first, info) = call(
        lambda *refs: first_step(*refs[:11], grps, cpd, *refs[11:]),
        [field, field, field, rows_out, near, near,
         ((3 * SLOT, coff.shape[1]), bf16)] + [near] * 4 + [small],
        first_got, own_pack, even_pack, odd_pack, first, jscale, prolong, blocks, notes, arrive,
        gather,
    )
    odd_near, even_near = exchange(odd, even)
    got = everyone(rows)
    basis_two, direction_two, image_two, scalars, rows = call(
        lambda *refs: second_step(*refs[:17], grps, cpd, *refs[17:]),
        [field, field, field, ((8, LANES), f32), rows_out],
        got, first_got, even_near, odd_near, odd_first, even_first, odd_weights, even_weights, matrix,
        info, basis, image, jscale, prolong, blocks, notes, arrive,
    )
    got = everyone(rows)
    solution, next_basis = call(
        finish, [field, field],
        got, scalars, guess, basis, basis_two, direction, direction_two, image_two, final=True,
    )
    return solution[None, None], next_basis[None, None]


def solution(mesh):
    return jax.shard_map(
        on_device,
        mesh=mesh,
        in_specs=(
            P("sub", "grp", None, None),
            P("sub", "grp", None, None),
            P("sub", "grp", None, None, None),
            P("sub", "grp", None),
            P("sub", "grp", None, None),
            P("sub", "grp", None, None),
            P("sub", "grp", None),
            P(("sub", "grp")),
            P(("sub", "grp"), None),
            P("sub", "grp", None, None),
            P("sub", "grp", None, None),
            P("sub", "grp", None),
        ),
        out_specs=(P("sub", "grp", None, None), P("sub", "grp", None, None)),
        check_vma=False,
    )
```

```python
import math

import jax
import jax.numpy as jnp
from jax import lax
from jax.experimental import pallas as pl
from jax.experimental.pallas import tpu as pltpu
from jax.sharding import PartitionSpec as P

penalty_gain = 3.0
coupling = 0.5

LANES = 128
SLOT = 64
AXES = ("sub", "grp")
f32 = jnp.float32
bf16 = jnp.bfloat16

SEND, RECV, AGG, VALVE = slice(0, 2), slice(2, 4), slice(4, 5), slice(5, 6)


def call(body, outs, *args, smem=(), hbm=(), scratch=(), limit=32, final=False, aliases=None):
    def spec(at):
        if at in hbm:
            return pl.BlockSpec(memory_space=pltpu.HBM)
        return pl.BlockSpec(memory_space=pltpu.SMEM if at in smem else pltpu.VMEM)

    args = [
        pltpu.with_memory_space_constraint(arg, pltpu.HBM) if at in hbm else arg
        for at, arg in enumerate(args)
    ]
    return pl.pallas_call(
        body,
        out_shape=[
            jax.ShapeDtypeStruct(shape, kind) if final else pltpu.VMEM(shape, kind)
            for shape, kind in outs
        ],
        in_specs=[spec(at) for at in range(len(args))],
        out_specs=[pl.BlockSpec(memory_space=pltpu.VMEM)] * len(outs),
        scratch_shapes=list(scratch),
        input_output_aliases=aliases or {},
        compiler_params=pltpu.CompilerParams(vmem_limit_bytes=limit * 1024 * 1024),
    )(*args)


def partner(place, side):
    return place - 1 + 2 * ((place + side) % 2)


def pairing(subs, grps, side):
    moves = []
    for place in range(subs):
        other = partner(place, side)
        for group in range(grps):
            if 0 <= other < subs:
                target = other * grps + group
            else:
                target = place * grps + (group ^ 1 if group ^ 1 < grps else group)
            moves.append((place * grps + group, target))
    return moves


def row_of(ref, flipped):
    return jnp.where(flipped == 0, ref[0:1, :], ref[1:2, :])


def parity(side):
    return (lax.axis_index("sub") + side + 1) % 2


def along_lanes(field, places):
    return jnp.take_along_axis(field, places, axis=1, mode="promise_in_bounds")


def pick(field, places):
    return along_lanes(field, jnp.broadcast_to(places, field.shape))


def pieces(field, count=2):
    result = []
    for _ in range(count):
        result.append(field.astype(bf16))
        field = field - result[-1].astype(f32)
    return result


def block_rows(blocks, field):
    return jnp.sum(blocks.astype(f32) * field[None], axis=1)


def local_product(blocks_ref, valve, field):
    rows = [block_rows(blocks_ref[at : at + 8], field) for at in range(0, blocks_ref.shape[0], 8)]
    return jnp.concatenate(rows, axis=0) + penalty_gain * valve.astype(f32) * field


def received(near, arrive_ref, count=2):
    parts = pieces(jnp.concatenate(near, axis=1), count)
    sums = jnp.dot(jnp.concatenate(parts, axis=0), arrive_ref[...], preferred_element_type=f32)
    size = near[0].shape[0]
    result = sums[:size]
    for at in range(size, count * size, size):
        result = result + sums[at : at + size]
    return result


def restricted(weighted, gather_ref):
    high = weighted.astype(bf16).astype(f32)
    rest = weighted - high
    middle = rest.astype(bf16).astype(f32)
    last = rest - middle
    row = lax.broadcasted_iota(jnp.int32, (8, weighted.shape[1]), 0)
    stack = jnp.where(row == 0, high, jnp.where(row == 1, middle, jnp.where(row == 2, last, 0.0)))
    sums = jnp.dot(stack.astype(bf16), gather_ref[...], preferred_element_type=f32)
    return jnp.sum(sums, axis=0, keepdims=True)


def total(field):
    return jnp.sum(jnp.sum(field, axis=0, keepdims=True), axis=1, keepdims=True)


def to_all(ref, row, first_lane, totals):
    lane = lax.broadcasted_iota(jnp.int32, (1, LANES), 1)
    for at, value in enumerate(totals):
        row = jnp.where(lane == first_lane + at, value, row)
    ref[...] = jnp.broadcast_to(row, ref.shape)


def summed(ref, first_lane, count):
    rows = jnp.broadcast_to(jnp.sum(ref[...], axis=0, keepdims=True), (8, LANES))
    return [
        along_lanes(rows, jnp.full((8, LANES), first_lane + at, jnp.int32))[0:1]
        for at in range(count)
    ]


def copy_all(pairs, sems):
    copies = [pltpu.make_async_copy(*pair, sems.at[at]) for at, pair in enumerate(pairs)]
    for copy in copies:
        copy.start()
    return copies


def first_send(guess_hbm, send_hbm, odd_ref, even_ref, guess_ref, send_ref, sems):
    for copy in copy_all(((send_hbm, send_ref), (guess_hbm, guess_ref)), sems):
        copy.wait()
    for side, ref in enumerate((odd_ref, even_ref)):
        ref[...] = pick(guess_ref[...], row_of(send_ref, parity(side)))


def wide(row):
    return jnp.concatenate([row, jnp.zeros((1, LANES - row.shape[1]), row.dtype)], axis=1)


def pack_constants(ref, coff_ref, prolong, agg, cdiag, places):
    cpd, width = coff_ref.shape
    for at in range(0, width, LANES):
        start = at // LANES * cpd
        ref[start : start + cpd, :] = coff_ref[:, at : at + LANES]
    base = cpd * (width // LANES)
    high, low = pieces(pick(prolong, places))
    size = high.shape[0]
    ref[base : base + size, :] = high
    ref[base + size : base + 2 * size, :] = low
    listed = pick(jnp.broadcast_to(agg.astype(f32), (8, LANES)), places)[0:1]
    one = cdiag.astype(bf16).astype(f32)
    two = (cdiag - one).astype(bf16).astype(f32)
    rows = [listed, one, two, cdiag - one - two, jnp.zeros((12, LANES), f32)]
    ref[base + 2 * size : base + 2 * size + 16, :] = jnp.concatenate(rows, axis=0).astype(bf16)


def prepare(agg_hbm, send_hbm, recv_hbm, valve_hbm, live_hbm, guess_hbm, rhs_hbm, blocks_hbm,
            coff_hbm, prolong_hbm, cdiag_hbm, local_ref, arrive_ref, gather_ref, odd_ref, even_ref,
            blocks_ref, notes_ref, agg_ref, send_ref, recv_ref, valve_ref, live_ref, guess_ref,
            rhs_ref, coff_ref, prolong_ref, cdiag_ref, sems):
    size = guess_ref.shape[0]
    chunk = size // 4
    pairs = [
        (agg_hbm, agg_ref), (send_hbm, send_ref), (recv_hbm, recv_ref), (valve_hbm, valve_ref),
        (coff_hbm, coff_ref), (prolong_hbm, prolong_ref), (cdiag_hbm, cdiag_ref),
        (live_hbm, live_ref), (guess_hbm, guess_ref),
    ]
    for at in range(0, size, chunk):
        pairs.append((blocks_hbm.at[at : at + chunk], blocks_ref.at[at : at + chunk]))
    copies = copy_all(pairs + [(rhs_hbm, rhs_ref)], sems)
    for copy in copies[:8]:
        copy.wait()
    notes_ref[...] = jnp.concatenate(
        [send_ref[...], recv_ref[...], agg_ref[...], valve_ref[...], jnp.zeros((2, LANES), jnp.int32)],
        axis=0,
    )
    cdiag = wide(cdiag_ref[...])
    for side, ref in enumerate((odd_ref, even_ref)):
        places = row_of(notes_ref.at[SEND], parity(side))
        pack_constants(ref, coff_ref, prolong_ref[...], notes_ref[AGG], cdiag, places)
    count = arrive_ref.shape[1]
    slots = notes_ref.shape[1]
    coarse = lax.broadcasted_iota(jnp.int32, (LANES, count), 0)
    gather_ref[...] = jnp.where(notes_ref[AGG] == coarse, 1.0, 0.0).T.astype(bf16)
    place = lax.axis_index("sub")
    row = lax.broadcasted_iota(jnp.int32, (count, slots), 0)
    slot = lax.broadcasted_iota(jnp.int32, (count, slots), 1)
    for side in (0, 1):
        other = place + 1 - 2 * parity(side)
        there = (other >= 0) & (other < lax.axis_size("sub"))
        which = 1 - parity(side)
        live = jnp.where(there, live_ref[0, which], 0)
        hit = (row_of(notes_ref.at[RECV], which) == row) & (slot < live)
        arrive_ref[side * slots : (side + 1) * slots, :] = jnp.where(hit, 1.0, 0.0).T.astype(bf16)
    copies[8].wait()
    guess = guess_ref[...]
    penalty = penalty_gain * notes_ref[VALVE].astype(f32)
    for at in range(0, size, 8):
        if at % chunk == 0:
            copies[9 + at // chunk].wait()
        part = slice(at, at + 8)
        local_ref[part, :] = block_rows(blocks_ref[part], guess) + penalty * guess[part]
    copies[-1].wait()
    local_ref[...] = rhs_ref[...] - local_ref[...]


def residual(local_ref, odd_near_ref, even_near_ref, arrive_ref, gather_ref, prolong_ref,
             jscale_ref, notes_ref, odd_pack_ref, even_pack_ref, cpd, first_ref, out_ref, odd_ref,
             even_ref):
    near = [odd_near_ref[...], even_near_ref[...]]
    first = local_ref[...] + coupling * received(near, arrive_ref, 3)
    first_ref[...] = first
    weighted = jnp.sum(prolong_ref[...] * first, axis=0, keepdims=True)
    to_all(out_ref, restricted(weighted, gather_ref), cpd, [total(first * first)])
    scaled = jscale_ref[...] * first
    size = first.shape[0]
    tail = odd_ref.shape[0] - 2 * size
    for side, ref in enumerate((odd_ref, even_ref)):
        high, low = pieces(pick(scaled, row_of(notes_ref.at[SEND], parity(side))))
        ref[tail : tail + size, :] = high
        ref[tail + size :, :] = low


def unpack(own_ref, even_ref, odd_ref, cpd, matrix_ref, odd_weights_ref, even_weights_ref,
           odd_first_ref, even_first_ref, info_ref):
    width = matrix_ref.shape[1]
    size = odd_first_ref.shape[0]
    base = cpd * (width // LANES)
    rows = []
    for slot, ref in enumerate((own_ref, odd_ref, even_ref)):
        for at in range(0, width, LANES):
            start = at // LANES * cpd
            matrix_ref[slot * SLOT : slot * SLOT + cpd, at : at + LANES] = ref[start : start + cpd, :]
        matrix_ref[slot * SLOT + cpd : (slot + 1) * SLOT, :] = jnp.zeros((SLOT - cpd, width), bf16)
        rows.append(ref[base + 2 * size : base + 2 * size + 16, :].astype(f32))
    for ref, weights_ref, near_ref in (
        (odd_ref, odd_weights_ref, odd_first_ref), (even_ref, even_weights_ref, even_first_ref)
    ):
        for start, to_ref in ((base, weights_ref), (base + 2 * size + 16, near_ref)):
            high, low = ref[start : start + size, :], ref[start + size : start + 2 * size, :]
            to_ref[...] = high.astype(f32) + low.astype(f32)
    infos = [row[1:2] + row[2:3] + row[3:4] for row in rows] + [row[0:1] for row in rows[1:]]
    info_ref[...] = jnp.concatenate(infos + [jnp.zeros((3, LANES), f32)], axis=0)


def solve_coarse(parts, matrix_ref, near_rows, cdiags, cpd):
    group = parts[0].shape[0]
    shape = (group, LANES)
    row = lax.broadcasted_iota(jnp.int32, shape, 0)
    lane = lax.broadcasted_iota(jnp.int32, shape, 1)
    masks = [(at + lane) // cpd == row for at in range(0, group * cpd, LANES)]
    source = lax.rem(lane - cpd * row + cpd * group, LANES)
    tiles = []
    for part in parts:
        shifted = along_lanes(part, source)
        tiles.extend(jnp.where(mask, shifted, 0.0) for mask in masks)
    product = lax.dot_general(
        jnp.concatenate(tiles, axis=1).astype(bf16), matrix_ref[...], (((1,), (1,)), ((), ())),
        preferred_element_type=f32,
    )
    product = jnp.sum(product, axis=0, keepdims=True)
    low = product[:, :LANES]
    high = jnp.concatenate([product[:, LANES:], jnp.zeros((1, LANES - SLOT), f32)], axis=1)
    turned = pltpu.roll(jnp.broadcast_to(low, (8, LANES)), LANES - SLOT, 1)[0:1]
    shares = (low, turned, high)
    return [cdiag * row + share for cdiag, row, share in zip(cdiags, near_rows, shares)]


def parts_of(ref, cpd):
    group = math.lcm(cpd, LANES) // cpd
    rows = ref[...]
    return [rows[at : at + group, :] for at in range(0, rows.shape[0], group)]


def rows_near(parts, grp_size):
    group = parts[0].shape[0]
    count = group * len(parts)
    me = lax.axis_index("sub") * grp_size + lax.axis_index("grp")
    place = lax.broadcasted_iota(jnp.int32, parts[0].shape, 0)
    rows = []
    for shift in [0] + [grp_size * (1 - 2 * parity(side)) for side in (0, 1)]:
        wanted = lax.rem(me + shift + count, count)
        found = jnp.where(place == wanted, parts[0], 0.0)
        for at, part in enumerate(parts[1:], 1):
            found = jnp.where(place + at * group == wanted, part, found)
        rows.append(jnp.sum(found, axis=0, keepdims=True))
    return rows


def spread_of(solution, agg):
    wide = jnp.broadcast_to(solution, (8, LANES))
    return along_lanes(wide, jnp.broadcast_to(agg, (8, LANES)))[0:1]


def near_spread(weights_ref, info_ref, side, solution):
    agg = info_ref[3 + side : 4 + side, :].astype(jnp.int32)
    return weights_ref[...] * spread_of(solution, agg)


def first_step(got_ref, own_pack_ref, even_pack_ref, odd_pack_ref, first_ref, jscale_ref,
               prolong_ref, blocks_ref, notes_ref, arrive_ref, gather_ref, grp_size, cpd,
               basis_ref, direction_ref, image_ref, out_ref, odd_ref, even_ref, matrix_ref,
               odd_weights_ref, even_weights_ref, odd_near_ref, even_near_ref, info_ref):
    unpack(own_pack_ref, even_pack_ref, odd_pack_ref, cpd, matrix_ref, odd_weights_ref,
           even_weights_ref, odd_near_ref, even_near_ref, info_ref)
    inverse = 1.0 / jnp.sqrt(summed(got_ref, cpd, 1)[0])
    parts = [part * inverse for part in parts_of(got_ref, cpd)]
    cdiags = [info_ref[at : at + 1, :] for at in range(3)]
    solved = solve_coarse(parts, matrix_ref, rows_near(parts, grp_size), cdiags, cpd)
    basis = first_ref[...] * inverse
    basis_ref[...] = basis
    spread = spread_of(solved[0], notes_ref[AGG])
    jscale, prolong = jscale_ref[...], prolong_ref[...]
    direction = jscale * basis + prolong * spread
    direction_ref[...] = direction
    near = [
        odd_near_ref[...] * inverse + near_spread(odd_weights_ref, info_ref, 0, solved[1]),
        even_near_ref[...] * inverse + near_spread(even_weights_ref, info_ref, 1, solved[2]),
    ]
    image = local_product(blocks_ref, notes_ref[VALVE], direction)
    image = image - coupling * received(near, arrive_ref)
    image_ref[...] = image
    weighted = jnp.sum(prolong * image, axis=0, keepdims=True)
    dots = [total(basis * image), total(image * image)]
    to_all(out_ref, restricted(weighted, gather_ref), cpd, dots)
    scaled = jscale * image
    for side, ref in enumerate((odd_ref, even_ref)):
        ref[...] = pick(scaled, row_of(notes_ref.at[SEND], parity(side)))


def second_step(got_ref, first_got_ref, even_near_ref, odd_near_ref, odd_first_ref, even_first_ref,
                odd_weights_ref, even_weights_ref, matrix_ref, info_ref, basis_ref, image_ref,
                jscale_ref, prolong_ref, blocks_ref, notes_ref, arrive_ref,
                grp_size, cpd, basis_two_ref, direction_ref, image_two_ref, scalars_ref, out_ref):
    beta = jnp.sqrt(summed(first_got_ref, cpd, 1)[0])
    along, energy = summed(got_ref, cpd, 2)
    height = jnp.sqrt(jnp.maximum(energy - along * along, 0.01 * energy))
    inverse = 1.0 / height
    slope = along / beta

    def mixed(new, old):
        return (new - slope * old) * inverse

    parts = [
        mixed(new, old) for new, old in zip(parts_of(got_ref, cpd), parts_of(first_got_ref, cpd))
    ]
    cdiags = [info_ref[at : at + 1, :] for at in range(3)]
    solved = solve_coarse(parts, matrix_ref, rows_near(parts, grp_size), cdiags, cpd)
    basis = (image_ref[...] - along * basis_ref[...]) * inverse
    basis_two_ref[...] = basis
    spread = spread_of(solved[0], notes_ref[AGG])
    direction = jscale_ref[...] * basis + prolong_ref[...] * spread
    direction_ref[...] = direction
    near = [
        mixed(odd_near_ref[...], odd_first_ref[...])
        + near_spread(odd_weights_ref, info_ref, 0, solved[1]),
        mixed(even_near_ref[...], even_first_ref[...])
        + near_spread(even_weights_ref, info_ref, 1, solved[2]),
    ]
    image = local_product(blocks_ref, notes_ref[VALVE], direction)
    image = image - coupling * received(near, arrive_ref)
    image_two_ref[...] = image
    scalars_ref[...] = jnp.concatenate([beta, along, height, jnp.zeros((5, LANES), f32)], axis=0)
    dots = [total(basis_ref[...] * image), total(basis * image), total(image * image)]
    to_all(out_ref, jnp.zeros((1, LANES), f32), 0, dots)


def finish(got_ref, scalars_ref, guess_ref, basis_ref, basis_two_ref, direction_ref,
           direction_two_ref, image_ref, solution_ref, next_ref):
    beta, h11, h21 = scalars_ref[0:1, :], scalars_ref[1:2, :], scalars_ref[2:3, :]
    h12, h22, energy = summed(got_ref, 0, 3)
    h32 = jnp.sqrt(jnp.maximum(energy - (h12 * h12 + h22 * h22), 0.01 * energy))
    g00 = h11 * h11 + h21 * h21
    g01 = h11 * h12 + h21 * h22
    g11 = h12 * h12 + h22 * h22 + h32 * h32
    t0, t1 = beta * h11, beta * h12
    factor = g01 / g00
    c1 = (t1 - factor * t0) / (g11 - factor * g01)
    c0 = (t0 - g01 * c1) / g00
    solution_ref[...] = guess_ref[...] + c0 * direction_ref[...] + c1 * direction_two_ref[...]
    next_ref[...] = (image_ref[...] - h12 * basis_ref[...] - h22 * basis_two_ref[...]) * (1.0 / h32)


def on_device(rhs, guess, blocks, valve, jscale, prolong, agg_map, cdiag, coff, send_rows,
              recv_rows, live_counts):
    rhs, guess, blocks, jscale, prolong = rhs[0, 0], guess[0, 0], blocks[0, 0], jscale[0, 0], prolong[0, 0]
    valve, agg, live = valve[0], agg_map[0], live_counts[0]
    send, recv = send_rows[0, 0], recv_rows[0, 0]
    size, count = guess.shape
    slots = send.shape[1]
    cpd = cdiag.shape[0]
    subs, grps = lax.axis_size("sub"), lax.axis_size("grp")
    devices = subs * grps
    cdiag = cdiag[None, :]
    moves = [pairing(subs, grps, side) for side in (0, 1)]

    def exchange(odd, even):
        return lax.ppermute(odd, AXES, moves[0]), lax.ppermute(even, AXES, moves[1])

    def everyone(rows):
        return lax.all_to_all(rows, AXES, 0, 0, tiled=True)

    field = ((size, count), f32)
    near = ((size, slots), f32)
    rows_out = ((devices, LANES), f32)
    small = ((8, LANES), f32)
    items = (guess, send)
    odd, even = call(
        first_send, [near, near], *items, hbm=range(2), limit=16,
        scratch=[pltpu.VMEM(item.shape, item.dtype) for item in items]
        + [pltpu.SemaphoreType.DMA((2,))],
    )
    odd_guess, even_guess = exchange(odd, even)
    packed = ((cpd * (coff.shape[1] // LANES) + 4 * size + 16, LANES), bf16)
    small_items = (agg, send, recv, valve)
    items = (guess, rhs, coff, prolong, cdiag)
    local, arrive, gather, odd, even, blocks, notes = call(
        prepare,
        [field, ((2 * slots, count), bf16), ((count, LANES), bf16), packed, packed,
         (blocks.shape, bf16), ((8, LANES), jnp.int32)],
        *small_items, live, guess, rhs, blocks, coff, prolong, cdiag, hbm=range(11),
        scratch=[pltpu.VMEM(item.shape, item.dtype) for item in small_items]
        + [pltpu.SMEM(live.shape, live.dtype)]
        + [pltpu.VMEM(item.shape, item.dtype) for item in items]
        + [pltpu.SemaphoreType.DMA((14,))],
    )
    first, rows, odd, even = call(
        lambda *refs: residual(*refs[:10], cpd, *refs[10:]), [field, rows_out, packed, packed],
        local, odd_guess, even_guess, arrive, gather, prolong, jscale, notes, odd, even,
        aliases={8: 2, 9: 3},
    )
    even_pack = lax.ppermute(even, AXES, moves[1])
    odd_pack = lax.ppermute(odd, AXES, moves[0])
    own_pack = odd
    first_got = everyone(rows)
    (basis, direction, image, rows, odd, even, matrix, odd_weights, even_weights, odd_first,
     even_first, info) = call(
        lambda *refs: first_step(*refs[:11], grps, cpd, *refs[11:]),
        [field, field, field, rows_out, near, near,
         ((3 * SLOT, coff.shape[1]), bf16)] + [near] * 4 + [small],
        first_got, own_pack, even_pack, odd_pack, first, jscale, prolong, blocks, notes, arrive,
        gather,
    )
    odd_near, even_near = exchange(odd, even)
    got = everyone(rows)
    basis_two, direction_two, image_two, scalars, rows = call(
        lambda *refs: second_step(*refs[:17], grps, cpd, *refs[17:]),
        [field, field, field, ((8, LANES), f32), rows_out],
        got, first_got, even_near, odd_near, odd_first, even_first, odd_weights, even_weights, matrix,
        info, basis, image, jscale, prolong, blocks, notes, arrive,
    )
    got = everyone(rows)
    solution, next_basis = call(
        finish, [field, field],
        got, scalars, guess, basis, basis_two, direction, direction_two, image_two, final=True,
    )
    return solution[None, None], next_basis[None, None]


def solution(mesh):
    return jax.shard_map(
        on_device,
        mesh=mesh,
        in_specs=(
            P("sub", "grp", None, None),
            P("sub", "grp", None, None),
            P("sub", "grp", None, None, None),
            P("sub", "grp", None),
            P("sub", "grp", None, None),
            P("sub", "grp", None, None),
            P("sub", "grp", None),
            P(("sub", "grp")),
            P(("sub", "grp"), None),
            P("sub", "grp", None, None),
            P("sub", "grp", None, None),
            P("sub", "grp", None),
        ),
        out_specs=(P("sub", "grp", None, None), P("sub", "grp", None, None)),
        check_vma=False,
    )
```

```python
import math

import jax
import jax.numpy as jnp
from jax import lax
from jax.experimental import pallas as pl
from jax.experimental.pallas import tpu as pltpu
from jax.sharding import PartitionSpec as P

penalty_gain = 3.0
coupling = 0.5

LANES = 128
SLOT = 64
AXES = ("sub", "grp")
f32 = jnp.float32
bf16 = jnp.bfloat16

SEND, RECV, AGG, VALVE = slice(0, 2), slice(2, 4), slice(4, 5), slice(5, 6)


def call(body, outs, *args, smem=(), hbm=(), scratch=(), limit=32, final=False, aliases=None):
    def spec(at):
        if at in hbm:
            return pl.BlockSpec(memory_space=pltpu.HBM)
        return pl.BlockSpec(memory_space=pltpu.SMEM if at in smem else pltpu.VMEM)

    args = [
        pltpu.with_memory_space_constraint(arg, pltpu.HBM) if at in hbm else arg
        for at, arg in enumerate(args)
    ]
    return pl.pallas_call(
        body,
        out_shape=[
            jax.ShapeDtypeStruct(shape, kind) if final else pltpu.VMEM(shape, kind)
            for shape, kind in outs
        ],
        in_specs=[spec(at) for at in range(len(args))],
        out_specs=[pl.BlockSpec(memory_space=pltpu.VMEM)] * len(outs),
        scratch_shapes=list(scratch),
        input_output_aliases=aliases or {},
        compiler_params=pltpu.CompilerParams(vmem_limit_bytes=limit * 1024 * 1024),
    )(*args)


def partner(place, side):
    return place - 1 + 2 * ((place + side) % 2)


def pairing(subs, grps, side):
    moves = []
    for place in range(subs):
        other = partner(place, side)
        for group in range(grps):
            if 0 <= other < subs:
                target = other * grps + group
            else:
                target = place * grps + (group ^ 1 if group ^ 1 < grps else group)
            moves.append((place * grps + group, target))
    return moves


def row_of(ref, flipped):
    return jnp.where(flipped == 0, ref[0:1, :], ref[1:2, :])


def parity(side):
    return (lax.axis_index("sub") + side + 1) % 2


def along_lanes(field, places):
    return jnp.take_along_axis(field, places, axis=1, mode="promise_in_bounds")


def pick(field, places):
    return along_lanes(field, jnp.broadcast_to(places, field.shape))


def pieces(field, count=2):
    result = []
    for _ in range(count):
        result.append(field.astype(bf16))
        field = field - result[-1].astype(f32)
    return result


def block_rows(blocks, field):
    return jnp.sum(blocks.astype(f32) * field[None], axis=1)


def local_product(blocks_ref, valve, field):
    rows = [block_rows(blocks_ref[at : at + 8], field) for at in range(0, blocks_ref.shape[0], 8)]
    return jnp.concatenate(rows, axis=0) + penalty_gain * valve.astype(f32) * field


def received(near, arrive_ref, count=2):
    parts = pieces(jnp.concatenate(near, axis=1), count)
    sums = jnp.dot(jnp.concatenate(parts, axis=0), arrive_ref[...], preferred_element_type=f32)
    size = near[0].shape[0]
    result = sums[:size]
    for at in range(size, count * size, size):
        result = result + sums[at : at + size]
    return result


def restricted(weighted, gather_ref):
    high = weighted.astype(bf16).astype(f32)
    rest = weighted - high
    middle = rest.astype(bf16).astype(f32)
    last = rest - middle
    row = lax.broadcasted_iota(jnp.int32, (8, weighted.shape[1]), 0)
    stack = jnp.where(row == 0, high, jnp.where(row == 1, middle, jnp.where(row == 2, last, 0.0)))
    sums = jnp.dot(stack.astype(bf16), gather_ref[...], preferred_element_type=f32)
    return jnp.sum(sums, axis=0, keepdims=True)


def total(field):
    return jnp.sum(jnp.sum(field, axis=0, keepdims=True), axis=1, keepdims=True)


def to_all(ref, row, first_lane, totals):
    lane = lax.broadcasted_iota(jnp.int32, (1, LANES), 1)
    for at, value in enumerate(totals):
        row = jnp.where(lane == first_lane + at, value, row)
    ref[...] = jnp.broadcast_to(row, ref.shape)


def summed(ref, first_lane, count):
    rows = jnp.broadcast_to(jnp.sum(ref[...], axis=0, keepdims=True), (8, LANES))
    return [
        along_lanes(rows, jnp.full((8, LANES), first_lane + at, jnp.int32))[0:1]
        for at in range(count)
    ]


def copy_all(pairs, sems):
    copies = [pltpu.make_async_copy(*pair, sems.at[at]) for at, pair in enumerate(pairs)]
    for copy in copies:
        copy.start()
    return copies


def first_send(guess_hbm, send_hbm, odd_ref, even_ref, guess_ref, send_ref, sems):
    for copy in copy_all(((send_hbm, send_ref), (guess_hbm, guess_ref)), sems):
        copy.wait()
    for side, ref in enumerate((odd_ref, even_ref)):
        ref[...] = pick(guess_ref[...], row_of(send_ref, parity(side)))


def wide(row):
    return jnp.concatenate([row, jnp.zeros((1, LANES - row.shape[1]), row.dtype)], axis=1)


def pack_constants(ref, coff_ref, prolong, agg, cdiag, places):
    cpd, width = coff_ref.shape
    for at in range(0, width, LANES):
        start = at // LANES * cpd
        ref[start : start + cpd, :] = coff_ref[:, at : at + LANES]
    base = cpd * (width // LANES)
    high, low = pieces(pick(prolong, places))
    size = high.shape[0]
    ref[base : base + size, :] = high
    ref[base + size : base + 2 * size, :] = low
    listed = pick(jnp.broadcast_to(agg.astype(f32), (8, LANES)), places)[0:1]
    one = cdiag.astype(bf16).astype(f32)
    two = (cdiag - one).astype(bf16).astype(f32)
    rows = [listed, one, two, cdiag - one - two, jnp.zeros((12, LANES), f32)]
    ref[base + 2 * size : base + 2 * size + 16, :] = jnp.concatenate(rows, axis=0).astype(bf16)


def prepare(agg_hbm, send_hbm, recv_hbm, valve_hbm, live_hbm, guess_hbm, rhs_hbm, blocks_hbm,
            coff_hbm, prolong_hbm, cdiag_hbm, local_ref, arrive_ref, gather_ref, odd_ref, even_ref,
            blocks_ref, notes_ref, agg_ref, send_ref, recv_ref, valve_ref, live_ref, guess_ref,
            rhs_ref, coff_ref, prolong_ref, cdiag_ref, sems):
    size = guess_ref.shape[0]
    chunk = size // 4
    pairs = [
        (agg_hbm, agg_ref), (send_hbm, send_ref), (recv_hbm, recv_ref), (valve_hbm, valve_ref),
        (coff_hbm, coff_ref), (prolong_hbm, prolong_ref), (cdiag_hbm, cdiag_ref),
        (live_hbm, live_ref), (guess_hbm, guess_ref),
    ]
    for at in range(0, size, chunk):
        pairs.append((blocks_hbm.at[at : at + chunk], blocks_ref.at[at : at + chunk]))
    copies = copy_all(pairs + [(rhs_hbm, rhs_ref)], sems)
    for copy in copies[:8]:
        copy.wait()
    notes_ref[...] = jnp.concatenate(
        [send_ref[...], recv_ref[...], agg_ref[...], valve_ref[...], jnp.zeros((2, LANES), jnp.int32)],
        axis=0,
    )
    cdiag = wide(cdiag_ref[...])
    for side, ref in enumerate((odd_ref, even_ref)):
        places = row_of(notes_ref.at[SEND], parity(side))
        pack_constants(ref, coff_ref, prolong_ref[...], notes_ref[AGG], cdiag, places)
    count = arrive_ref.shape[1]
    slots = notes_ref.shape[1]
    coarse = lax.broadcasted_iota(jnp.int32, (LANES, count), 0)
    gather_ref[...] = jnp.where(notes_ref[AGG] == coarse, 1.0, 0.0).T.astype(bf16)
    place = lax.axis_index("sub")
    row = lax.broadcasted_iota(jnp.int32, (count, slots), 0)
    slot = lax.broadcasted_iota(jnp.int32, (count, slots), 1)
    for side in (0, 1):
        other = place + 1 - 2 * parity(side)
        there = (other >= 0) & (other < lax.axis_size("sub"))
        which = 1 - parity(side)
        live = jnp.where(there, live_ref[0, which], 0)
        hit = (row_of(notes_ref.at[RECV], which) == row) & (slot < live)
        arrive_ref[side * slots : (side + 1) * slots, :] = jnp.where(hit, 1.0, 0.0).T.astype(bf16)
    copies[8].wait()
    guess = guess_ref[...]
    penalty = penalty_gain * notes_ref[VALVE].astype(f32)
    for at in range(0, size, 8):
        if at % chunk == 0:
            copies[9 + at // chunk].wait()
        part = slice(at, at + 8)
        local_ref[part, :] = block_rows(blocks_ref[part], guess) + penalty * guess[part]
    copies[-1].wait()
    local_ref[...] = rhs_ref[...] - local_ref[...]


def residual(local_ref, odd_near_ref, even_near_ref, arrive_ref, gather_ref, prolong_ref,
             jscale_ref, notes_ref, odd_pack_ref, even_pack_ref, cpd, first_ref, out_ref, odd_ref,
             even_ref):
    near = [odd_near_ref[...], even_near_ref[...]]
    first = local_ref[...] + coupling * received(near, arrive_ref, 3)
    first_ref[...] = first
    weighted = jnp.sum(prolong_ref[...] * first, axis=0, keepdims=True)
    to_all(out_ref, restricted(weighted, gather_ref), cpd, [total(first * first)])
    scaled = jscale_ref[...] * first
    size = first.shape[0]
    tail = odd_ref.shape[0] - 2 * size
    for side, ref in enumerate((odd_ref, even_ref)):
        high, low = pieces(pick(scaled, row_of(notes_ref.at[SEND], parity(side))))
        ref[tail : tail + size, :] = high
        ref[tail + size :, :] = low


def unpack(own_ref, even_ref, odd_ref, cpd, matrix_ref, odd_weights_ref, even_weights_ref,
           odd_first_ref, even_first_ref, info_ref):
    width = matrix_ref.shape[1]
    size = odd_first_ref.shape[0]
    base = cpd * (width // LANES)
    rows = []
    for slot, ref in enumerate((own_ref, odd_ref, even_ref)):
        for at in range(0, width, LANES):
            start = at // LANES * cpd
            matrix_ref[slot * SLOT : slot * SLOT + cpd, at : at + LANES] = ref[start : start + cpd, :]
        matrix_ref[slot * SLOT + cpd : (slot + 1) * SLOT, :] = jnp.zeros((SLOT - cpd, width), bf16)
        rows.append(ref[base + 2 * size : base + 2 * size + 16, :].astype(f32))
    for ref, weights_ref, near_ref in (
        (odd_ref, odd_weights_ref, odd_first_ref), (even_ref, even_weights_ref, even_first_ref)
    ):
        for start, to_ref in ((base, weights_ref), (base + 2 * size + 16, near_ref)):
            high, low = ref[start : start + size, :], ref[start + size : start + 2 * size, :]
            to_ref[...] = high.astype(f32) + low.astype(f32)
    infos = [row[1:2] + row[2:3] + row[3:4] for row in rows] + [row[0:1] for row in rows[1:]]
    info_ref[...] = jnp.concatenate(infos + [jnp.zeros((3, LANES), f32)], axis=0)


def solve_coarse(parts, matrix_ref, near_rows, cdiags, cpd):
    group = parts[0].shape[0]
    shape = (group, LANES)
    row = lax.broadcasted_iota(jnp.int32, shape, 0)
    lane = lax.broadcasted_iota(jnp.int32, shape, 1)
    masks = [(at + lane) // cpd == row for at in range(0, group * cpd, LANES)]
    source = lax.rem(lane - cpd * row + cpd * group, LANES)
    tiles = []
    for part in parts:
        shifted = along_lanes(part, source)
        tiles.extend(jnp.where(mask, shifted, 0.0) for mask in masks)
    product = lax.dot_general(
        jnp.concatenate(tiles, axis=1).astype(bf16), matrix_ref[...], (((1,), (1,)), ((), ())),
        preferred_element_type=f32,
    )
    product = jnp.sum(product, axis=0, keepdims=True)
    low = product[:, :LANES]
    high = jnp.concatenate([product[:, LANES:], jnp.zeros((1, LANES - SLOT), f32)], axis=1)
    turned = pltpu.roll(jnp.broadcast_to(low, (8, LANES)), LANES - SLOT, 1)[0:1]
    shares = (low, turned, high)
    return [cdiag * row + share for cdiag, row, share in zip(cdiags, near_rows, shares)]


def solve_at_blocks(parts, matrix_ref, near_rows, cdiags, aggs, cpd):
    group = parts[0].shape[0]
    shape = (group, LANES)
    row = lax.broadcasted_iota(jnp.int32, shape, 0)
    lane = lax.broadcasted_iota(jnp.int32, shape, 1)
    masks = [(at + lane) // cpd == row for at in range(0, group * cpd, LANES)]
    source = lax.rem(lane - cpd * row + cpd * group, LANES)
    tiles = []
    for part in parts:
        shifted = along_lanes(part, source)
        for mask in masks:
            tiles.append(jnp.sum(jnp.where(mask, shifted, 0.0), axis=0, keepdims=True))
    vector = jnp.concatenate(tiles, axis=1)
    product = lax.dot_general(
        matrix_ref[...], jnp.broadcast_to(vector, (LANES, vector.shape[1])).astype(bf16),
        (((1,), (1,)), ((), ())), preferred_element_type=f32,
    )
    unknown = lax.broadcasted_iota(jnp.int32, (cpd, LANES), 0)
    spreads = []
    for slot, (cdiag, near_row, agg) in enumerate(zip(cdiags, near_rows, aggs)):
        share = jnp.where(unknown == agg, product[slot * SLOT : slot * SLOT + cpd], 0.0)
        spreads.append(spread_of(cdiag * near_row, agg) + jnp.sum(share, axis=0, keepdims=True))
    return spreads


def parts_of(ref, cpd):
    group = math.lcm(cpd, LANES) // cpd
    rows = ref[...]
    return [rows[at : at + group, :] for at in range(0, rows.shape[0], group)]


def rows_near(parts, grp_size):
    group = parts[0].shape[0]
    count = group * len(parts)
    me = lax.axis_index("sub") * grp_size + lax.axis_index("grp")
    place = lax.broadcasted_iota(jnp.int32, parts[0].shape, 0)
    rows = []
    for shift in [0] + [grp_size * (1 - 2 * parity(side)) for side in (0, 1)]:
        wanted = lax.rem(me + shift + count, count)
        found = jnp.where(place == wanted, parts[0], 0.0)
        for at, part in enumerate(parts[1:], 1):
            found = jnp.where(place + at * group == wanted, part, found)
        rows.append(jnp.sum(found, axis=0, keepdims=True))
    return rows


def spread_of(solution, agg):
    wide = jnp.broadcast_to(solution, (8, LANES))
    return along_lanes(wide, jnp.broadcast_to(agg, (8, LANES)))[0:1]


def near_spread(weights_ref, info_ref, side, solution):
    agg = info_ref[3 + side : 4 + side, :].astype(jnp.int32)
    return weights_ref[...] * spread_of(solution, agg)


def first_step(got_ref, own_pack_ref, even_pack_ref, odd_pack_ref, first_ref, jscale_ref,
               prolong_ref, blocks_ref, notes_ref, arrive_ref, gather_ref, grp_size, cpd,
               basis_ref, direction_ref, image_ref, out_ref, odd_ref, even_ref, matrix_ref,
               odd_weights_ref, even_weights_ref, odd_near_ref, even_near_ref, info_ref):
    unpack(own_pack_ref, even_pack_ref, odd_pack_ref, cpd, matrix_ref, odd_weights_ref,
           even_weights_ref, odd_near_ref, even_near_ref, info_ref)
    inverse = 1.0 / jnp.sqrt(summed(got_ref, cpd, 1)[0])
    parts = [part * inverse for part in parts_of(got_ref, cpd)]
    cdiags = [info_ref[at : at + 1, :] for at in range(3)]
    aggs = [notes_ref[AGG]] + [info_ref[at : at + 1, :].astype(jnp.int32) for at in (3, 4)]
    spreads = solve_at_blocks(parts, matrix_ref, rows_near(parts, grp_size), cdiags, aggs, cpd)
    basis = first_ref[...] * inverse
    basis_ref[...] = basis
    jscale, prolong = jscale_ref[...], prolong_ref[...]
    direction = jscale * basis + prolong * spreads[0]
    direction_ref[...] = direction
    near = [
        odd_near_ref[...] * inverse + odd_weights_ref[...] * spreads[1],
        even_near_ref[...] * inverse + even_weights_ref[...] * spreads[2],
    ]
    image = local_product(blocks_ref, notes_ref[VALVE], direction)
    image = image - coupling * received(near, arrive_ref)
    image_ref[...] = image
    weighted = jnp.sum(prolong * image, axis=0, keepdims=True)
    dots = [total(basis * image), total(image * image)]
    to_all(out_ref, restricted(weighted, gather_ref), cpd, dots)
    scaled = jscale * image
    for side, ref in enumerate((odd_ref, even_ref)):
        ref[...] = pick(scaled, row_of(notes_ref.at[SEND], parity(side)))


def second_step(got_ref, first_got_ref, even_near_ref, odd_near_ref, odd_first_ref, even_first_ref,
                odd_weights_ref, even_weights_ref, matrix_ref, info_ref, basis_ref, image_ref,
                jscale_ref, prolong_ref, blocks_ref, notes_ref, arrive_ref,
                grp_size, cpd, basis_two_ref, direction_ref, image_two_ref, scalars_ref, out_ref):
    beta = jnp.sqrt(summed(first_got_ref, cpd, 1)[0])
    along, energy = summed(got_ref, cpd, 2)
    height = jnp.sqrt(jnp.maximum(energy - along * along, 0.01 * energy))
    inverse = 1.0 / height
    slope = along / beta

    def mixed(new, old):
        return (new - slope * old) * inverse

    parts = [
        mixed(new, old) for new, old in zip(parts_of(got_ref, cpd), parts_of(first_got_ref, cpd))
    ]
    cdiags = [info_ref[at : at + 1, :] for at in range(3)]
    solved = solve_coarse(parts, matrix_ref, rows_near(parts, grp_size), cdiags, cpd)
    basis = (image_ref[...] - along * basis_ref[...]) * inverse
    basis_two_ref[...] = basis
    spread = spread_of(solved[0], notes_ref[AGG])
    direction = jscale_ref[...] * basis + prolong_ref[...] * spread
    direction_ref[...] = direction
    near = [
        mixed(odd_near_ref[...], odd_first_ref[...])
        + near_spread(odd_weights_ref, info_ref, 0, solved[1]),
        mixed(even_near_ref[...], even_first_ref[...])
        + near_spread(even_weights_ref, info_ref, 1, solved[2]),
    ]
    image = local_product(blocks_ref, notes_ref[VALVE], direction)
    image = image - coupling * received(near, arrive_ref)
    image_two_ref[...] = image
    scalars_ref[...] = jnp.concatenate([beta, along, height, jnp.zeros((5, LANES), f32)], axis=0)
    dots = [total(basis_ref[...] * image), total(basis * image), total(image * image)]
    to_all(out_ref, jnp.zeros((1, LANES), f32), 0, dots)


def finish(got_ref, scalars_ref, guess_ref, basis_ref, basis_two_ref, direction_ref,
           direction_two_ref, image_ref, solution_ref, next_ref):
    beta, h11, h21 = scalars_ref[0:1, :], scalars_ref[1:2, :], scalars_ref[2:3, :]
    h12, h22, energy = summed(got_ref, 0, 3)
    h32 = jnp.sqrt(jnp.maximum(energy - (h12 * h12 + h22 * h22), 0.01 * energy))
    g00 = h11 * h11 + h21 * h21
    g01 = h11 * h12 + h21 * h22
    g11 = h12 * h12 + h22 * h22 + h32 * h32
    t0, t1 = beta * h11, beta * h12
    factor = g01 / g00
    c1 = (t1 - factor * t0) / (g11 - factor * g01)
    c0 = (t0 - g01 * c1) / g00
    solution_ref[...] = guess_ref[...] + c0 * direction_ref[...] + c1 * direction_two_ref[...]
    next_ref[...] = (image_ref[...] - h12 * basis_ref[...] - h22 * basis_two_ref[...]) * (1.0 / h32)


def on_device(rhs, guess, blocks, valve, jscale, prolong, agg_map, cdiag, coff, send_rows,
              recv_rows, live_counts):
    rhs, guess, blocks, jscale, prolong = rhs[0, 0], guess[0, 0], blocks[0, 0], jscale[0, 0], prolong[0, 0]
    valve, agg, live = valve[0], agg_map[0], live_counts[0]
    send, recv = send_rows[0, 0], recv_rows[0, 0]
    size, count = guess.shape
    slots = send.shape[1]
    cpd = cdiag.shape[0]
    subs, grps = lax.axis_size("sub"), lax.axis_size("grp")
    devices = subs * grps
    cdiag = cdiag[None, :]
    moves = [pairing(subs, grps, side) for side in (0, 1)]

    def exchange(odd, even):
        return lax.ppermute(odd, AXES, moves[0]), lax.ppermute(even, AXES, moves[1])

    def everyone(rows):
        return lax.all_to_all(rows, AXES, 0, 0, tiled=True)

    field = ((size, count), f32)
    near = ((size, slots), f32)
    rows_out = ((devices, LANES), f32)
    small = ((8, LANES), f32)
    items = (guess, send)
    odd, even = call(
        first_send, [near, near], *items, hbm=range(2), limit=16,
        scratch=[pltpu.VMEM(item.shape, item.dtype) for item in items]
        + [pltpu.SemaphoreType.DMA((2,))],
    )
    odd_guess, even_guess = exchange(odd, even)
    packed = ((cpd * (coff.shape[1] // LANES) + 4 * size + 16, LANES), bf16)
    small_items = (agg, send, recv, valve)
    items = (guess, rhs, coff, prolong, cdiag)
    local, arrive, gather, odd, even, blocks, notes = call(
        prepare,
        [field, ((2 * slots, count), bf16), ((count, LANES), bf16), packed, packed,
         (blocks.shape, bf16), ((8, LANES), jnp.int32)],
        *small_items, live, guess, rhs, blocks, coff, prolong, cdiag, hbm=range(11),
        scratch=[pltpu.VMEM(item.shape, item.dtype) for item in small_items]
        + [pltpu.SMEM(live.shape, live.dtype)]
        + [pltpu.VMEM(item.shape, item.dtype) for item in items]
        + [pltpu.SemaphoreType.DMA((14,))],
    )
    first, rows, odd, even = call(
        lambda *refs: residual(*refs[:10], cpd, *refs[10:]), [field, rows_out, packed, packed],
        local, odd_guess, even_guess, arrive, gather, prolong, jscale, notes, odd, even,
        aliases={8: 2, 9: 3},
    )
    even_pack = lax.ppermute(even, AXES, moves[1])
    odd_pack = lax.ppermute(odd, AXES, moves[0])
    own_pack = odd
    first_got = everyone(rows)
    (basis, direction, image, rows, odd, even, matrix, odd_weights, even_weights, odd_first,
     even_first, info) = call(
        lambda *refs: first_step(*refs[:11], grps, cpd, *refs[11:]),
        [field, field, field, rows_out, near, near,
         ((3 * SLOT, coff.shape[1]), bf16)] + [near] * 4 + [small],
        first_got, own_pack, even_pack, odd_pack, first, jscale, prolong, blocks, notes, arrive,
        gather,
    )
    odd_near, even_near = exchange(odd, even)
    got = everyone(rows)
    basis_two, direction_two, image_two, scalars, rows = call(
        lambda *refs: second_step(*refs[:17], grps, cpd, *refs[17:]),
        [field, field, field, ((8, LANES), f32), rows_out],
        got, first_got, even_near, odd_near, odd_first, even_first, odd_weights, even_weights, matrix,
        info, basis, image, jscale, prolong, blocks, notes, arrive,
    )
    got = everyone(rows)
    solution, next_basis = call(
        finish, [field, field],
        got, scalars, guess, basis, basis_two, direction, direction_two, image_two, final=True,
    )
    return solution[None, None], next_basis[None, None]


def solution(mesh):
    return jax.shard_map(
        on_device,
        mesh=mesh,
        in_specs=(
            P("sub", "grp", None, None),
            P("sub", "grp", None, None),
            P("sub", "grp", None, None, None),
            P("sub", "grp", None),
            P("sub", "grp", None, None),
            P("sub", "grp", None, None),
            P("sub", "grp", None),
            P(("sub", "grp")),
            P(("sub", "grp"), None),
            P("sub", "grp", None, None),
            P("sub", "grp", None, None),
            P("sub", "grp", None),
        ),
        out_specs=(P("sub", "grp", None, None), P("sub", "grp", None, None)),
        check_vma=False,
    )
```

```python
import math

import jax
import jax.numpy as jnp
from jax import lax
from jax.experimental import pallas as pl
from jax.experimental.pallas import tpu as pltpu
from jax.sharding import PartitionSpec as P

penalty_gain = 3.0
coupling = 0.5

LANES = 128
SLOT = 64
AXES = ("sub", "grp")
f32 = jnp.float32
bf16 = jnp.bfloat16

SEND, RECV, AGG, VALVE = slice(0, 2), slice(2, 4), slice(4, 5), slice(5, 6)


def call(body, outs, *args, smem=(), hbm=(), scratch=(), limit=32, final=False, aliases=None):
    def spec(at):
        if at in hbm:
            return pl.BlockSpec(memory_space=pltpu.HBM)
        return pl.BlockSpec(memory_space=pltpu.SMEM if at in smem else pltpu.VMEM)

    args = [
        pltpu.with_memory_space_constraint(arg, pltpu.HBM) if at in hbm else arg
        for at, arg in enumerate(args)
    ]
    return pl.pallas_call(
        body,
        out_shape=[
            jax.ShapeDtypeStruct(shape, kind) if final else pltpu.VMEM(shape, kind)
            for shape, kind in outs
        ],
        in_specs=[spec(at) for at in range(len(args))],
        out_specs=[pl.BlockSpec(memory_space=pltpu.VMEM)] * len(outs),
        scratch_shapes=list(scratch),
        input_output_aliases=aliases or {},
        compiler_params=pltpu.CompilerParams(vmem_limit_bytes=limit * 1024 * 1024),
    )(*args)


def partner(place, side):
    return place - 1 + 2 * ((place + side) % 2)


def pairing(subs, grps, side):
    moves = []
    for place in range(subs):
        other = partner(place, side)
        for group in range(grps):
            if 0 <= other < subs:
                target = other * grps + group
            else:
                target = place * grps + (group ^ 1 if group ^ 1 < grps else group)
            moves.append((place * grps + group, target))
    return moves


def row_of(ref, flipped):
    return jnp.where(flipped == 0, ref[0:1, :], ref[1:2, :])


def parity(side):
    return (lax.axis_index("sub") + side + 1) % 2


def along_lanes(field, places):
    return jnp.take_along_axis(field, places, axis=1, mode="promise_in_bounds")


def pick(field, places):
    return along_lanes(field, jnp.broadcast_to(places, field.shape))


def pieces(field, count=2):
    result = []
    for _ in range(count):
        result.append(field.astype(bf16))
        field = field - result[-1].astype(f32)
    return result


def block_rows(blocks, field):
    return jnp.sum(blocks.astype(f32) * field[None], axis=1)


def local_product(blocks_ref, valve, field):
    rows = [block_rows(blocks_ref[at : at + 8], field) for at in range(0, blocks_ref.shape[0], 8)]
    return jnp.concatenate(rows, axis=0) + penalty_gain * valve.astype(f32) * field


def received(near, arrive_ref, count=2):
    parts = pieces(jnp.concatenate(near, axis=1), count)
    sums = jnp.dot(jnp.concatenate(parts, axis=0), arrive_ref[...], preferred_element_type=f32)
    size = near[0].shape[0]
    result = sums[:size]
    for at in range(size, count * size, size):
        result = result + sums[at : at + size]
    return result


def restricted(weighted, gather_ref):
    high = weighted.astype(bf16).astype(f32)
    rest = weighted - high
    middle = rest.astype(bf16).astype(f32)
    last = rest - middle
    row = lax.broadcasted_iota(jnp.int32, (8, weighted.shape[1]), 0)
    stack = jnp.where(row == 0, high, jnp.where(row == 1, middle, jnp.where(row == 2, last, 0.0)))
    sums = jnp.dot(stack.astype(bf16), gather_ref[...], preferred_element_type=f32)
    return jnp.sum(sums, axis=0, keepdims=True)


def total(field):
    return jnp.sum(jnp.sum(field, axis=0, keepdims=True), axis=1, keepdims=True)


def to_all(ref, row, first_lane, totals):
    lane = lax.broadcasted_iota(jnp.int32, (1, LANES), 1)
    for at, value in enumerate(totals):
        row = jnp.where(lane == first_lane + at, value, row)
    ref[...] = jnp.broadcast_to(row, ref.shape)


def summed(ref, first_lane, count):
    rows = jnp.broadcast_to(jnp.sum(ref[...], axis=0, keepdims=True), (8, LANES))
    return [
        along_lanes(rows, jnp.full((8, LANES), first_lane + at, jnp.int32))[0:1]
        for at in range(count)
    ]


def copy_all(pairs, sems):
    copies = [pltpu.make_async_copy(*pair, sems.at[at]) for at, pair in enumerate(pairs)]
    for copy in copies:
        copy.start()
    return copies


def first_send(guess_hbm, send_hbm, odd_ref, even_ref, guess_ref, send_ref, sems):
    for copy in copy_all(((send_hbm, send_ref), (guess_hbm, guess_ref)), sems):
        copy.wait()
    for side, ref in enumerate((odd_ref, even_ref)):
        ref[...] = pick(guess_ref[...], row_of(send_ref, parity(side)))


def wide(row):
    return jnp.concatenate([row, jnp.zeros((1, LANES - row.shape[1]), row.dtype)], axis=1)


def pack_constants(ref, coff_ref, prolong, agg, cdiag, places):
    cpd, width = coff_ref.shape
    for at in range(0, width, LANES):
        start = at // LANES * cpd
        ref[start : start + cpd, :] = coff_ref[:, at : at + LANES]
    base = cpd * (width // LANES)
    high, low = pieces(pick(prolong, places))
    size = high.shape[0]
    ref[base : base + size, :] = high
    ref[base + size : base + 2 * size, :] = low
    listed = pick(jnp.broadcast_to(agg.astype(f32), (8, LANES)), places)[0:1]
    one = cdiag.astype(bf16).astype(f32)
    two = (cdiag - one).astype(bf16).astype(f32)
    rows = [listed, one, two, cdiag - one - two, jnp.zeros((12, LANES), f32)]
    ref[base + 2 * size : base + 2 * size + 16, :] = jnp.concatenate(rows, axis=0).astype(bf16)


def prepare(agg_hbm, send_hbm, recv_hbm, valve_hbm, live_hbm, guess_hbm, rhs_hbm, blocks_hbm,
            coff_hbm, prolong_hbm, cdiag_hbm, local_ref, arrive_ref, gather_ref, odd_ref, even_ref,
            blocks_ref, notes_ref, agg_ref, send_ref, recv_ref, valve_ref, live_ref, guess_ref,
            rhs_ref, coff_ref, prolong_ref, cdiag_ref, sems):
    size = guess_ref.shape[0]
    chunk = size // 4
    pairs = [
        (agg_hbm, agg_ref), (send_hbm, send_ref), (recv_hbm, recv_ref), (valve_hbm, valve_ref),
        (coff_hbm, coff_ref), (prolong_hbm, prolong_ref), (cdiag_hbm, cdiag_ref),
        (live_hbm, live_ref), (guess_hbm, guess_ref),
    ]
    for at in range(0, size, chunk):
        pairs.append((blocks_hbm.at[at : at + chunk], blocks_ref.at[at : at + chunk]))
    copies = copy_all(pairs + [(rhs_hbm, rhs_ref)], sems)
    for copy in copies[:8]:
        copy.wait()
    notes_ref[...] = jnp.concatenate(
        [send_ref[...], recv_ref[...], agg_ref[...], valve_ref[...], jnp.zeros((2, LANES), jnp.int32)],
        axis=0,
    )
    cdiag = wide(cdiag_ref[...])
    for side, ref in enumerate((odd_ref, even_ref)):
        places = row_of(notes_ref.at[SEND], parity(side))
        pack_constants(ref, coff_ref, prolong_ref[...], notes_ref[AGG], cdiag, places)
    count = arrive_ref.shape[1]
    slots = notes_ref.shape[1]
    coarse = lax.broadcasted_iota(jnp.int32, (LANES, count), 0)
    gather_ref[...] = jnp.where(notes_ref[AGG] == coarse, 1.0, 0.0).T.astype(bf16)
    place = lax.axis_index("sub")
    row = lax.broadcasted_iota(jnp.int32, (count, slots), 0)
    slot = lax.broadcasted_iota(jnp.int32, (count, slots), 1)
    for side in (0, 1):
        other = place + 1 - 2 * parity(side)
        there = (other >= 0) & (other < lax.axis_size("sub"))
        which = 1 - parity(side)
        live = jnp.where(there, live_ref[0, which], 0)
        hit = (row_of(notes_ref.at[RECV], which) == row) & (slot < live)
        arrive_ref[side * slots : (side + 1) * slots, :] = jnp.where(hit, 1.0, 0.0).T.astype(bf16)
    copies[8].wait()
    guess = guess_ref[...]
    penalty = penalty_gain * notes_ref[VALVE].astype(f32)
    for at in range(0, size, 8):
        if at % chunk == 0:
            copies[9 + at // chunk].wait()
        part = slice(at, at + 8)
        local_ref[part, :] = block_rows(blocks_ref[part], guess) + penalty * guess[part]
    copies[-1].wait()
    local_ref[...] = rhs_ref[...] - local_ref[...]


def residual(local_ref, odd_near_ref, even_near_ref, arrive_ref, gather_ref, prolong_ref,
             jscale_ref, notes_ref, odd_pack_ref, even_pack_ref, cpd, first_ref, out_ref, odd_ref,
             even_ref):
    near = [odd_near_ref[...], even_near_ref[...]]
    first = local_ref[...] + coupling * received(near, arrive_ref, 3)
    first_ref[...] = first
    weighted = jnp.sum(prolong_ref[...] * first, axis=0, keepdims=True)
    to_all(out_ref, restricted(weighted, gather_ref), cpd, [total(first * first)])
    scaled = jscale_ref[...] * first
    size = first.shape[0]
    tail = odd_ref.shape[0] - 2 * size
    for side, ref in enumerate((odd_ref, even_ref)):
        high, low = pieces(pick(scaled, row_of(notes_ref.at[SEND], parity(side))))
        ref[tail : tail + size, :] = high
        ref[tail + size :, :] = low


def unpack(own_ref, even_ref, odd_ref, cpd, matrix_ref, odd_weights_ref, even_weights_ref,
           odd_first_ref, even_first_ref, info_ref):
    width = matrix_ref.shape[1]
    size = odd_first_ref.shape[0]
    base = cpd * (width // LANES)
    rows = []
    for slot, ref in enumerate((own_ref, odd_ref, even_ref)):
        for at in range(0, width, LANES):
            start = at // LANES * cpd
            matrix_ref[slot * SLOT : slot * SLOT + cpd, at : at + LANES] = ref[start : start + cpd, :]
        matrix_ref[slot * SLOT + cpd : (slot + 1) * SLOT, :] = jnp.zeros((SLOT - cpd, width), bf16)
        rows.append(ref[base + 2 * size : base + 2 * size + 16, :].astype(f32))
    for ref, weights_ref, near_ref in (
        (odd_ref, odd_weights_ref, odd_first_ref), (even_ref, even_weights_ref, even_first_ref)
    ):
        for start, to_ref in ((base, weights_ref), (base + 2 * size + 16, near_ref)):
            high, low = ref[start : start + size, :], ref[start + size : start + 2 * size, :]
            to_ref[...] = high.astype(f32) + low.astype(f32)
    infos = [row[1:2] + row[2:3] + row[3:4] for row in rows] + [row[0:1] for row in rows[1:]]
    info_ref[...] = jnp.concatenate(infos + [jnp.zeros((3, LANES), f32)], axis=0)


def solve_coarse(parts, matrix_ref, near_rows, cdiags, cpd):
    group = parts[0].shape[0]
    shape = (group, LANES)
    row = lax.broadcasted_iota(jnp.int32, shape, 0)
    lane = lax.broadcasted_iota(jnp.int32, shape, 1)
    masks = [(at + lane) // cpd == row for at in range(0, group * cpd, LANES)]
    source = lax.rem(lane - cpd * row + cpd * group, LANES)
    tiles = []
    for part in parts:
        shifted = along_lanes(part, source)
        tiles.extend(jnp.where(mask, shifted, 0.0) for mask in masks)
    product = lax.dot_general(
        jnp.concatenate(tiles, axis=1).astype(bf16), matrix_ref[...], (((1,), (1,)), ((), ())),
        preferred_element_type=f32,
    )
    product = jnp.sum(product, axis=0, keepdims=True)
    low = product[:, :LANES]
    high = jnp.concatenate([product[:, LANES:], jnp.zeros((1, LANES - SLOT), f32)], axis=1)
    turned = pltpu.roll(jnp.broadcast_to(low, (8, LANES)), LANES - SLOT, 1)[0:1]
    shares = (low, turned, high)
    return [cdiag * row + share for cdiag, row, share in zip(cdiags, near_rows, shares)]


def solve_at_blocks(parts, matrix_ref, near_rows, cdiags, aggs, cpd):
    group = parts[0].shape[0]
    shape = (group, LANES)
    row = lax.broadcasted_iota(jnp.int32, shape, 0)
    lane = lax.broadcasted_iota(jnp.int32, shape, 1)
    masks = [(at + lane) // cpd == row for at in range(0, group * cpd, LANES)]
    source = lax.rem(lane - cpd * row + cpd * group, LANES)
    tiles = []
    for part in parts:
        shifted = along_lanes(part, source)
        for mask in masks:
            tiles.append(jnp.sum(jnp.where(mask, shifted, 0.0), axis=0, keepdims=True))
    vector = jnp.concatenate(tiles, axis=1)
    product = lax.dot_general(
        matrix_ref[...], jnp.broadcast_to(vector, (LANES, vector.shape[1])).astype(bf16),
        (((1,), (1,)), ((), ())), preferred_element_type=f32,
    )
    unknown = lax.broadcasted_iota(jnp.int32, (cpd, LANES), 0)
    spreads = []
    for slot, (cdiag, near_row, agg) in enumerate(zip(cdiags, near_rows, aggs)):
        share = jnp.where(unknown == agg, product[slot * SLOT : slot * SLOT + cpd], 0.0)
        spreads.append(spread_of(cdiag * near_row, agg) + jnp.sum(share, axis=0, keepdims=True))
    return spreads


def parts_of(ref, cpd):
    group = math.lcm(cpd, LANES) // cpd
    rows = ref[...]
    return [rows[at : at + group, :] for at in range(0, rows.shape[0], group)]


def rows_near(parts, grp_size):
    group = parts[0].shape[0]
    count = group * len(parts)
    me = lax.axis_index("sub") * grp_size + lax.axis_index("grp")
    place = lax.broadcasted_iota(jnp.int32, parts[0].shape, 0)
    rows = []
    for shift in [0] + [grp_size * (1 - 2 * parity(side)) for side in (0, 1)]:
        wanted = lax.rem(me + shift + count, count)
        found = jnp.where(place == wanted, parts[0], 0.0)
        for at, part in enumerate(parts[1:], 1):
            found = jnp.where(place + at * group == wanted, part, found)
        rows.append(jnp.sum(found, axis=0, keepdims=True))
    return rows


def spread_of(solution, agg):
    wide = jnp.broadcast_to(solution, (8, LANES))
    return along_lanes(wide, jnp.broadcast_to(agg, (8, LANES)))[0:1]


def near_spread(weights_ref, info_ref, side, solution):
    agg = info_ref[3 + side : 4 + side, :].astype(jnp.int32)
    return weights_ref[...] * spread_of(solution, agg)


def first_step(got_ref, own_pack_ref, even_pack_ref, odd_pack_ref, first_ref, jscale_ref,
               prolong_ref, blocks_ref, notes_ref, arrive_ref, gather_ref, grp_size, cpd,
               basis_ref, direction_ref, image_ref, out_ref, odd_ref, even_ref, matrix_ref,
               odd_weights_ref, even_weights_ref, odd_near_ref, even_near_ref, info_ref):
    unpack(own_pack_ref, even_pack_ref, odd_pack_ref, cpd, matrix_ref, odd_weights_ref,
           even_weights_ref, odd_near_ref, even_near_ref, info_ref)
    inverse = lax.rsqrt(summed(got_ref, cpd, 1)[0])
    parts = [part * inverse for part in parts_of(got_ref, cpd)]
    cdiags = [info_ref[at : at + 1, :] for at in range(3)]
    aggs = [notes_ref[AGG]] + [info_ref[at : at + 1, :].astype(jnp.int32) for at in (3, 4)]
    spreads = solve_at_blocks(parts, matrix_ref, rows_near(parts, grp_size), cdiags, aggs, cpd)
    basis = first_ref[...] * inverse
    basis_ref[...] = basis
    jscale, prolong = jscale_ref[...], prolong_ref[...]
    direction = jscale * basis + prolong * spreads[0]
    direction_ref[...] = direction
    near = [
        odd_near_ref[...] * inverse + odd_weights_ref[...] * spreads[1],
        even_near_ref[...] * inverse + even_weights_ref[...] * spreads[2],
    ]
    image = local_product(blocks_ref, notes_ref[VALVE], direction)
    image = image - coupling * received(near, arrive_ref)
    image_ref[...] = image
    weighted = jnp.sum(prolong * image, axis=0, keepdims=True)
    dots = [total(basis * image), total(image * image)]
    to_all(out_ref, restricted(weighted, gather_ref), cpd, dots)
    scaled = jscale * image
    for side, ref in enumerate((odd_ref, even_ref)):
        ref[...] = pick(scaled, row_of(notes_ref.at[SEND], parity(side)))


def second_step(got_ref, first_got_ref, even_near_ref, odd_near_ref, odd_first_ref, even_first_ref,
                odd_weights_ref, even_weights_ref, matrix_ref, info_ref, basis_ref, image_ref,
                jscale_ref, prolong_ref, blocks_ref, notes_ref, arrive_ref,
                grp_size, cpd, basis_two_ref, direction_ref, image_two_ref, scalars_ref, out_ref):
    beta = jnp.sqrt(summed(first_got_ref, cpd, 1)[0])
    along, energy = summed(got_ref, cpd, 2)
    height = jnp.sqrt(jnp.maximum(energy - along * along, 0.01 * energy))
    inverse = 1.0 / height
    slope = along * (1.0 / beta)

    def mixed(new, old):
        return (new - slope * old) * inverse

    parts = [
        mixed(new, old) for new, old in zip(parts_of(got_ref, cpd), parts_of(first_got_ref, cpd))
    ]
    cdiags = [info_ref[at : at + 1, :] for at in range(3)]
    solved = solve_coarse(parts, matrix_ref, rows_near(parts, grp_size), cdiags, cpd)
    basis = (image_ref[...] - along * basis_ref[...]) * inverse
    basis_two_ref[...] = basis
    spread = spread_of(solved[0], notes_ref[AGG])
    direction = jscale_ref[...] * basis + prolong_ref[...] * spread
    direction_ref[...] = direction
    near = [
        mixed(odd_near_ref[...], odd_first_ref[...])
        + near_spread(odd_weights_ref, info_ref, 0, solved[1]),
        mixed(even_near_ref[...], even_first_ref[...])
        + near_spread(even_weights_ref, info_ref, 1, solved[2]),
    ]
    image = local_product(blocks_ref, notes_ref[VALVE], direction)
    image = image - coupling * received(near, arrive_ref)
    image_two_ref[...] = image
    scalars_ref[...] = jnp.concatenate([beta, along, height, jnp.zeros((5, LANES), f32)], axis=0)
    dots = [total(basis_ref[...] * image), total(basis * image), total(image * image)]
    to_all(out_ref, jnp.zeros((1, LANES), f32), 0, dots)


def finish(got_ref, scalars_ref, guess_ref, basis_ref, basis_two_ref, direction_ref,
           direction_two_ref, image_ref, solution_ref, next_ref):
    beta, h11, h21 = scalars_ref[0:1, :], scalars_ref[1:2, :], scalars_ref[2:3, :]
    h12, h22, energy = summed(got_ref, 0, 3)
    h32 = jnp.sqrt(jnp.maximum(energy - (h12 * h12 + h22 * h22), 0.01 * energy))
    g00 = h11 * h11 + h21 * h21
    g01 = h11 * h12 + h21 * h22
    g11 = h12 * h12 + h22 * h22 + h32 * h32
    t0, t1 = beta * h11, beta * h12
    factor = g01 / g00
    c1 = (t1 - factor * t0) / (g11 - factor * g01)
    c0 = (t0 - g01 * c1) / g00
    solution_ref[...] = guess_ref[...] + c0 * direction_ref[...] + c1 * direction_two_ref[...]
    next_ref[...] = (image_ref[...] - h12 * basis_ref[...] - h22 * basis_two_ref[...]) * (1.0 / h32)


def on_device(rhs, guess, blocks, valve, jscale, prolong, agg_map, cdiag, coff, send_rows,
              recv_rows, live_counts):
    rhs, guess, blocks, jscale, prolong = rhs[0, 0], guess[0, 0], blocks[0, 0], jscale[0, 0], prolong[0, 0]
    valve, agg, live = valve[0], agg_map[0], live_counts[0]
    send, recv = send_rows[0, 0], recv_rows[0, 0]
    size, count = guess.shape
    slots = send.shape[1]
    cpd = cdiag.shape[0]
    subs, grps = lax.axis_size("sub"), lax.axis_size("grp")
    devices = subs * grps
    cdiag = cdiag[None, :]
    moves = [pairing(subs, grps, side) for side in (0, 1)]

    def exchange(odd, even):
        return lax.ppermute(odd, AXES, moves[0]), lax.ppermute(even, AXES, moves[1])

    def everyone(rows):
        return lax.all_to_all(rows, AXES, 0, 0, tiled=True)

    field = ((size, count), f32)
    near = ((size, slots), f32)
    rows_out = ((devices, LANES), f32)
    small = ((8, LANES), f32)
    items = (guess, send)
    odd, even = call(
        first_send, [near, near], *items, hbm=range(2), limit=16,
        scratch=[pltpu.VMEM(item.shape, item.dtype) for item in items]
        + [pltpu.SemaphoreType.DMA((2,))],
    )
    odd_guess, even_guess = exchange(odd, even)
    packed = ((cpd * (coff.shape[1] // LANES) + 4 * size + 16, LANES), bf16)
    small_items = (agg, send, recv, valve)
    items = (guess, rhs, coff, prolong, cdiag)
    local, arrive, gather, odd, even, blocks, notes = call(
        prepare,
        [field, ((2 * slots, count), bf16), ((count, LANES), bf16), packed, packed,
         (blocks.shape, bf16), ((8, LANES), jnp.int32)],
        *small_items, live, guess, rhs, blocks, coff, prolong, cdiag, hbm=range(11),
        scratch=[pltpu.VMEM(item.shape, item.dtype) for item in small_items]
        + [pltpu.SMEM(live.shape, live.dtype)]
        + [pltpu.VMEM(item.shape, item.dtype) for item in items]
        + [pltpu.SemaphoreType.DMA((14,))],
    )
    first, rows, odd, even = call(
        lambda *refs: residual(*refs[:10], cpd, *refs[10:]), [field, rows_out, packed, packed],
        local, odd_guess, even_guess, arrive, gather, prolong, jscale, notes, odd, even,
        aliases={8: 2, 9: 3},
    )
    even_pack = lax.ppermute(even, AXES, moves[1])
    odd_pack = lax.ppermute(odd, AXES, moves[0])
    own_pack = odd
    first_got = everyone(rows)
    (basis, direction, image, rows, odd, even, matrix, odd_weights, even_weights, odd_first,
     even_first, info) = call(
        lambda *refs: first_step(*refs[:11], grps, cpd, *refs[11:]),
        [field, field, field, rows_out, near, near,
         ((3 * SLOT, coff.shape[1]), bf16)] + [near] * 4 + [small],
        first_got, own_pack, even_pack, odd_pack, first, jscale, prolong, blocks, notes, arrive,
        gather,
    )
    odd_near, even_near = exchange(odd, even)
    got = everyone(rows)
    basis_two, direction_two, image_two, scalars, rows = call(
        lambda *refs: second_step(*refs[:17], grps, cpd, *refs[17:]),
        [field, field, field, ((8, LANES), f32), rows_out],
        got, first_got, even_near, odd_near, odd_first, even_first, odd_weights, even_weights, matrix,
        info, basis, image, jscale, prolong, blocks, notes, arrive,
    )
    got = everyone(rows)
    solution, next_basis = call(
        finish, [field, field],
        got, scalars, guess, basis, basis_two, direction, direction_two, image_two, final=True,
    )
    return solution[None, None], next_basis[None, None]


def solution(mesh):
    return jax.shard_map(
        on_device,
        mesh=mesh,
        in_specs=(
            P("sub", "grp", None, None),
            P("sub", "grp", None, None),
            P("sub", "grp", None, None, None),
            P("sub", "grp", None),
            P("sub", "grp", None, None),
            P("sub", "grp", None, None),
            P("sub", "grp", None),
            P(("sub", "grp")),
            P(("sub", "grp"), None),
            P("sub", "grp", None, None),
            P("sub", "grp", None, None),
            P("sub", "grp", None),
        ),
        out_specs=(P("sub", "grp", None, None), P("sub", "grp", None, None)),
        check_vma=False,
    )
```
